256 devices in a mesh: slab: 8 (over y, core), row: 32 (over x, z).
Axes of the slice: x: 4, y: 4, z: 8, core: 2. Of those that a mesh axis runs over, the one named last changes fastest.
Arguments:
- a_blocks: bfloat16 [16384, 64, 448], P(('slab', 'row')), may hold values from -0.25 to 0.25
- p_blocks: bfloat16 [16384, 64, 256], P(('slab', 'row')), may hold values from -1.5 to 1.5
- a_cols: int32 [16384, 7], P(('slab', 'row')), may hold values from 0 to 95
- p_slots: int32 [16384, 4], P(('slab', 'row')), may hold values from 0 to 63, as said below
- touched: int32 [256, 32, 2], P(('slab', 'row')), may hold values from -1 to 3, as said below
- touch_cols: int32 [256, 32, 2, 8], P(('slab', 'row')), may hold values from -1 to 1023, as said below
- halo_rows: int32 [256, 4, 8], P(('slab', 'row')), may hold values from 0 to 63, as said below
Outputs:
- coarse_ops: float32 [1024, 64, 512], P(('slab', 'row'))
The draws below stay inside these ranges and needn't reach their ends.
Inputs may be any that keep to these rules, and one draw needn't show every extreme that they name: touched[d, p, :] lists distinct row indices among the 4 coarse rows owned by device p of d's slab, used entries first, -1 in unused slots; in every slab two owners have all 2 slots used by every device of the slab. `p_slots`: each fine row names 4 distinct used slots of its own device's touched table. touch_cols[d, p, c, :] holds 8 distinct global coarse row ids, the same list on every device naming that coarse row; -1 in unused slots. halo_rows[d, j, :] holds 8 distinct local fine row indices of device d.
All inputs are finite; a program needn't handle non-finite values.
Results may differ from the reference program's by a relative error of at most 0.013.
Values may be sent and summed in bfloat16 or wider, within the bound.
A program may use at most 128 MiB of HBM per device.

```python
import jax
import jax.numpy as jnp
from jax import lax

B = 64
KA = 7
KP = 4
KC = 8
NC = 4
CAP = 2
H = 8
NF = 64
FINE = 16384
N_SLAB = 8
N_ROW = 32
DEVICES = 256


def to_front(order, value):
    place = jnp.argmax(order == value)
    first = order[0]
    return order.at[place].set(first).at[0].set(value)


def layout(key):
    k_hot, k_count, k_rows, k_pattern = jax.random.split(key, 4)
    slab_perm = jax.vmap(lambda k: jax.random.permutation(k, N_ROW))(jax.random.split(k_hot, N_SLAB)).astype(jnp.int32)
    last_perm = to_front(slab_perm[N_SLAB - 1], N_ROW - 1)
    slab_perm = slab_perm.at[N_SLAB - 1].set(last_perm)
    peers = jnp.arange(N_ROW, dtype=jnp.int32)
    is_hot = (peers[None, :] == slab_perm[:, 0:1]) | (peers[None, :] == slab_perm[:, 1:2])
    dev_slab = jnp.arange(DEVICES, dtype=jnp.int32) // N_ROW
    light = jax.random.randint(k_count, (DEVICES, N_ROW), 0, CAP // 2 + 1)
    counts = jnp.where(is_hot[dev_slab], CAP, light)
    row_perm = jax.vmap(lambda k: jax.random.permutation(k, NC))(jax.random.split(k_rows, DEVICES * N_ROW))
    row_perm = row_perm.reshape(DEVICES, N_ROW, NC)[:, :, :CAP]
    touched = jnp.where(jnp.arange(CAP)[None, None, :] < counts[:, :, None], row_perm, -1).astype(jnp.int32)
    slabs = jnp.arange(N_SLAB, dtype=jnp.int32)
    near = (slabs[:, None] + jnp.array([-1, 0, 1], dtype=jnp.int32)[None, :]) % N_SLAB
    hot_peers = slab_perm[near][:, :, :2]
    pool = ((near[:, :, None, None] * N_ROW + hot_peers[:, :, :, None]) * NC + jnp.arange(NC, dtype=jnp.int32)[None, None, None, :]).reshape(N_SLAB, 6 * NC)
    top_place = jnp.argmax(pool, axis=1).astype(jnp.int32)
    coarse_slab = jnp.arange(DEVICES * NC, dtype=jnp.int32) // (N_ROW * NC)
    orders = jax.vmap(lambda k: jax.random.permutation(k, 6 * NC))(jax.random.split(k_pattern, DEVICES * NC)).astype(jnp.int32)
    orders = jax.vmap(to_front)(orders, top_place[coarse_slab])
    choose = orders[:, :KC]
    pattern_table = jnp.take_along_axis(pool[coarse_slab], choose, axis=1).astype(jnp.int32)
    return (touched, pattern_table)


def draw_touched(key, part):
    touched, pattern_table = layout(key)
    return touched


def draw_touch_cols(key, part):
    touched, pattern_table = layout(key)
    dev_slab = jnp.arange(DEVICES, dtype=jnp.int32) // N_ROW
    peers = jnp.arange(N_ROW, dtype=jnp.int32)
    global_rows = (dev_slab[:, None, None] * N_ROW + peers[None, :, None]) * NC + touched
    columns = pattern_table[jnp.maximum(global_rows, 0)]
    return jnp.where(touched[..., None] >= 0, columns, -1).astype(jnp.int32)


def draw_p_slots(key, part):
    touched, pattern_table = layout(key)
    key = jax.random.fold_in(key, 7)
    slots = N_ROW * CAP
    valid = (touched.reshape(DEVICES, slots) >= 0).astype(jnp.int32)
    order = jax.vmap(lambda k: jax.random.permutation(k, slots))(jax.random.split(key, FINE)).astype(jnp.int32)
    owner = jnp.arange(FINE, dtype=jnp.int32) // NF
    score = valid[owner] * slots + order
    return lax.top_k(score, KP)[1].astype(jnp.int32)


def draw_halo_rows(key, part):
    key = jax.random.fold_in(key, 11)
    order = jax.vmap(lambda k: jax.random.permutation(k, NF))(jax.random.split(key, DEVICES * 4))
    return order.reshape(DEVICES, 4, NF)[:, :, :H].astype(jnp.int32)


def plant(entries, stream_key, low, top_value):
    longest = entries.shape.index(max(entries.shape))
    spots = []
    for shift in (0, 1):
        where = [jax.random.randint(jax.random.fold_in(stream_key, axis), (), 0, length) for axis, length in enumerate(entries.shape)]
        where[longest] = (where[longest] + shift) % entries.shape[longest]
        spots.append(tuple(where))
    return entries.at[spots[0]].set(low).at[spots[1]].set(top_value)


def levels(key, dims, shards, least, high):
    def one(dim, shards_of):
        steps = jax.random.uniform(jax.random.fold_in(jax.random.fold_in(key, 6), dim), (shards_of,), jnp.float32, least / len(shards), high / len(shards))
        return jnp.repeat(jnp.exp(steps), dims[dim] // shards_of).reshape((-1,) + (1,) * (len(dims) - dim - 1))

    gain = one(*shards[0])
    for cut in shards[1:]:
        gain = gain * one(*cut)
    return gain


def noise(rng, shape, width, reach, pieces=(), held_as=jnp.bfloat16):
    values = width * jax.random.normal(rng, shape, jnp.float32)
    if pieces:
        values = values * levels(rng, shape, pieces, -0.22, 0.18)
    return jnp.clip(values, -reach, reach).astype(held_as)


def setup_inputs(seed: int = 0) -> dict:
    key_of = jax.random.split(jax.random.key(seed), 8)
    return {
        "a_blocks": noise(key_of[0], (FINE, B, KA * B), (KA * B) ** -0.5, 0.25, ((0, 256),)),
        "p_blocks": noise(key_of[1], (FINE, B, KP * B), 0.25, 1.5, ((0, 256),)),
        "a_cols": plant(jax.random.randint(key_of[2], (FINE, KA), 0, NF + 4 * H), jax.random.fold_in(key_of[2], 1), 0, (NF + 4 * H) - 1).astype(jnp.int32),
        "p_slots": draw_p_slots(jax.random.fold_in(key_of[7], 71), 0),
        "touched": draw_touched(jax.random.fold_in(key_of[7], 71), 0),
        "touch_cols": draw_touch_cols(jax.random.fold_in(key_of[7], 71), 0),
        "halo_rows": draw_halo_rows(jax.random.fold_in(key_of[7], 71), 0),
    }


def shift_down(values, axis):
    zeros = jnp.zeros_like(lax.slice_in_dim(values, 0, 1, axis=axis))
    return jnp.concatenate([zeros, lax.slice_in_dim(values, 0, values.shape[axis] - 1, axis=axis)], axis)


def shift_up(values, axis):
    zeros = jnp.zeros_like(lax.slice_in_dim(values, 0, 1, axis=axis))
    return jnp.concatenate([lax.slice_in_dim(values, 1, values.shape[axis], axis=axis), zeros], axis)


def extend(own, sent):
    parts = [own, shift_down(sent[:, :, 1], 0), shift_up(sent[:, :, 0], 0), shift_down(sent[:, :, 3], 1), shift_up(sent[:, :, 2], 1)]
    return jnp.concatenate(parts, axis=2)


def one_device(operands):
    matrix, ext_blocks, ext_ids, cols, interp, slot_rows, patterns = operands
    gathered = ext_blocks[cols]
    product = jnp.einsum('irkc,ikcq->irkq', matrix.reshape(NF, B, KA, B).astype(jnp.float32), gathered.astype(jnp.float32), precision=lax.Precision.HIGHEST)
    product = product.reshape(NF, B, KA * KP, B)
    reached = ext_ids[cols].reshape(NF, KA * KP)
    wanted = patterns[slot_rows]
    match = (reached[:, None, :, None] == wanted[:, :, None, :]).astype(jnp.float32)
    merged = jnp.einsum('irjc,imjs->imrsc', product, match, precision=lax.Precision.HIGHEST)
    merged = merged.astype(jnp.bfloat16).reshape(NF, KP, B, KC * B)
    term = jnp.einsum('irmc,imrx->imcx', interp.reshape(NF, B, KP, B).astype(jnp.float32), merged.astype(jnp.float32), precision=lax.Precision.HIGHEST)
    term = term.reshape(NF * KP, B * KC * B)
    total = jax.ops.segment_sum(term, slot_rows.reshape(NF * KP), num_segments=N_ROW * CAP)
    return total.astype(jnp.bfloat16)


def one_slab(operands):
    partials, owners = operands
    pick = (owners[..., None] == jnp.arange(NC, dtype=jnp.int32)).astype(jnp.float32)
    return jnp.einsum('rpcl,rpcx->plx', pick, partials.astype(jnp.float32), precision=lax.Precision.HIGHEST)


def reference(a_blocks, p_blocks, a_cols, p_slots, touched, touch_cols, halo_rows):
    devices = N_SLAB * N_ROW
    slots = N_ROW * CAP
    blocks = p_blocks.reshape(N_SLAB, N_ROW, NF, B, KP * B)
    table = touched.reshape(devices, slots)
    flat_slots = p_slots.reshape(devices, NF * KP)
    local_ids = jnp.take_along_axis(table, flat_slots, axis=1)
    slab_of = (jnp.arange(devices, dtype=jnp.int32) // N_ROW).astype(jnp.int32)
    coarse_ids = ((slab_of[:, None] * N_ROW + flat_slots // CAP) * NC + local_ids).astype(jnp.int32)
    coarse_ids = coarse_ids.reshape(N_SLAB, N_ROW, NF, KP)
    lists = halo_rows.reshape(N_SLAB, N_ROW, 4, H)
    sent_blocks = jax.vmap(jax.vmap(lambda rows_all, picks: rows_all[picks]))(blocks, lists)
    sent_ids = jax.vmap(jax.vmap(lambda rows_all, picks: rows_all[picks]))(coarse_ids, lists)
    ext_blocks = extend(blocks, sent_blocks).reshape(devices, NF + 4 * H, B, KP * B)
    ext_ids = extend(coarse_ids, sent_ids).reshape(devices, NF + 4 * H, KP)
    partials = lax.map(one_device, (a_blocks.reshape(devices, NF, B, KA * B), ext_blocks, ext_ids, a_cols.reshape(devices, NF, KA), p_blocks.reshape(devices, NF, B, KP * B), p_slots.reshape(devices, NF, KP), touch_cols.reshape(devices, slots, KC)))
    summed = lax.map(one_slab, (partials.reshape(N_SLAB, N_ROW, N_ROW, CAP, B * KC * B), touched.reshape(N_SLAB, N_ROW, N_ROW, CAP)))
    return summed.reshape(N_SLAB * N_ROW * NC, B, KC * B)
```

```python
import functools

import jax
import jax.numpy as jnp
from jax import lax
from jax.experimental import pallas as pl
from jax.experimental.pallas import tpu as pltpu
from jax.sharding import PartitionSpec as P

NC = 4
UNROLL = 8


def coarse_kernel(cols, slots, masks, places, a_hbm, p_hbm, halo_hbm, out_ref, a_v, ext_v, g_v, acc, items, sems):
    rows, width, span = a_v.shape
    ka = span // width
    kp = ext_v.shape[2] // width
    kq = ka * kp
    nslots, _, outspan = out_ref.shape
    kc = outspan // width
    pair = 2 * width
    copy_a = pltpu.make_async_copy(a_hbm, a_v, sems.at[0])
    copy_p = pltpu.make_async_copy(p_hbm, ext_v.at[pl.ds(0, rows)], sems.at[1])
    copy_h = pltpu.make_async_copy(halo_hbm, ext_v.at[pl.ds(rows, halo_hbm.shape[0])], sems.at[2])
    copy_a.start()
    copy_p.start()
    copy_h.start()

    def clear(t, unused):
        acc[pl.ds(t * kc, kc)] = jnp.zeros((kc, width, pair), jnp.float32)
        return unused

    lax.fori_loop(0, nslots, clear, 0)
    acc[pl.ds(nslots * kc, 1)] = jnp.zeros((1, width, pair), jnp.float32)

    def gather_items(im, count):
        slot = slots[im]
        head = im * 32

        def more(state):
            return state[0] != 0

        def take(state):
            mask, at = state
            bit = 31 - lax.clz(mask)
            items[at] = (head + bit) * 1024 + slot * kc + places[im * kq + bit]
            return (mask - lax.shift_left(1, bit), at + 1)

        return lax.while_loop(more, take, (masks[im], count))[1]

    count = lax.fori_loop(0, rows * kp, gather_items, 0)
    for u in range(UNROLL):
        items[count + u] = nslots * kc
    copy_a.wait()
    copy_p.wait()
    copy_h.wait()

    def products(i, unused):
        row = a_v[i]
        for k in range(ka):
            right = ext_v[cols[i * ka + k]]
            value = jnp.dot(row[:, k * width : (k + 1) * width], right, preferred_element_type=jnp.float32).astype(
                jnp.bfloat16
            )
            for h in range(kp // 2):
                g_v[(i * ka + k) * (kp // 2) + h] = value[:, h * pair : (h + 1) * pair]
        return unused

    lax.fori_loop(0, rows, products, 0)
    upper = lax.broadcasted_iota(jnp.int32, (width, pair), 1) // width

    def batch(b, unused):
        found = []
        for u in range(UNROLL):
            word = items[b * UNROLL + u]
            target = word % 1024
            bit = (word // 1024) % 32
            im = word // 32768
            i = im // kp
            m = im % kp
            k = bit // kp
            q = bit % kp
            g = g_v[(i * ka + k) * (kp // 2) + q // 2]
            g = jnp.where(upper == q % 2, g, jnp.zeros_like(g))
            p = ext_v[i, :, pl.ds(pl.multiple_of((m // 2) * pair, pair), pair)]
            z = lax.dot_general(p, g, (((0,), (0,)), ((), ())), preferred_element_type=jnp.float32)
            z = jnp.where(m % 2 == 1, z[width:], z[:width])
            found.append((target, z))
        for target, z in found:
            acc[target] = acc[target] + z
        return unused

    lax.fori_loop(0, (count + UNROLL - 1) // UNROLL, batch, 0)

    def finish(t, unused):
        for h in range(kc // 2):
            one = acc[t * kc + 2 * h]
            two = acc[t * kc + 2 * h + 1]
            one = one + pltpu.roll(one, width, 1)
            two = two + pltpu.roll(two, width, 1)
            out_ref[t, :, h * pair : (h + 1) * pair] = jnp.where(upper == 0, one, two).astype(jnp.bfloat16)
        return unused

    lax.fori_loop(0, nslots, finish, 0)


def coarse_partials(cols, slots, masks, places, a_blocks, p_blocks, halo, nslots, kc):
    rows, width, span = a_blocks.shape
    kp = p_blocks.shape[2] // width
    ka = span // width
    extended = rows + halo.shape[0]
    smem = pl.BlockSpec(memory_space=pltpu.SMEM)
    hbm = pl.BlockSpec(memory_space=pl.ANY)
    return pl.pallas_call(
        coarse_kernel,
        out_shape=jax.ShapeDtypeStruct((nslots, width, kc * width), jnp.bfloat16),
        in_specs=[smem, smem, smem, smem, hbm, hbm, hbm],
        out_specs=pl.BlockSpec(memory_space=pltpu.VMEM),
        scratch_shapes=[
            pltpu.VMEM((rows, width, span), jnp.bfloat16),
            pltpu.VMEM((extended, width, kp * width), jnp.bfloat16),
            pltpu.VMEM((rows * ka * (kp // 2), width, 2 * width), jnp.bfloat16),
            pltpu.VMEM((nslots * kc + 1, width, 2 * width), jnp.float32),
            pltpu.SMEM((rows * kp * ka * kp + UNROLL,), jnp.int32),
            pltpu.SemaphoreType.DMA((3,)),
        ],
        compiler_params=pltpu.CompilerParams(vmem_limit_bytes=56 * 2**20),
        name="coarse_partials",
    )(cols, slots, masks, places, a_blocks, p_blocks, halo)


def sum_kernel(ids, parts, out_ref):
    out_ref[...] = jnp.zeros_like(out_ref)

    def one(n, unused):
        row = ids[n]

        @pl.when(row >= 0)
        def _():
            out_ref[row] = out_ref[row] + parts[n].astype(jnp.float32)

        return unused

    lax.fori_loop(0, parts.shape[0], one, 0)


def sum_parts(ids, parts):
    return pl.pallas_call(
        sum_kernel,
        out_shape=jax.ShapeDtypeStruct((NC,) + parts.shape[1:], jnp.float32),
        in_specs=[pl.BlockSpec(memory_space=pltpu.SMEM), pl.BlockSpec(memory_space=pltpu.VMEM)],
        out_specs=pl.BlockSpec(memory_space=pltpu.VMEM),
        compiler_params=pltpu.CompilerParams(vmem_limit_bytes=32 * 2**20),
        name="sum_parts",
    )(ids, parts)


def lookup(table, index):
    hot = index[..., None] == jnp.arange(table.shape[0], dtype=jnp.int32)
    return jnp.sum(jnp.where(hot, table, 0), axis=-1)


def find_matches(ext_ids, a_cols, p_slots, patterns):
    rows = a_cols.shape[0]
    kp = p_slots.shape[1]
    reached = jnp.stack([lookup(ext_ids[:, q], a_cols) for q in range(kp)], -1).reshape(rows, -1)
    wanted = jnp.stack([lookup(patterns[:, j], p_slots) for j in range(patterns.shape[1])], 0)
    order = jnp.arange(1, patterns.shape[1] + 1, dtype=jnp.int32)[:, None, None, None]
    places = jnp.sum(jnp.where(reached[None, :, None, :] == wanted[..., None], order, 0), 0)
    bits = lax.shift_left(1, jnp.arange(reached.shape[1], dtype=jnp.int32))
    masks = jnp.sum(jnp.where(places > 0, bits, 0), -1)
    return places - 1, masks


def per_device(a_blocks, p_blocks, a_cols, p_slots, touched, touch_cols, halo_rows):
    nrow = lax.axis_size("row")
    nslab = lax.axis_size("slab")
    slab_at = lax.axis_index("slab")
    cap = touched.shape[2]
    slots = touched.shape[1] * cap
    table = touched.reshape(slots)
    patterns = touch_cols.reshape(slots, touch_cols.shape[3])
    kc = patterns.shape[1]
    coarse_ids = (slab_at * nrow + p_slots // cap) * NC + lookup(table, p_slots)
    lists = halo_rows[0]
    sent_blocks = p_blocks[lists]
    sent_ids = coarse_ids[lists]
    routes = (
        (1, "slab", [(i, i + 1) for i in range(nslab - 1)]),
        (0, "slab", [(i + 1, i) for i in range(nslab - 1)]),
        (3, "row", [(i, i + 1) for i in range(nrow - 1)]),
        (2, "row", [(i + 1, i) for i in range(nrow - 1)]),
    )
    halo_ids = jnp.concatenate([lax.ppermute(sent_ids[n], axis, way) for n, axis, way in routes], 0)
    halo = jnp.concatenate([lax.ppermute(sent_blocks[n], axis, way) for n, axis, way in routes], 0)
    ext_ids = jnp.concatenate([coarse_ids, halo_ids], 0)
    places, masks = find_matches(ext_ids, a_cols, p_slots, patterns)
    partial = coarse_partials(
        a_cols.reshape(-1), p_slots.reshape(-1), masks.reshape(-1), places.reshape(-1), a_blocks, p_blocks, halo, slots, kc
    )
    width = a_blocks.shape[1]
    parts = lax.all_to_all(partial.reshape(nrow, cap * width, kc * width), "row", 0, 0)
    ids = lax.all_to_all(touched[0], "row", 0, 0)
    return sum_parts(ids.reshape(-1), parts.reshape(slots, width, kc * width))


def solution(mesh):
    in_specs = (
        P(("slab", "row"), None, None),
        P(("slab", "row"), None, None),
        P(("slab", "row"), None),
        P(("slab", "row"), None),
        P(("slab", "row"), None, None),
        P(("slab", "row"), None, None, None),
        P(("slab", "row"), None, None),
    )
    out_specs = P(("slab", "row"), None, None)
    return jax.shard_map(per_device, mesh=mesh, in_specs=in_specs, out_specs=out_specs, check_vma=False)
```

```python
import functools

import jax
import jax.numpy as jnp
from jax import lax
from jax.experimental import pallas as pl
from jax.experimental.pallas import tpu as pltpu
from jax.sharding import PartitionSpec as P

NC = 4
UNROLL = 8
BLOCKS = 144
IDS = 256


def load_operands(a_hbm, p_hbm, halo_hbm, a_v, ext_v, sems):
    rows = p_hbm.shape[0]
    return (
        pltpu.make_async_copy(a_hbm, a_v, sems.at[0]),
        pltpu.make_async_copy(p_hbm, ext_v.at[pl.ds(0, rows)], sems.at[1]),
        pltpu.make_async_copy(halo_hbm, ext_v.at[pl.ds(rows, halo_hbm.shape[0])], sems.at[2]),
    )


def all_products(cols, a_v, ext_v, g_v):
    rows, width, span = a_v.shape
    ka = span // width
    pairs = ext_v.shape[2] // (2 * width)
    pair = 2 * width

    def products(i, unused):
        row = a_v[i]
        for k in range(ka):
            right = ext_v[cols[i * ka + k]]
            value = jnp.dot(row[:, k * width : (k + 1) * width], right, preferred_element_type=jnp.float32).astype(
                jnp.bfloat16
            )
            for h in range(pairs):
                g_v[(i * ka + k) * pairs + h] = value[:, h * pair : (h + 1) * pair]
        return unused

    lax.fori_loop(0, rows, products, 0)


def add_items(count, items, ext_v, g_v, acc, width, ka):
    pair = 2 * width
    kp = ext_v.shape[2] // width
    upper = lax.broadcasted_iota(jnp.int32, (width, pair), 1) // width

    def batch(b, unused):
        found = []
        for u in range(UNROLL):
            word = items[b * UNROLL + u]
            target = word % 1024
            bit = (word // 1024) % 32
            im = word // 32768
            i = im // kp
            m = im % kp
            k = bit // kp
            q = bit % kp
            g = g_v[(i * ka + k) * (kp // 2) + q // 2]
            g = jnp.where(upper == q % 2, g, jnp.zeros_like(g))
            p = ext_v[i, :, pl.ds(pl.multiple_of((m // 2) * pair, pair), pair)]
            z = lax.dot_general(p, g, (((0,), (0,)), ((), ())), preferred_element_type=jnp.float32)
            z = jnp.where(m % 2 == 1, z[width:], z[:width])
            found.append((pl.ds(pl.multiple_of(target * width, width), width), z))
        for where, z in found:
            acc[where, :] = acc[where, :] + z
        return unused

    lax.fori_loop(0, (count + UNROLL - 1) // UNROLL, batch, 0)


def clear_rows(acc, step):
    def clear(n, unused):
        acc[pl.ds(pl.multiple_of(n * step, step), step), :] = jnp.zeros((step, acc.shape[1]), jnp.float32)
        return unused

    lax.fori_loop(0, acc.shape[0] // step, clear, 0)


def packed_kernel(
    cols, slots, masks, places, bases, a_hbm, p_hbm, halo_hbm, out_ref, ids_ref, count_ref, a_v, ext_v, g_v, acc, items, index, sems
):
    rows, width, span = a_v.shape
    ka = span // width
    kp = ext_v.shape[2] // width
    kq = ka * kp
    pair = 2 * width
    half = width // 2
    kc = index.shape[0] // bases.shape[0]
    copies = load_operands(a_hbm, p_hbm, halo_hbm, a_v, ext_v, sems)
    for copy in copies:
        copy.start()
    clear_rows(acc, 16 * width)

    def unset(n, unused):
        for u in range(8):
            index[n * 8 + u] = -1
        return unused

    lax.fori_loop(0, index.shape[0] // 8, unset, 0)

    def no_id(n, unused):
        for u in range(8):
            ids_ref[0, n * 8 + u] = -1
        return unused

    lax.fori_loop(0, ids_ref.shape[1] // 8, no_id, 0)

    def gather_items(im, state):
        slot = slots[im]
        base = bases[slot]
        head = im * 32

        def more(state):
            return state[0] != 0

        def take(state):
            mask, at, blocks = state
            bit = 31 - lax.clz(mask)
            place = places[im * kq + bit]
            old = index[slot * kc + place]
            fresh = old < 0
            block = jnp.where(fresh, blocks, old)
            index[slot * kc + place] = block
            kept = jnp.minimum(block, BLOCKS)
            ids_ref[0, kept] = base + place
            items[at] = (head + bit) * 1024 + kept
            return (mask - lax.shift_left(1, bit), at + 1, blocks + fresh.astype(jnp.int32))

        return lax.while_loop(more, take, (masks[im],) + state)[1:]

    count, blocks = lax.fori_loop(0, rows * kp, gather_items, (0, 0))
    for u in range(UNROLL):
        items[count + u] = BLOCKS
    count_ref[0] = blocks
    for copy in copies:
        copy.wait()
    all_products(cols, a_v, ext_v, g_v)
    add_items(count, items, ext_v, g_v, acc, width, ka)
    lower = lax.broadcasted_iota(jnp.int32, (16, pair), 1) < width

    def finish(n, unused):
        for r in range(half):
            one = acc[pl.ds(n * 16 * width + r, 16, stride=width), :]
            two = acc[pl.ds(n * 16 * width + half + r, 16, stride=width), :]
            one = one + pltpu.roll(one, width, 1)
            two = two + pltpu.roll(two, width, 1)
            out_ref[r, pl.ds(pl.multiple_of(n * 16, 16), 16), :] = jnp.where(lower, one, two).astype(jnp.bfloat16)
        return unused

    lax.fori_loop(0, BLOCKS // 16, finish, 0)


def packed_partials(cols, slots, masks, places, bases, a_blocks, p_blocks, halo, kc):
    rows, width, span = a_blocks.shape
    kp = p_blocks.shape[2] // width
    ka = span // width
    extended = rows + halo.shape[0]
    smem = pl.BlockSpec(memory_space=pltpu.SMEM)
    vmem = pl.BlockSpec(memory_space=pltpu.VMEM)
    hbm = pl.BlockSpec(memory_space=pl.ANY)
    return pl.pallas_call(
        packed_kernel,
        out_shape=(
            jax.ShapeDtypeStruct((width // 2, BLOCKS, 2 * width), jnp.bfloat16),
            jax.ShapeDtypeStruct((1, IDS), jnp.int32),
            jax.ShapeDtypeStruct((1,), jnp.int32),
        ),
        in_specs=[smem, smem, smem, smem, smem, hbm, hbm, hbm],
        out_specs=(vmem, smem, smem),
        scratch_shapes=[
            pltpu.VMEM((rows, width, span), jnp.bfloat16),
            pltpu.VMEM((extended, width, kp * width), jnp.bfloat16),
            pltpu.VMEM((rows * ka * (kp // 2), width, 2 * width), jnp.bfloat16),
            pltpu.VMEM(((BLOCKS + 16) * width, 2 * width), jnp.float32),
            pltpu.SMEM((rows * kp * ka * kp + UNROLL,), jnp.int32),
            pltpu.SMEM((bases.shape[0] * kc,), jnp.int32),
            pltpu.SemaphoreType.DMA((3,)),
        ],
        compiler_params=pltpu.CompilerParams(vmem_limit_bytes=48 * 2**20),
        name="packed_partials",
    )(cols, slots, masks, places, bases, a_blocks, p_blocks, halo)


def exchange_kernel(count, *refs):
    sends, takes = refs[:count], refs[count : 2 * count]
    here_sem, send_sem, take_sem = refs[2 * count :]
    me = lax.axis_index("row")
    n = lax.axis_size("row")
    barrier = pltpu.get_barrier_semaphore()

    def greet(o, unused):
        pl.semaphore_signal(
            barrier, inc=1, device_id={"row": lax.rem(me + o, n)}, device_id_type=pl.DeviceIdType.MESH
        )
        return unused

    lax.fori_loop(1, n, greet, 0)
    pl.semaphore_wait(barrier, n - 1)

    def source(x, to):
        return sends[x].at[to] if sends[x].shape[0] == n else sends[x].at[0]

    def remote(x, o):
        to = lax.rem(me + o, n)
        return pltpu.make_async_remote_copy(
            src_ref=source(x, to),
            dst_ref=takes[x].at[me],
            send_sem=send_sem.at[x, o],
            recv_sem=take_sem.at[x, o],
            device_id={"row": to},
            device_id_type=pl.DeviceIdType.MESH,
        )

    def arriving(x, o):
        came = lax.rem(me + n - o, n)
        return pltpu.make_async_remote_copy(
            src_ref=source(x, came),
            dst_ref=takes[x].at[came],
            send_sem=send_sem.at[x, o],
            recv_sem=take_sem.at[x, o],
            device_id={"row": came},
            device_id_type=pl.DeviceIdType.MESH,
        )

    def begin(o, unused):
        for x in range(count):
            remote(x, o).start()
        return unused

    lax.fori_loop(1, n, begin, 0)
    for x in range(count):
        pltpu.make_async_copy(source(x, me), takes[x].at[me], here_sem.at[x]).start()

    def end(o, unused):
        for x in range(count):
            remote(x, o).wait_send()
            arriving(x, o).wait_recv()
        return unused

    lax.fori_loop(1, n, end, 0)
    for x in range(count):
        pltpu.make_async_copy(source(x, me), takes[x].at[me], here_sem.at[x]).wait()


def exchange(arrays, n, collective_id):
    hbm = pl.BlockSpec(memory_space=pl.ANY)
    count = len(arrays)
    return pl.pallas_call(
        functools.partial(exchange_kernel, count),
        out_shape=tuple(jax.ShapeDtypeStruct((n,) + x.shape[1:], x.dtype) for x in arrays),
        in_specs=[hbm] * count,
        out_specs=(hbm,) * count,
        scratch_shapes=[
            pltpu.SemaphoreType.DMA((count,)),
            pltpu.SemaphoreType.DMA((count, n)),
            pltpu.SemaphoreType.DMA((count, n)),
        ],
        compiler_params=pltpu.CompilerParams(collective_id=collective_id, has_side_effects=True),
        name="exchange",
    )(*arrays)


def relay_kernel(ids_ref, parts_ref, out_ref, acc):
    n, blocks, lanes = parts_ref.shape
    targets = acc.shape[0]
    acc[...] = jnp.zeros_like(acc)
    order = lax.broadcasted_iota(jnp.int32, (targets, blocks), 0)

    def one(d, unused):
        hot = jnp.where(order == ids_ref[d, :, :blocks], 1.0, 0.0).astype(jnp.bfloat16)
        acc[...] += jnp.dot(hot, parts_ref[d], preferred_element_type=jnp.float32)
        return unused

    lax.fori_loop(0, n, one, 0)
    out_ref[...] = acc[...].astype(jnp.bfloat16)


def relay_sums(ids, parts, targets):
    vmem = pl.BlockSpec(memory_space=pltpu.VMEM)
    return pl.pallas_call(
        relay_kernel,
        out_shape=jax.ShapeDtypeStruct((targets, parts.shape[2]), jnp.bfloat16),
        in_specs=[vmem, vmem],
        out_specs=vmem,
        scratch_shapes=[pltpu.VMEM((targets, parts.shape[2]), jnp.float32)],
        compiler_params=pltpu.CompilerParams(vmem_limit_bytes=32 * 2**20),
        name="relay_sums",
    )(ids, parts)


def assemble_kernel(pieces_ref, out_ref, wide):
    n, targets, pair = pieces_ref.shape
    owned, width, outspan = out_ref.shape
    half = width // 2
    kc = targets // owned
    lower = lax.broadcasted_iota(jnp.int32, (half, pair), 1) < half * 2
    wide[...] = pieces_ref[...].reshape(n * targets, pair).astype(jnp.float32)
    for g in range(owned):
        for h in range(kc // 2):
            one = wide[pl.ds(g * kc + 2 * h, n, stride=targets), :]
            two = wide[pl.ds(g * kc + 2 * h + 1, n, stride=targets), :]
            span = slice(h * pair, (h + 1) * pair)
            out_ref[g, :half, span] = jnp.where(lower, one, pltpu.roll(two, width, 1))
            out_ref[g, half:, span] = jnp.where(lower, pltpu.roll(one, width, 1), two)


def assemble(pieces, width, kc):
    vmem = pl.BlockSpec(memory_space=pltpu.VMEM)
    n, targets, pair = pieces.shape
    return pl.pallas_call(
        assemble_kernel,
        out_shape=jax.ShapeDtypeStruct((NC, width, kc * width), jnp.float32),
        in_specs=[vmem],
        out_specs=vmem,
        scratch_shapes=[pltpu.VMEM((n * targets, pair), jnp.float32)],
        name="assemble",
    )(pieces)


def coarse_kernel(cols, slots, masks, places, a_hbm, p_hbm, halo_hbm, out_ref, a_v, ext_v, g_v, acc, items, sems):
    rows, width, span = a_v.shape
    ka = span // width
    kp = ext_v.shape[2] // width
    kq = ka * kp
    nslots, _, outspan = out_ref.shape
    kc = outspan // width
    pair = 2 * width
    copies = load_operands(a_hbm, p_hbm, halo_hbm, a_v, ext_v, sems)
    for copy in copies:
        copy.start()
    clear_rows(acc, width)

    def gather_items(im, count):
        slot = slots[im]
        head = im * 32

        def more(state):
            return state[0] != 0

        def take(state):
            mask, at = state
            bit = 31 - lax.clz(mask)
            items[at] = (head + bit) * 1024 + slot * kc + places[im * kq + bit]
            return (mask - lax.shift_left(1, bit), at + 1)

        return lax.while_loop(more, take, (masks[im], count))[1]

    count = lax.fori_loop(0, rows * kp, gather_items, 0)
    for u in range(UNROLL):
        items[count + u] = nslots * kc
    for copy in copies:
        copy.wait()
    all_products(cols, a_v, ext_v, g_v)
    add_items(count, items, ext_v, g_v, acc, width, ka)
    lower = lax.broadcasted_iota(jnp.int32, (width, pair), 1) < width

    def finish(t, unused):
        for h in range(kc // 2):
            one = acc[pl.ds(pl.multiple_of((t * kc + 2 * h) * width, width), width), :]
            two = acc[pl.ds(pl.multiple_of((t * kc + 2 * h + 1) * width, width), width), :]
            one = one + pltpu.roll(one, width, 1)
            two = two + pltpu.roll(two, width, 1)
            out_ref[t, :, h * pair : (h + 1) * pair] = jnp.where(lower, one, two).astype(jnp.bfloat16)
        return unused

    lax.fori_loop(0, nslots, finish, 0)


def coarse_partials(cols, slots, masks, places, a_blocks, p_blocks, halo, nslots, kc):
    rows, width, span = a_blocks.shape
    kp = p_blocks.shape[2] // width
    ka = span // width
    extended = rows + halo.shape[0]
    smem = pl.BlockSpec(memory_space=pltpu.SMEM)
    hbm = pl.BlockSpec(memory_space=pl.ANY)
    return pl.pallas_call(
        coarse_kernel,
        out_shape=jax.ShapeDtypeStruct((nslots, width, kc * width), jnp.bfloat16),
        in_specs=[smem, smem, smem, smem, hbm, hbm, hbm],
        out_specs=pl.BlockSpec(memory_space=pltpu.VMEM),
        scratch_shapes=[
            pltpu.VMEM((rows, width, span), jnp.bfloat16),
            pltpu.VMEM((extended, width, kp * width), jnp.bfloat16),
            pltpu.VMEM((rows * ka * (kp // 2), width, 2 * width), jnp.bfloat16),
            pltpu.VMEM(((nslots * kc + 1) * width, 2 * width), jnp.float32),
            pltpu.SMEM((rows * kp * ka * kp + UNROLL,), jnp.int32),
            pltpu.SemaphoreType.DMA((3,)),
        ],
        compiler_params=pltpu.CompilerParams(vmem_limit_bytes=56 * 2**20),
        name="coarse_partials",
    )(cols, slots, masks, places, a_blocks, p_blocks, halo)


def sum_kernel(ids, parts, out_ref):
    out_ref[...] = jnp.zeros_like(out_ref)

    def one(n, unused):
        row = ids[n]

        @pl.when(row >= 0)
        def _():
            out_ref[row] = out_ref[row] + parts[n].astype(jnp.float32)

        return unused

    lax.fori_loop(0, parts.shape[0], one, 0)


def sum_parts(ids, parts):
    return pl.pallas_call(
        sum_kernel,
        out_shape=jax.ShapeDtypeStruct((NC,) + parts.shape[1:], jnp.float32),
        in_specs=[pl.BlockSpec(memory_space=pltpu.SMEM), pl.BlockSpec(memory_space=pltpu.VMEM)],
        out_specs=pl.BlockSpec(memory_space=pltpu.VMEM),
        compiler_params=pltpu.CompilerParams(vmem_limit_bytes=32 * 2**20),
        name="sum_parts",
    )(ids, parts)


def lookup(table, index):
    hot = index[..., None] == jnp.arange(table.shape[0], dtype=jnp.int32)
    return jnp.sum(jnp.where(hot, table, 0), axis=-1)


def find_matches(ext_ids, a_cols, p_slots, patterns):
    rows = a_cols.shape[0]
    kp = p_slots.shape[1]
    reached = jnp.stack([lookup(ext_ids[:, q], a_cols) for q in range(kp)], -1).reshape(rows, -1)
    wanted = jnp.stack([lookup(patterns[:, j], p_slots) for j in range(patterns.shape[1])], 0)
    order = jnp.arange(1, patterns.shape[1] + 1, dtype=jnp.int32)[:, None, None, None]
    places = jnp.sum(jnp.where(reached[None, :, None, :] == wanted[..., None], order, 0), 0)
    bits = lax.shift_left(1, jnp.arange(reached.shape[1], dtype=jnp.int32))
    masks = jnp.sum(jnp.where(places > 0, bits, 0), -1)
    return places - 1, masks


def per_device(a_blocks, p_blocks, a_cols, p_slots, touched, touch_cols, halo_rows):
    nrow = lax.axis_size("row")
    nslab = lax.axis_size("slab")
    slab_at = lax.axis_index("slab")
    cap = touched.shape[2]
    slots = touched.shape[1] * cap
    table = touched.reshape(slots)
    patterns = touch_cols.reshape(slots, touch_cols.shape[3])
    kc = patterns.shape[1]
    coarse_ids = (slab_at * nrow + p_slots // cap) * NC + lookup(table, p_slots)
    lists = halo_rows[0]
    sent_blocks = p_blocks[lists]
    sent_ids = coarse_ids[lists]
    routes = (
        (1, "slab", [(i, i + 1) for i in range(nslab - 1)]),
        (0, "slab", [(i + 1, i) for i in range(nslab - 1)]),
        (3, "row", [(i, i + 1) for i in range(nrow - 1)]),
        (2, "row", [(i + 1, i) for i in range(nrow - 1)]),
    )
    halo_ids = jnp.concatenate([lax.ppermute(sent_ids[n], axis, way) for n, axis, way in routes], 0)
    halo = jnp.concatenate([lax.ppermute(sent_blocks[n], axis, way) for n, axis, way in routes], 0)
    ext_ids = jnp.concatenate([coarse_ids, halo_ids], 0)
    places, masks = find_matches(ext_ids, a_cols, p_slots, patterns)
    width = a_blocks.shape[1]
    lists_in = (a_cols.reshape(-1), p_slots.reshape(-1), masks.reshape(-1), places.reshape(-1))
    bases = (jnp.arange(slots, dtype=jnp.int32) // cap * NC + table) * kc
    packed, ids, blocks = packed_partials(*lists_in, bases, a_blocks, p_blocks, halo, kc)
    most = lax.pmax(blocks[0], ("slab", "row"))
    parts, part_ids = exchange((packed, ids.reshape(1, 1, IDS)), nrow, 0)
    sums = relay_sums(part_ids, parts, nrow * NC * kc)
    (pieces,) = exchange((sums.reshape(nrow, NC * kc, 2 * width),), nrow, 1)
    result = assemble(pieces, width, kc)

    def whole(unused):
        partial = coarse_partials(*lists_in, a_blocks, p_blocks, halo, slots, kc)
        parts = lax.all_to_all(partial.reshape(nrow, cap * width, kc * width), "row", 0, 0)
        owners = lax.all_to_all(touched[0], "row", 0, 0)
        return sum_parts(owners.reshape(-1), parts.reshape(slots, width, kc * width))

    return lax.cond(most > BLOCKS, whole, lambda x: x, result)


def solution(mesh):
    in_specs = (
        P(("slab", "row"), None, None),
        P(("slab", "row"), None, None),
        P(("slab", "row"), None),
        P(("slab", "row"), None),
        P(("slab", "row"), None, None),
        P(("slab", "row"), None, None, None),
        P(("slab", "row"), None, None),
    )
    out_specs = P(("slab", "row"), None, None)
    return jax.shard_map(per_device, mesh=mesh, in_specs=in_specs, out_specs=out_specs, check_vma=False)
```

```python
import functools

import jax
import jax.numpy as jnp
from jax import lax
from jax.experimental import pallas as pl
from jax.experimental.pallas import tpu as pltpu
from jax.sharding import PartitionSpec as P

NC = 4
UNROLL = 16
BLOCKS = 144
IDS = 256


def load_operands(a_hbm, p_hbm, halo_hbm, a_v, ext_v, sems):
    rows = p_hbm.shape[0]
    return (
        pltpu.make_async_copy(a_hbm, a_v, sems.at[0]),
        pltpu.make_async_copy(p_hbm, ext_v.at[pl.ds(0, rows)], sems.at[1]),
        pltpu.make_async_copy(halo_hbm, ext_v.at[pl.ds(rows, halo_hbm.shape[0])], sems.at[2]),
    )


def all_products(cols, a_v, ext_v, g_v, pt_v):
    rows, width, span = a_v.shape
    ka = span // width
    pairs = ext_v.shape[2] // (2 * width)
    pair = 2 * width

    def products(i, unused):
        row = a_v[i]
        turned = ext_v[i].T
        for m in range(2 * pairs):
            pt_v[i * 2 * pairs + m] = turned[m * width : (m + 1) * width, :]
        for k in range(ka):
            right = ext_v[cols[i * ka + k]]
            value = jnp.dot(row[:, k * width : (k + 1) * width], right, preferred_element_type=jnp.float32).astype(
                jnp.bfloat16
            )
            for h in range(pairs):
                g_v[(i * ka + k) * pairs + h] = value[:, h * pair : (h + 1) * pair]
        return unused

    lax.fori_loop(0, rows, products, 0)


def add_items(count, items, pt_v, g_v, acc, width, ka, kp):
    pair = 2 * width
    upper = (lax.broadcasted_iota(jnp.int32, (width, pair), 1) >= width).astype(jnp.int32)

    def batch(b, unused):
        found = []
        for u in range(UNROLL):
            word = items[b * UNROLL + u]
            target = word & 1023
            bit = lax.shift_right_logical(word, 10) & 31
            im = lax.shift_right_logical(word, 15)
            g = g_v[lax.shift_right_logical(im, kp.bit_length() - 1) * (ka * kp // 2) + lax.shift_right_logical(bit, 1)]
            g = jnp.where(upper == (bit & 1), g, jnp.zeros_like(g))
            z = jnp.dot(pt_v[im], g, preferred_element_type=jnp.float32)
            found.append((pl.ds(pl.multiple_of(target * width, width), width), z))
        for where, z in found:
            acc[where, :] = acc[where, :] + z
        return unused

    lax.fori_loop(0, lax.div(count + UNROLL - 1, UNROLL), batch, 0)


def clear_rows(acc, step):
    def clear(n, unused):
        acc[pl.ds(pl.multiple_of(n * step, step), step), :] = jnp.zeros((step, acc.shape[1]), jnp.float32)
        return unused

    lax.fori_loop(0, acc.shape[0] // step, clear, 0)


def packed_kernel(
    cols, slots, masks, places, bases, a_hbm, p_hbm, halo_hbm, out_ref, ids_ref, a_v, ext_v, g_v, pt_v, acc, items, index, sems
):
    rows, width, span = a_v.shape
    ka = span // width
    kp = ext_v.shape[2] // width
    kq = ka * kp
    pair = 2 * width
    half = width // 2
    kc = index.shape[0] // bases.shape[0]
    copies = load_operands(a_hbm, p_hbm, halo_hbm, a_v, ext_v, sems)
    for copy in copies:
        copy.start()
    clear_rows(acc, 16 * width)

    def unset(n, unused):
        for u in range(8):
            index[n * 8 + u] = -1
        return unused

    lax.fori_loop(0, index.shape[0] // 8, unset, 0)

    def no_id(n, unused):
        for u in range(8):
            ids_ref[0, n * 8 + u] = -1
        return unused

    lax.fori_loop(0, ids_ref.shape[1] // 8, no_id, 0)

    def gather_items(im, state):
        slot = slots[im]
        base = bases[slot]
        head = im * 32

        def more(state):
            return state[0] != 0

        def take(state):
            mask, at, blocks = state
            bit = 31 - lax.clz(mask)
            place = places[im * kq + bit]
            old = index[slot * kc + place]
            fresh = old < 0
            block = jnp.where(fresh, blocks, old)
            index[slot * kc + place] = block
            kept = jnp.minimum(block, BLOCKS)
            ids_ref[0, kept] = base + place
            items[at] = (head + bit) * 1024 + kept
            return (mask - lax.shift_left(1, bit), at + 1, blocks + fresh.astype(jnp.int32))

        return lax.while_loop(more, take, (masks[im],) + state)[1:]

    count, blocks = lax.fori_loop(0, rows * kp, gather_items, (0, 0))
    for u in range(UNROLL):
        items[count + u] = BLOCKS
    ids_ref[0, IDS - 1] = blocks
    for copy in copies:
        copy.wait()
    all_products(cols, a_v, ext_v, g_v, pt_v)
    add_items(count, items, pt_v, g_v, acc, width, ka, kp)
    lower = lax.broadcasted_iota(jnp.int32, (16, pair), 1) < width

    def finish(n, unused):
        for r in range(half):
            one = acc[pl.ds(n * 16 * width + r, 16, stride=width), :]
            two = acc[pl.ds(n * 16 * width + half + r, 16, stride=width), :]
            one = one + pltpu.roll(one, width, 1)
            two = two + pltpu.roll(two, width, 1)
            out_ref[r, pl.ds(pl.multiple_of(n * 16, 16), 16), :] = jnp.where(lower, one, two).astype(jnp.bfloat16)
        return unused

    lax.fori_loop(0, BLOCKS // 16, finish, 0)


def packed_partials(cols, slots, masks, places, bases, a_blocks, p_blocks, halo, kc):
    rows, width, span = a_blocks.shape
    kp = p_blocks.shape[2] // width
    ka = span // width
    extended = rows + halo.shape[0]
    smem = pl.BlockSpec(memory_space=pltpu.SMEM)
    vmem = pl.BlockSpec(memory_space=pltpu.VMEM)
    hbm = pl.BlockSpec(memory_space=pl.ANY)
    return pl.pallas_call(
        packed_kernel,
        out_shape=(
            jax.ShapeDtypeStruct((width // 2, BLOCKS, 2 * width), jnp.bfloat16),
            jax.ShapeDtypeStruct((1, IDS), jnp.int32),
        ),
        in_specs=[smem, smem, smem, smem, smem, hbm, hbm, hbm],
        out_specs=(vmem, smem),
        scratch_shapes=[
            pltpu.VMEM((rows, width, span), jnp.bfloat16),
            pltpu.VMEM((extended, width, kp * width), jnp.bfloat16),
            pltpu.VMEM((rows * ka * (kp // 2), width, 2 * width), jnp.bfloat16),
            pltpu.VMEM((rows * kp, width, width), jnp.bfloat16),
            pltpu.VMEM(((BLOCKS + 16) * width, 2 * width), jnp.float32),
            pltpu.SMEM((rows * kp * ka * kp + UNROLL,), jnp.int32),
            pltpu.SMEM((bases.shape[0] * kc,), jnp.int32),
            pltpu.SemaphoreType.DMA((3,)),
        ],
        compiler_params=pltpu.CompilerParams(vmem_limit_bytes=48 * 2**20),
        name="packed_partials",
    )(cols, slots, masks, places, bases, a_blocks, p_blocks, halo)


def exchange_kernel(axes, *refs):
    count = len(axes)
    sends, takes = refs[:count], refs[count : 2 * count]
    here_sem, send_sem, take_sem = refs[2 * count :]
    me = {axis: lax.axis_index(axis) for axis in axes}
    size = {axis: lax.axis_size(axis) for axis in axes}
    barrier = pltpu.get_barrier_semaphore()
    for axis in me:

        def greet(o, unused, axis=axis):
            to = lax.rem(me[axis] + o, size[axis])
            pl.semaphore_signal(barrier, inc=1, device_id={axis: to}, device_id_type=pl.DeviceIdType.MESH)
            return unused

        lax.fori_loop(1, size[axis], greet, 0)
    pl.semaphore_wait(barrier, sum(n - 1 for n in size.values()))

    def source(x, to):
        return sends[x].at[to] if sends[x].shape[0] > 1 else sends[x].at[0]

    def remote(x, o):
        axis = axes[x]
        to = lax.rem(me[axis] + o, size[axis])
        return pltpu.make_async_remote_copy(
            src_ref=source(x, to),
            dst_ref=takes[x].at[me[axis]],
            send_sem=send_sem.at[x, o],
            recv_sem=take_sem.at[x, o],
            device_id={axis: to},
            device_id_type=pl.DeviceIdType.MESH,
        )

    def arriving(x, o):
        axis = axes[x]
        came = lax.rem(me[axis] + size[axis] - o, size[axis])
        return pltpu.make_async_remote_copy(
            src_ref=source(x, came),
            dst_ref=takes[x].at[came],
            send_sem=send_sem.at[x, o],
            recv_sem=take_sem.at[x, o],
            device_id={axis: came},
            device_id_type=pl.DeviceIdType.MESH,
        )

    def here(x):
        at = me[axes[x]]
        return pltpu.make_async_copy(source(x, at), takes[x].at[at], here_sem.at[x])

    for x in range(count):

        def begin(o, unused, x=x):
            remote(x, o).start()
            return unused

        lax.fori_loop(1, size[axes[x]], begin, 0)
        here(x).start()
    for x in range(count):

        def end(o, unused, x=x):
            remote(x, o).wait_send()
            arriving(x, o).wait_recv()
            return unused

        lax.fori_loop(1, size[axes[x]], end, 0)
        here(x).wait()


def exchange(arrays, axes, collective_id):
    hbm = pl.BlockSpec(memory_space=pl.ANY)
    count = len(arrays)
    most = max(lax.axis_size(axis) for axis in axes)
    return pl.pallas_call(
        functools.partial(exchange_kernel, axes),
        out_shape=tuple(jax.ShapeDtypeStruct((lax.axis_size(a),) + x.shape[1:], x.dtype) for x, a in zip(arrays, axes)),
        in_specs=[hbm] * count,
        out_specs=(hbm,) * count,
        scratch_shapes=[
            pltpu.SemaphoreType.DMA((count,)),
            pltpu.SemaphoreType.DMA((count, most)),
            pltpu.SemaphoreType.DMA((count, most)),
        ],
        compiler_params=pltpu.CompilerParams(collective_id=collective_id, has_side_effects=True),
        name="exchange",
    )(*arrays)


def halo_kernel(blocks, ids, out_blocks, out_ids, send_sem, take_sem):
    barrier = pltpu.get_barrier_semaphore()
    routes = []
    for axis, way, chosen in (("slab", 1, 1), ("slab", -1, 0), ("row", 1, 3), ("row", -1, 2)):
        n = lax.axis_size(axis)
        routes.append(({axis: lax.rem(lax.axis_index(axis) + way + n, n)}, chosen))
    for to, chosen in routes:
        pl.semaphore_signal(barrier, inc=1, device_id=to, device_id_type=pl.DeviceIdType.MESH)
    pl.semaphore_wait(barrier, len(routes))
    copies = []
    for x, (to, chosen) in enumerate(routes):
        for y, (src, dst) in enumerate(((ids, out_ids), (blocks, out_blocks))):
            copies.append(
                pltpu.make_async_remote_copy(
                    src_ref=src.at[chosen],
                    dst_ref=dst.at[x],
                    send_sem=send_sem.at[y, x],
                    recv_sem=take_sem.at[y, x],
                    device_id=to,
                    device_id_type=pl.DeviceIdType.MESH,
                )
            )
            copies[-1].start()
    for copy in copies:
        copy.wait()


def exchange_halo(blocks, ids):
    hbm = pl.BlockSpec(memory_space=pl.ANY)
    return pl.pallas_call(
        halo_kernel,
        out_shape=(jax.ShapeDtypeStruct(blocks.shape, blocks.dtype), jax.ShapeDtypeStruct(ids.shape, ids.dtype)),
        in_specs=[hbm, hbm],
        out_specs=(hbm, hbm),
        scratch_shapes=[pltpu.SemaphoreType.DMA((2, 4)), pltpu.SemaphoreType.DMA((2, 4))],
        compiler_params=pltpu.CompilerParams(collective_id=2, has_side_effects=True),
        name="exchange_halo",
    )(blocks, ids)


def relay_kernel(ids_ref, parts_ref, out_ref, most_ref, acc):
    n, blocks, lanes = parts_ref.shape
    targets = acc.shape[0]
    acc[...] = jnp.zeros_like(acc)
    order = lax.broadcasted_iota(jnp.int32, (targets, blocks), 0)

    def one(d, unused):
        hot = jnp.where(order == ids_ref[d, :, :blocks], 1.0, 0.0).astype(jnp.bfloat16)
        acc[...] += jnp.dot(hot, parts_ref[d], preferred_element_type=jnp.float32)
        return unused

    lax.fori_loop(0, n, one, 0)
    out_ref[...] = acc[...].astype(jnp.bfloat16)
    ids = ids_ref[...]
    counts = jnp.where(lax.broadcasted_iota(jnp.int32, ids.shape, 2) == ids.shape[2] - 1, ids, 0)
    most_ref[...] = jnp.full(most_ref.shape, jnp.max(counts), jnp.int32)


def relay_sums(ids, parts, targets):
    vmem = pl.BlockSpec(memory_space=pltpu.VMEM)
    return pl.pallas_call(
        relay_kernel,
        out_shape=(
            jax.ShapeDtypeStruct((targets, parts.shape[2]), jnp.bfloat16),
            jax.ShapeDtypeStruct((1, 1, 128), jnp.int32),
        ),
        in_specs=[vmem, vmem],
        out_specs=(vmem, vmem),
        scratch_shapes=[pltpu.VMEM((targets, parts.shape[2]), jnp.float32)],
        compiler_params=pltpu.CompilerParams(vmem_limit_bytes=32 * 2**20),
        name="relay_sums",
    )(ids, parts)


def assemble_kernel(pieces_ref, out_ref, wide):
    n, targets, pair = pieces_ref.shape
    owned, width, outspan = out_ref.shape
    half = width // 2
    kc = targets // owned
    lower = lax.broadcasted_iota(jnp.int32, (half, pair), 1) < half * 2
    wide[...] = pieces_ref[...].reshape(n * targets, pair).astype(jnp.float32)
    for g in range(owned):
        for h in range(kc // 2):
            one = wide[pl.ds(g * kc + 2 * h, n, stride=targets), :]
            two = wide[pl.ds(g * kc + 2 * h + 1, n, stride=targets), :]
            span = slice(h * pair, (h + 1) * pair)
            out_ref[g, :half, span] = jnp.where(lower, one, pltpu.roll(two, width, 1))
            out_ref[g, half:, span] = jnp.where(lower, pltpu.roll(one, width, 1), two)


def assemble(pieces, width, kc):
    vmem = pl.BlockSpec(memory_space=pltpu.VMEM)
    n, targets, pair = pieces.shape
    return pl.pallas_call(
        assemble_kernel,
        out_shape=jax.ShapeDtypeStruct((NC, width, kc * width), jnp.float32),
        in_specs=[vmem],
        out_specs=vmem,
        scratch_shapes=[pltpu.VMEM((n * targets, pair), jnp.float32)],
        name="assemble",
    )(pieces)


def coarse_kernel(cols, slots, masks, places, a_hbm, p_hbm, halo_hbm, out_ref, a_v, ext_v, g_v, pt_v, acc, items, sems):
    rows, width, span = a_v.shape
    ka = span // width
    kp = ext_v.shape[2] // width
    kq = ka * kp
    nslots, _, outspan = out_ref.shape
    kc = outspan // width
    pair = 2 * width
    copies = load_operands(a_hbm, p_hbm, halo_hbm, a_v, ext_v, sems)
    for copy in copies:
        copy.start()
    clear_rows(acc, width)

    def gather_items(im, count):
        slot = slots[im]
        head = im * 32

        def more(state):
            return state[0] != 0

        def take(state):
            mask, at = state
            bit = 31 - lax.clz(mask)
            items[at] = (head + bit) * 1024 + slot * kc + places[im * kq + bit]
            return (mask - lax.shift_left(1, bit), at + 1)

        return lax.while_loop(more, take, (masks[im], count))[1]

    count = lax.fori_loop(0, rows * kp, gather_items, 0)
    for u in range(UNROLL):
        items[count + u] = nslots * kc
    for copy in copies:
        copy.wait()
    all_products(cols, a_v, ext_v, g_v, pt_v)
    add_items(count, items, pt_v, g_v, acc, width, ka, kp)
    lower = lax.broadcasted_iota(jnp.int32, (width, pair), 1) < width

    def finish(t, unused):
        for h in range(kc // 2):
            one = acc[pl.ds(pl.multiple_of((t * kc + 2 * h) * width, width), width), :]
            two = acc[pl.ds(pl.multiple_of((t * kc + 2 * h + 1) * width, width), width), :]
            one = one + pltpu.roll(one, width, 1)
            two = two + pltpu.roll(two, width, 1)
            out_ref[t, :, h * pair : (h + 1) * pair] = jnp.where(lower, one, two).astype(jnp.bfloat16)
        return unused

    lax.fori_loop(0, nslots, finish, 0)


def coarse_partials(cols, slots, masks, places, a_blocks, p_blocks, halo, nslots, kc):
    rows, width, span = a_blocks.shape
    kp = p_blocks.shape[2] // width
    ka = span // width
    extended = rows + halo.shape[0]
    smem = pl.BlockSpec(memory_space=pltpu.SMEM)
    hbm = pl.BlockSpec(memory_space=pl.ANY)
    return pl.pallas_call(
        coarse_kernel,
        out_shape=jax.ShapeDtypeStruct((nslots, width, kc * width), jnp.bfloat16),
        in_specs=[smem, smem, smem, smem, hbm, hbm, hbm],
        out_specs=pl.BlockSpec(memory_space=pltpu.VMEM),
        scratch_shapes=[
            pltpu.VMEM((rows, width, span), jnp.bfloat16),
            pltpu.VMEM((extended, width, kp * width), jnp.bfloat16),
            pltpu.VMEM((rows * ka * (kp // 2), width, 2 * width), jnp.bfloat16),
            pltpu.VMEM((rows * kp, width, width), jnp.bfloat16),
            pltpu.VMEM(((nslots * kc + 1) * width, 2 * width), jnp.float32),
            pltpu.SMEM((rows * kp * ka * kp + UNROLL,), jnp.int32),
            pltpu.SemaphoreType.DMA((3,)),
        ],
        compiler_params=pltpu.CompilerParams(vmem_limit_bytes=56 * 2**20),
        name="coarse_partials",
    )(cols, slots, masks, places, a_blocks, p_blocks, halo)


def sum_kernel(ids, parts, out_ref):
    out_ref[...] = jnp.zeros_like(out_ref)

    def one(n, unused):
        row = ids[n]

        @pl.when(row >= 0)
        def _():
            out_ref[row] = out_ref[row] + parts[n].astype(jnp.float32)

        return unused

    lax.fori_loop(0, parts.shape[0], one, 0)


def sum_parts(ids, parts):
    return pl.pallas_call(
        sum_kernel,
        out_shape=jax.ShapeDtypeStruct((NC,) + parts.shape[1:], jnp.float32),
        in_specs=[pl.BlockSpec(memory_space=pltpu.SMEM), pl.BlockSpec(memory_space=pltpu.VMEM)],
        out_specs=pl.BlockSpec(memory_space=pltpu.VMEM),
        compiler_params=pltpu.CompilerParams(vmem_limit_bytes=32 * 2**20),
        name="sum_parts",
    )(ids, parts)


def lookup(table, index):
    hot = index[..., None] == jnp.arange(table.shape[0], dtype=jnp.int32)
    return jnp.sum(jnp.where(hot, table, 0), axis=-1)


def find_matches(ext_ids, a_cols, p_slots, patterns):
    rows = a_cols.shape[0]
    kp = p_slots.shape[1]
    reached = jnp.stack([lookup(ext_ids[:, q], a_cols) for q in range(kp)], -1).reshape(rows, -1)
    wanted = jnp.stack([lookup(patterns[:, j], p_slots) for j in range(patterns.shape[1])], 0)
    order = jnp.arange(1, patterns.shape[1] + 1, dtype=jnp.int32)[:, None, None, None]
    places = jnp.sum(jnp.where(reached[None, :, None, :] == wanted[..., None], order, 0), 0)
    bits = lax.shift_left(1, jnp.arange(reached.shape[1], dtype=jnp.int32))
    masks = jnp.sum(jnp.where(places > 0, bits, 0), -1)
    return places - 1, masks


def per_device(a_blocks, p_blocks, a_cols, p_slots, touched, touch_cols, halo_rows):
    nrow = lax.axis_size("row")
    nslab = lax.axis_size("slab")
    slab_at = lax.axis_index("slab")
    cap = touched.shape[2]
    slots = touched.shape[1] * cap
    table = touched.reshape(slots)
    patterns = touch_cols.reshape(slots, touch_cols.shape[3])
    kc = patterns.shape[1]
    coarse_ids = (slab_at * nrow + p_slots // cap) * NC + lookup(table, p_slots)
    lists = halo_rows[0]
    sent_blocks = p_blocks[lists]
    sent_ids = coarse_ids[lists]
    depth = lists.shape[1]
    kp = p_slots.shape[1]
    row_at = lax.axis_index("row")
    ids_out = jnp.pad(sent_ids.reshape(4, 1, depth * kp), ((0, 0), (0, 0), (0, 128 - depth * kp)))
    halo, halo_ids = exchange_halo(sent_blocks, ids_out)
    outside = jnp.stack([slab_at == 0, slab_at == nslab - 1, row_at == 0, row_at == nrow - 1])
    halo_ids = jnp.where(outside[:, None], -1, halo_ids[:, 0, : depth * kp]).reshape(4 * depth, kp)
    halo = halo.reshape((4 * depth,) + halo.shape[2:])
    ext_ids = jnp.concatenate([coarse_ids, halo_ids], 0)
    places, masks = find_matches(ext_ids, a_cols, p_slots, patterns)
    width = a_blocks.shape[1]
    lists_in = (a_cols.reshape(-1), p_slots.reshape(-1), masks.reshape(-1), places.reshape(-1))
    bases = (jnp.arange(slots, dtype=jnp.int32) // cap * NC + table) * kc
    packed, ids = packed_partials(*lists_in, bases, a_blocks, p_blocks, halo, kc)
    parts, part_ids = exchange((packed, ids.reshape(1, 1, IDS)), ("row", "row"), 0)
    sums, most = relay_sums(part_ids, parts, nrow * NC * kc)
    pieces, counts = exchange((sums.reshape(nrow, NC * kc, 2 * width), most), ("row", "slab"), 1)

    def whole(unused):
        partial = coarse_partials(*lists_in, a_blocks, p_blocks, halo, slots, kc)
        parts = lax.all_to_all(partial.reshape(nrow, cap * width, kc * width), "row", 0, 0)
        owners = lax.all_to_all(touched[0], "row", 0, 0)
        return sum_parts(owners.reshape(-1), parts.reshape(slots, width, kc * width))

    return lax.cond(jnp.max(counts) > BLOCKS, whole, lambda unused: assemble(pieces, width, kc), 0)


def solution(mesh):
    in_specs = (
        P(("slab", "row"), None, None),
        P(("slab", "row"), None, None),
        P(("slab", "row"), None),
        P(("slab", "row"), None),
        P(("slab", "row"), None, None),
        P(("slab", "row"), None, None, None),
        P(("slab", "row"), None, None),
    )
    out_specs = P(("slab", "row"), None, None)
    return jax.shard_map(per_device, mesh=mesh, in_specs=in_specs, out_specs=out_specs, check_vma=False)
```

```python
import functools

import jax
import jax.numpy as jnp
from jax import lax
from jax.experimental import pallas as pl
from jax.experimental.pallas import tpu as pltpu
from jax.sharding import PartitionSpec as P

NC = 4
UNROLL = 16
BLOCKS = 144
IDS = 256


def load_operands(a_hbm, p_hbm, halo_hbm, a_v, ext_v, sems):
    rows = p_hbm.shape[0]
    return (
        pltpu.make_async_copy(a_hbm, a_v, sems.at[0]),
        pltpu.make_async_copy(p_hbm, ext_v.at[pl.ds(0, rows)], sems.at[1]),
        pltpu.make_async_copy(halo_hbm, ext_v.at[pl.ds(rows, halo_hbm.shape[0])], sems.at[2]),
    )


def all_products(cols, a_v, ext_v, g_v, pt_v):
    rows, width, span = a_v.shape
    ka = span // width
    pairs = ext_v.shape[2] // (2 * width)
    pair = 2 * width

    def products(i, unused):
        row = a_v[i]
        turned = ext_v[i].T
        for m in range(2 * pairs):
            pt_v[i * 2 * pairs + m] = turned[m * width : (m + 1) * width, :]
        for k in range(ka):
            right = ext_v[cols[i * ka + k]]
            value = jnp.dot(row[:, k * width : (k + 1) * width], right, preferred_element_type=jnp.float32).astype(
                jnp.bfloat16
            )
            for h in range(pairs):
                g_v[(i * ka + k) * pairs + h] = value[:, h * pair : (h + 1) * pair]
        return unused

    lax.fori_loop(0, rows, products, 0)


def add_items(count, items, pt_v, g_v, acc, width, ka, kp):
    pair = 2 * width
    upper = (lax.broadcasted_iota(jnp.int32, (width, pair), 1) >= width).astype(jnp.int32)

    def batch(b, unused):
        found = []
        for u in range(UNROLL):
            word = items[b * UNROLL + u]
            target = word & 1023
            bit = lax.shift_right_logical(word, 10) & 31
            im = lax.shift_right_logical(word, 15)
            g = g_v[lax.shift_right_logical(im, kp.bit_length() - 1) * (ka * kp // 2) + lax.shift_right_logical(bit, 1)]
            g = jnp.where(upper == (bit & 1), g, jnp.zeros_like(g))
            z = jnp.dot(pt_v[im], g, preferred_element_type=jnp.float32)
            found.append((pl.ds(pl.multiple_of(target * width, width), width), z))
        for where, z in found:
            acc[where, :] = acc[where, :] + z
        return unused

    lax.fori_loop(0, lax.div(count + UNROLL - 1, UNROLL), batch, 0)


def clear_rows(acc, step):
    def clear(n, unused):
        acc[pl.ds(pl.multiple_of(n * step, step), step), :] = jnp.zeros((step, acc.shape[1]), jnp.float32)
        return unused

    lax.fori_loop(0, acc.shape[0] // step, clear, 0)


def packed_kernel(
    cols, slots, masks, places, bases, a_hbm, p_hbm, halo_hbm, out_ref, ids_ref, a_v, ext_v, g_v, pt_v, acc, items, index, sems
):
    rows, width, span = a_v.shape
    ka = span // width
    kp = ext_v.shape[2] // width
    kq = ka * kp
    pair = 2 * width
    half = width // 2
    kc = index.shape[0] // bases.shape[0]
    copies = load_operands(a_hbm, p_hbm, halo_hbm, a_v, ext_v, sems)
    for copy in copies:
        copy.start()
    clear_rows(acc, 16 * width)

    def unset(n, unused):
        for u in range(8):
            index[n * 8 + u] = -1
        return unused

    lax.fori_loop(0, index.shape[0] // 8, unset, 0)

    def no_id(n, unused):
        for u in range(8):
            ids_ref[0, n * 8 + u] = -1
        return unused

    lax.fori_loop(0, ids_ref.shape[1] // 8, no_id, 0)

    def gather_items(im, state):
        slot = slots[im]
        base = bases[slot]
        head = im * 32

        def more(state):
            return state[0] != 0

        def take(state):
            mask, at, blocks = state
            bit = 31 - lax.clz(mask)
            place = places[im * kq + bit]
            old = index[slot * kc + place]
            fresh = old < 0
            block = jnp.where(fresh, blocks, old)
            index[slot * kc + place] = block
            kept = jnp.minimum(block, BLOCKS)
            ids_ref[0, kept] = base + place
            items[at] = (head + bit) * 1024 + kept
            return (mask - lax.shift_left(1, bit), at + 1, blocks + fresh.astype(jnp.int32))

        return lax.while_loop(more, take, (masks[im],) + state)[1:]

    count, blocks = lax.fori_loop(0, rows * kp, gather_items, (0, 0))
    for u in range(UNROLL):
        items[count + u] = BLOCKS
    ids_ref[0, IDS - 1] = blocks
    for copy in copies:
        copy.wait()
    all_products(cols, a_v, ext_v, g_v, pt_v)
    add_items(count, items, pt_v, g_v, acc, width, ka, kp)
    lower = lax.broadcasted_iota(jnp.int32, (16, pair), 1) < width

    def finish(n, unused):
        for r in range(half):
            one = acc[pl.ds(n * 16 * width + r, 16, stride=width), :]
            two = acc[pl.ds(n * 16 * width + half + r, 16, stride=width), :]
            one = one + pltpu.roll(one, width, 1)
            two = two + pltpu.roll(two, width, 1)
            out_ref[r, pl.ds(pl.multiple_of(n * 16, 16), 16), :] = jnp.where(lower, one, two).astype(jnp.bfloat16)
        return unused

    lax.fori_loop(0, BLOCKS // 16, finish, 0)


def packed_partials(cols, slots, masks, places, bases, a_blocks, p_blocks, halo, kc):
    rows, width, span = a_blocks.shape
    kp = p_blocks.shape[2] // width
    ka = span // width
    extended = rows + halo.shape[0]
    smem = pl.BlockSpec(memory_space=pltpu.SMEM)
    vmem = pl.BlockSpec(memory_space=pltpu.VMEM)
    hbm = pl.BlockSpec(memory_space=pl.ANY)
    return pl.pallas_call(
        packed_kernel,
        out_shape=(
            jax.ShapeDtypeStruct((width // 2, BLOCKS, 2 * width), jnp.bfloat16),
            jax.ShapeDtypeStruct((1, IDS), jnp.int32),
        ),
        in_specs=[smem, smem, smem, smem, smem, hbm, hbm, hbm],
        out_specs=(vmem, smem),
        scratch_shapes=[
            pltpu.VMEM((rows, width, span), jnp.bfloat16),
            pltpu.VMEM((extended, width, kp * width), jnp.bfloat16),
            pltpu.VMEM((rows * ka * (kp // 2), width, 2 * width), jnp.bfloat16),
            pltpu.VMEM((rows * kp, width, width), jnp.bfloat16),
            pltpu.VMEM(((BLOCKS + 16) * width, 2 * width), jnp.float32),
            pltpu.SMEM((rows * kp * ka * kp + UNROLL,), jnp.int32),
            pltpu.SMEM((bases.shape[0] * kc,), jnp.int32),
            pltpu.SemaphoreType.DMA((3,)),
        ],
        compiler_params=pltpu.CompilerParams(vmem_limit_bytes=48 * 2**20),
        name="packed_partials",
    )(cols, slots, masks, places, bases, a_blocks, p_blocks, halo)


def halo_kernel(blocks, ids, out_blocks, out_ids, send_sem, take_sem):
    barrier = pltpu.get_barrier_semaphore()
    routes = []
    for axis, way, chosen in (("slab", 1, 1), ("slab", -1, 0), ("row", 1, 3), ("row", -1, 2)):
        n = lax.axis_size(axis)
        routes.append(({axis: lax.rem(lax.axis_index(axis) + way + n, n)}, chosen))
    for to, chosen in routes:
        pl.semaphore_signal(barrier, inc=1, device_id=to, device_id_type=pl.DeviceIdType.MESH)
    pl.semaphore_wait(barrier, len(routes))
    copies = []
    for x, (to, chosen) in enumerate(routes):
        for y, (src, dst) in enumerate(((ids, out_ids), (blocks, out_blocks))):
            copies.append(
                pltpu.make_async_remote_copy(
                    src_ref=src.at[chosen],
                    dst_ref=dst.at[x],
                    send_sem=send_sem.at[y, x],
                    recv_sem=take_sem.at[y, x],
                    device_id=to,
                    device_id_type=pl.DeviceIdType.MESH,
                )
            )
            copies[-1].start()
    for copy in copies:
        copy.wait()


def exchange_halo(blocks, ids):
    hbm = pl.BlockSpec(memory_space=pl.ANY)
    return pl.pallas_call(
        halo_kernel,
        out_shape=(jax.ShapeDtypeStruct(blocks.shape, blocks.dtype), jax.ShapeDtypeStruct(ids.shape, ids.dtype)),
        in_specs=[hbm, hbm],
        out_specs=(hbm, hbm),
        scratch_shapes=[pltpu.SemaphoreType.DMA((2, 4)), pltpu.SemaphoreType.DMA((2, 4))],
        compiler_params=pltpu.CompilerParams(collective_id=1, has_side_effects=True),
        name="exchange_halo",
    )(blocks, ids)


def reduce_kernel(
    parts, ids, pieces, most_ref, came_parts, came_ids, sums, flag, came_flags, acc, send_sem, take_sem, flag_send, flag_take
):
    row, slab = lax.axis_index("row"), lax.axis_index("slab")
    n, slabs = lax.axis_size("row"), lax.axis_size("slab")
    blocks = parts.shape[1]
    targets, lanes = acc.shape
    share = targets // n
    barrier = pltpu.get_barrier_semaphore()
    mesh_id = pl.DeviceIdType.MESH

    def greet_row(o, unused):
        pl.semaphore_signal(barrier, inc=1, device_id={"row": lax.rem(row + o, n)}, device_id_type=mesh_id)
        return unused

    def greet_slab(o, unused):
        pl.semaphore_signal(barrier, inc=1, device_id={"slab": lax.rem(slab + o, slabs)}, device_id_type=mesh_id)
        return unused

    lax.fori_loop(1, n, greet_row, 0)
    lax.fori_loop(1, slabs, greet_slab, 0)
    pl.semaphore_wait(barrier, n + slabs - 2)

    def row_copy(x, o, src, dst, other):
        return pltpu.make_async_remote_copy(
            src_ref=src,
            dst_ref=dst,
            send_sem=send_sem.at[x, o],
            recv_sem=take_sem.at[x, o],
            device_id={"row": other},
            device_id_type=mesh_id,
        )

    def to_of(o):
        return lax.rem(row + o, n)

    def from_of(o):
        return lax.rem(row + n - o, n)

    def begin(o, unused):
        to = to_of(o)
        row_copy(0, o, ids.at[0], came_ids.at[row], to).start()
        row_copy(1, o, parts.at[to], came_parts.at[row], to).start()
        return unused

    lax.fori_loop(1, n, begin, 0)
    order = lax.broadcasted_iota(jnp.int32, (targets, blocks), 0)

    def spread(names, values):
        hot = jnp.where(order == names[:, :blocks], 1.0, 0.0).astype(jnp.bfloat16)
        return jnp.dot(hot, values, preferred_element_type=jnp.float32)

    own = ids[0]
    acc[...] = spread(own, parts[row])
    last = lax.broadcasted_iota(jnp.int32, own.shape, 1) == own.shape[1] - 1

    def add(o, most):
        came = from_of(o)
        row_copy(0, o, ids.at[0], came_ids.at[came], came).wait_recv()
        row_copy(1, o, parts.at[came], came_parts.at[came], came).wait_recv()
        names = came_ids[came]
        acc[...] += spread(names, came_parts[came])
        return jnp.maximum(most, names)

    most = lax.fori_loop(1, n, add, own)
    flag[...] = jnp.where(last, most, 0)

    def flag_copy(o, at, other):
        return pltpu.make_async_remote_copy(
            src_ref=flag,
            dst_ref=came_flags.at[at],
            send_sem=flag_send.at[o],
            recv_sem=flag_take.at[o],
            device_id={"slab": other},
            device_id_type=mesh_id,
        )

    def begin_flag(o, unused):
        flag_copy(o, slab, lax.rem(slab + o, slabs)).start()
        return unused

    lax.fori_loop(1, slabs, begin_flag, 0)
    for p in range(n):
        sums[p] = acc[p * share : (p + 1) * share, :].astype(jnp.bfloat16)

    def begin_sums(o, unused):
        to = to_of(o)
        row_copy(2, o, sums.at[to], pieces.at[row], to).start()
        return unused

    lax.fori_loop(1, n, begin_sums, 0)
    pieces[row] = sums[row]

    def end_flag(o, most):
        came = lax.rem(slab + slabs - o, slabs)
        flag_copy(o, slab, lax.rem(slab + o, slabs)).wait_send()
        flag_copy(o, came, came).wait_recv()
        return jnp.maximum(most, came_flags[came])

    most_ref[...] = lax.fori_loop(1, slabs, end_flag, flag[...])

    def end(o, unused):
        to, came = to_of(o), from_of(o)
        row_copy(0, o, ids.at[0], came_ids.at[row], to).wait_send()
        row_copy(1, o, parts.at[to], came_parts.at[row], to).wait_send()
        row_copy(2, o, sums.at[to], pieces.at[row], to).wait_send()
        row_copy(2, o, sums.at[came], pieces.at[came], came).wait_recv()
        return unused

    lax.fori_loop(1, n, end, 0)


def reduce_parts(parts, ids, share):
    n, slabs = lax.axis_size("row"), lax.axis_size("slab")
    _, blocks, lanes = parts.shape
    vmem = pl.BlockSpec(memory_space=pltpu.VMEM)
    return pl.pallas_call(
        reduce_kernel,
        out_shape=(
            jax.ShapeDtypeStruct((n, share, lanes), jnp.bfloat16),
            jax.ShapeDtypeStruct((1, IDS), jnp.int32),
        ),
        in_specs=[vmem, vmem],
        out_specs=(vmem, vmem),
        scratch_shapes=[
            pltpu.VMEM((n, blocks, lanes), jnp.bfloat16),
            pltpu.VMEM((n, 1, IDS), jnp.int32),
            pltpu.VMEM((n, share, lanes), jnp.bfloat16),
            pltpu.VMEM((1, IDS), jnp.int32),
            pltpu.VMEM((slabs, 1, IDS), jnp.int32),
            pltpu.VMEM((n * share, lanes), jnp.float32),
            pltpu.SemaphoreType.DMA((3, n)),
            pltpu.SemaphoreType.DMA((3, n)),
            pltpu.SemaphoreType.DMA((slabs,)),
            pltpu.SemaphoreType.DMA((slabs,)),
        ],
        compiler_params=pltpu.CompilerParams(
            collective_id=0, has_side_effects=True, vmem_limit_bytes=32 * 2**20
        ),
        name="reduce_parts",
    )(parts, ids)


def assemble_kernel(pieces_ref, out_ref, wide):
    n, targets, pair = pieces_ref.shape
    owned, width, outspan = out_ref.shape
    half = width // 2
    kc = targets // owned
    lower = lax.broadcasted_iota(jnp.int32, (half, pair), 1) < half * 2
    wide[...] = pieces_ref[...].reshape(n * targets, pair).astype(jnp.float32)
    for g in range(owned):
        for h in range(kc // 2):
            one = wide[pl.ds(g * kc + 2 * h, n, stride=targets), :]
            two = wide[pl.ds(g * kc + 2 * h + 1, n, stride=targets), :]
            span = slice(h * pair, (h + 1) * pair)
            out_ref[g, :half, span] = jnp.where(lower, one, pltpu.roll(two, width, 1))
            out_ref[g, half:, span] = jnp.where(lower, pltpu.roll(one, width, 1), two)


def assemble(pieces, width, kc):
    vmem = pl.BlockSpec(memory_space=pltpu.VMEM)
    n, targets, pair = pieces.shape
    return pl.pallas_call(
        assemble_kernel,
        out_shape=jax.ShapeDtypeStruct((NC, width, kc * width), jnp.float32),
        in_specs=[vmem],
        out_specs=vmem,
        scratch_shapes=[pltpu.VMEM((n * targets, pair), jnp.float32)],
        name="assemble",
    )(pieces)


def coarse_kernel(cols, slots, masks, places, a_hbm, p_hbm, halo_hbm, out_ref, a_v, ext_v, g_v, pt_v, acc, items, sems):
    rows, width, span = a_v.shape
    ka = span // width
    kp = ext_v.shape[2] // width
    kq = ka * kp
    nslots, _, outspan = out_ref.shape
    kc = outspan // width
    pair = 2 * width
    copies = load_operands(a_hbm, p_hbm, halo_hbm, a_v, ext_v, sems)
    for copy in copies:
        copy.start()
    clear_rows(acc, width)

    def gather_items(im, count):
        slot = slots[im]
        head = im * 32

        def more(state):
            return state[0] != 0

        def take(state):
            mask, at = state
            bit = 31 - lax.clz(mask)
            items[at] = (head + bit) * 1024 + slot * kc + places[im * kq + bit]
            return (mask - lax.shift_left(1, bit), at + 1)

        return lax.while_loop(more, take, (masks[im], count))[1]

    count = lax.fori_loop(0, rows * kp, gather_items, 0)
    for u in range(UNROLL):
        items[count + u] = nslots * kc
    for copy in copies:
        copy.wait()
    all_products(cols, a_v, ext_v, g_v, pt_v)
    add_items(count, items, pt_v, g_v, acc, width, ka, kp)
    lower = lax.broadcasted_iota(jnp.int32, (width, pair), 1) < width

    def finish(t, unused):
        for h in range(kc // 2):
            one = acc[pl.ds(pl.multiple_of((t * kc + 2 * h) * width, width), width), :]
            two = acc[pl.ds(pl.multiple_of((t * kc + 2 * h + 1) * width, width), width), :]
            one = one + pltpu.roll(one, width, 1)
            two = two + pltpu.roll(two, width, 1)
            out_ref[t, :, h * pair : (h + 1) * pair] = jnp.where(lower, one, two).astype(jnp.bfloat16)
        return unused

    lax.fori_loop(0, nslots, finish, 0)


def coarse_partials(cols, slots, masks, places, a_blocks, p_blocks, halo, nslots, kc):
    rows, width, span = a_blocks.shape
    kp = p_blocks.shape[2] // width
    ka = span // width
    extended = rows + halo.shape[0]
    smem = pl.BlockSpec(memory_space=pltpu.SMEM)
    hbm = pl.BlockSpec(memory_space=pl.ANY)
    return pl.pallas_call(
        coarse_kernel,
        out_shape=jax.ShapeDtypeStruct((nslots, width, kc * width), jnp.bfloat16),
        in_specs=[smem, smem, smem, smem, hbm, hbm, hbm],
        out_specs=pl.BlockSpec(memory_space=pltpu.VMEM),
        scratch_shapes=[
            pltpu.VMEM((rows, width, span), jnp.bfloat16),
            pltpu.VMEM((extended, width, kp * width), jnp.bfloat16),
            pltpu.VMEM((rows * ka * (kp // 2), width, 2 * width), jnp.bfloat16),
            pltpu.VMEM((rows * kp, width, width), jnp.bfloat16),
            pltpu.VMEM(((nslots * kc + 1) * width, 2 * width), jnp.float32),
            pltpu.SMEM((rows * kp * ka * kp + UNROLL,), jnp.int32),
            pltpu.SemaphoreType.DMA((3,)),
        ],
        compiler_params=pltpu.CompilerParams(vmem_limit_bytes=56 * 2**20),
        name="coarse_partials",
    )(cols, slots, masks, places, a_blocks, p_blocks, halo)


def sum_kernel(ids, parts, out_ref):
    out_ref[...] = jnp.zeros_like(out_ref)

    def one(n, unused):
        row = ids[n]

        @pl.when(row >= 0)
        def _():
            out_ref[row] = out_ref[row] + parts[n].astype(jnp.float32)

        return unused

    lax.fori_loop(0, parts.shape[0], one, 0)


def sum_parts(ids, parts):
    return pl.pallas_call(
        sum_kernel,
        out_shape=jax.ShapeDtypeStruct((NC,) + parts.shape[1:], jnp.float32),
        in_specs=[pl.BlockSpec(memory_space=pltpu.SMEM), pl.BlockSpec(memory_space=pltpu.VMEM)],
        out_specs=pl.BlockSpec(memory_space=pltpu.VMEM),
        compiler_params=pltpu.CompilerParams(vmem_limit_bytes=32 * 2**20),
        name="sum_parts",
    )(ids, parts)


def lookup(table, index):
    hot = index[..., None] == jnp.arange(table.shape[0], dtype=jnp.int32)
    return jnp.sum(jnp.where(hot, table, 0), axis=-1)


def find_matches(ext_ids, a_cols, p_slots, patterns):
    rows = a_cols.shape[0]
    kp = p_slots.shape[1]
    reached = jnp.stack([lookup(ext_ids[:, q], a_cols) for q in range(kp)], -1).reshape(rows, -1)
    wanted = jnp.stack([lookup(patterns[:, j], p_slots) for j in range(patterns.shape[1])], 0)
    order = jnp.arange(1, patterns.shape[1] + 1, dtype=jnp.int32)[:, None, None, None]
    places = jnp.sum(jnp.where(reached[None, :, None, :] == wanted[..., None], order, 0), 0)
    bits = lax.shift_left(1, jnp.arange(reached.shape[1], dtype=jnp.int32))
    masks = jnp.sum(jnp.where(places > 0, bits, 0), -1)
    return places - 1, masks


def per_device(a_blocks, p_blocks, a_cols, p_slots, touched, touch_cols, halo_rows):
    nrow = lax.axis_size("row")
    nslab = lax.axis_size("slab")
    slab_at = lax.axis_index("slab")
    cap = touched.shape[2]
    slots = touched.shape[1] * cap
    table = touched.reshape(slots)
    patterns = touch_cols.reshape(slots, touch_cols.shape[3])
    kc = patterns.shape[1]
    coarse_ids = (slab_at * nrow + p_slots // cap) * NC + lookup(table, p_slots)
    lists = halo_rows[0]
    sent_blocks = p_blocks[lists]
    sent_ids = coarse_ids[lists]
    depth = lists.shape[1]
    kp = p_slots.shape[1]
    row_at = lax.axis_index("row")
    ids_out = jnp.pad(sent_ids.reshape(4, 1, depth * kp), ((0, 0), (0, 0), (0, 128 - depth * kp)))
    halo, halo_ids = exchange_halo(sent_blocks, ids_out)
    outside = jnp.stack([slab_at == 0, slab_at == nslab - 1, row_at == 0, row_at == nrow - 1])
    halo_ids = jnp.where(outside[:, None], -1, halo_ids[:, 0, : depth * kp]).reshape(4 * depth, kp)
    halo = halo.reshape((4 * depth,) + halo.shape[2:])
    ext_ids = jnp.concatenate([coarse_ids, halo_ids], 0)
    places, masks = find_matches(ext_ids, a_cols, p_slots, patterns)
    width = a_blocks.shape[1]
    lists_in = (a_cols.reshape(-1), p_slots.reshape(-1), masks.reshape(-1), places.reshape(-1))
    bases = (jnp.arange(slots, dtype=jnp.int32) // cap * NC + table) * kc
    packed, ids = packed_partials(*lists_in, bases, a_blocks, p_blocks, halo, kc)
    pieces, counts = reduce_parts(packed, ids.reshape(1, 1, IDS), NC * kc)

    def whole(unused):
        partial = coarse_partials(*lists_in, a_blocks, p_blocks, halo, slots, kc)
        parts = lax.all_to_all(partial.reshape(nrow, cap * width, kc * width), "row", 0, 0)
        owners = lax.all_to_all(touched[0], "row", 0, 0)
        return sum_parts(owners.reshape(-1), parts.reshape(slots, width, kc * width))

    return lax.cond(counts[0, IDS - 1] > BLOCKS, whole, lambda unused: assemble(pieces, width, kc), 0)


def solution(mesh):
    in_specs = (
        P(("slab", "row"), None, None),
        P(("slab", "row"), None, None),
        P(("slab", "row"), None),
        P(("slab", "row"), None),
        P(("slab", "row"), None, None),
        P(("slab", "row"), None, None, None),
        P(("slab", "row"), None, None),
    )
    out_specs = P(("slab", "row"), None, None)
    return jax.shard_map(per_device, mesh=mesh, in_specs=in_specs, out_specs=out_specs, check_vma=False)
```

```python
import functools

import jax
import jax.numpy as jnp
from jax import lax
from jax.experimental import pallas as pl
from jax.experimental.pallas import tpu as pltpu
from jax.sharding import PartitionSpec as P

NC = 4
UNROLL = 64
BLOCKS = 128
IDS = 256


def load_operands(a_hbm, p_hbm, halo_hbm, a_v, ext_v, sems):
    rows = p_hbm.shape[0]
    return (
        pltpu.make_async_copy(a_hbm, a_v, sems.at[0]),
        pltpu.make_async_copy(p_hbm, ext_v.at[pl.ds(0, rows)], sems.at[1]),
        pltpu.make_async_copy(halo_hbm, ext_v.at[pl.ds(rows, halo_hbm.shape[0])], sems.at[2]),
    )


def all_products(cols, a_v, ext_v, g_v, pt_v):
    rows, width, span = a_v.shape
    ka = span // width
    pairs = ext_v.shape[2] // (2 * width)
    pair = 2 * width

    def products(i, unused):
        row = a_v[i]
        turned = ext_v[i].T
        for m in range(2 * pairs):
            pt_v[i * 2 * pairs + m] = turned[m * width : (m + 1) * width, :]
        for k in range(ka):
            right = ext_v[cols[i * ka + k]]
            value = jnp.dot(row[:, k * width : (k + 1) * width], right, preferred_element_type=jnp.float32).astype(
                jnp.bfloat16
            )
            for h in range(pairs):
                g_v[(i * ka + k) * pairs + h] = value[:, h * pair : (h + 1) * pair]
        return unused

    lax.fori_loop(0, rows, products, 0, unroll=8)


def add_items(count, items, pt_v, g_v, acc, width, ka, kp):
    pair = 2 * width
    upper = (lax.broadcasted_iota(jnp.int32, (width, pair), 1) >= width).astype(jnp.int32)

    def batch(b, unused):
        found = []
        for u in range(UNROLL):
            word = items[b * UNROLL + u]
            target = word & 1023
            bit = lax.shift_right_logical(word, 10) & 31
            im = lax.shift_right_logical(word, 15)
            g = g_v[lax.shift_right_logical(im, kp.bit_length() - 1) * (ka * kp // 2) + lax.shift_right_logical(bit, 1)]
            g = jnp.where(upper == (bit & 1), g, jnp.zeros_like(g))
            z = jnp.dot(pt_v[im], g, preferred_element_type=jnp.float32)
            found.append((pl.ds(pl.multiple_of(target * width, width), width), z))
        for where, z in found:
            acc[where, :] = acc[where, :] + z
        return unused

    lax.fori_loop(0, lax.div(count + UNROLL - 1, UNROLL), batch, 0)


def clear_rows(acc, step, first, last):
    def clear(n, unused):
        acc[pl.ds(pl.multiple_of(n * step, step), step), :] = jnp.zeros((step, acc.shape[1]), jnp.float32)
        return unused

    lax.fori_loop(first, last, clear, 0)


def packed_kernel(
    cols, words, bases, a_hbm, p_hbm, halo_hbm, out_ref, ids_ref, a_v, ext_v, g_v, pt_v, acc, items, index, sems
):
    rows, width, span = a_v.shape
    ka = span // width
    kp = ext_v.shape[2] // width
    pair = 2 * width
    half = width // 2
    kc = index.shape[0] // bases.shape[0]
    copies = load_operands(a_hbm, p_hbm, halo_hbm, a_v, ext_v, sems)
    for copy in copies:
        copy.start()

    def unset(n, unused):
        for u in range(8):
            index[n * 8 + u] = -1
        return unused

    lax.fori_loop(0, index.shape[0] // 8, unset, 0)

    def no_id(n, unused):
        for u in range(8):
            ids_ref[0, n * 8 + u] = -1
        return unused

    lax.fori_loop(0, ids_ref.shape[1] // 8, no_id, 0)

    last = words.shape[0] - 1

    def more(state):
        return state[0] != last

    def take(state):
        at, count, blocks = state
        word = words[at]
        place = word & 511
        old = index[place]
        fresh = old < 0
        block = jnp.where(fresh, blocks, old)
        index[place] = block
        kept = jnp.minimum(block, BLOCKS)
        ids_ref[0, kept] = bases[lax.shift_right_logical(place, 3)] + (place & 7)
        items[count] = at * 1024 + kept
        return (lax.shift_right_logical(word, 9), count + 1, blocks + fresh.astype(jnp.int32))

    _, count, blocks = lax.while_loop(more, take, (lax.shift_right_logical(words[last], 9), 0, 0))
    for u in range(UNROLL):
        items[count + u] = BLOCKS
    ids_ref[0, IDS - 1] = blocks
    full = jnp.minimum(lax.div(blocks + 15, 16), BLOCKS // 16)
    clear_rows(acc, 16 * width, 0, full)
    clear_rows(acc, 16 * width, BLOCKS // 16, BLOCKS // 16 + 1)
    for copy in copies:
        copy.wait()
    all_products(cols, a_v, ext_v, g_v, pt_v)
    add_items(count, items, pt_v, g_v, acc, width, ka, kp)
    lower = lax.broadcasted_iota(jnp.int32, (16, pair), 1) < width

    def finish(n, unused):
        for r in range(half):
            one = acc[pl.ds(n * 16 * width + r, 16, stride=width), :]
            two = acc[pl.ds(n * 16 * width + half + r, 16, stride=width), :]
            one = one + pltpu.roll(one, width, 1)
            two = two + pltpu.roll(two, width, 1)
            out_ref[r, pl.ds(pl.multiple_of(n * 16, 16), 16), :] = jnp.where(lower, one, two).astype(jnp.bfloat16)
        return unused

    def empty(n, unused):
        for r in range(half):
            out_ref[r, pl.ds(pl.multiple_of(n * 16, 16), 16), :] = jnp.zeros((16, pair), jnp.bfloat16)
        return unused

    lax.fori_loop(0, full, finish, 0)
    lax.fori_loop(full, BLOCKS // 16, empty, 0)


def packed_partials(cols, words, bases, a_blocks, p_blocks, halo, kc):
    rows, width, span = a_blocks.shape
    kp = p_blocks.shape[2] // width
    ka = span // width
    extended = rows + halo.shape[0]
    smem = pl.BlockSpec(memory_space=pltpu.SMEM)
    vmem = pl.BlockSpec(memory_space=pltpu.VMEM)
    hbm = pl.BlockSpec(memory_space=pl.ANY)
    return pl.pallas_call(
        packed_kernel,
        out_shape=(
            jax.ShapeDtypeStruct((width // 2, BLOCKS, 2 * width), jnp.bfloat16),
            jax.ShapeDtypeStruct((1, IDS), jnp.int32),
        ),
        in_specs=[smem, smem, smem, hbm, hbm, hbm],
        out_specs=(vmem, smem),
        scratch_shapes=[
            pltpu.VMEM((rows, width, span), jnp.bfloat16),
            pltpu.VMEM((extended, width, kp * width), jnp.bfloat16),
            pltpu.VMEM((rows * ka * (kp // 2), width, 2 * width), jnp.bfloat16),
            pltpu.VMEM((rows * kp, width, width), jnp.bfloat16),
            pltpu.VMEM(((BLOCKS + 16) * width, 2 * width), jnp.float32),
            pltpu.SMEM((rows * kp * ka * kp + UNROLL,), jnp.int32),
            pltpu.SMEM((bases.shape[0] * kc,), jnp.int32),
            pltpu.SemaphoreType.DMA((3,)),
        ],
        compiler_params=pltpu.CompilerParams(vmem_limit_bytes=48 * 2**20),
        name="packed_partials",
    )(cols, words, bases, a_blocks, p_blocks, halo)


def halo_kernel(blocks, ids, out_blocks, out_ids, send_sem, take_sem):
    barrier = pltpu.get_barrier_semaphore()
    routes = []
    for axis, way, chosen in (("slab", 1, 1), ("slab", -1, 0), ("row", 1, 3), ("row", -1, 2)):
        n = lax.axis_size(axis)
        routes.append(({axis: lax.rem(lax.axis_index(axis) + way + n, n)}, chosen))
    for to, chosen in routes:
        pl.semaphore_signal(barrier, inc=1, device_id=to, device_id_type=pl.DeviceIdType.MESH)
    pl.semaphore_wait(barrier, len(routes))
    copies = []
    for x, (to, chosen) in enumerate(routes):
        for y, (src, dst) in enumerate(((ids, out_ids), (blocks, out_blocks))):
            copies.append(
                pltpu.make_async_remote_copy(
                    src_ref=src.at[chosen],
                    dst_ref=dst.at[x],
                    send_sem=send_sem.at[y, x],
                    recv_sem=take_sem.at[y, x],
                    device_id=to,
                    device_id_type=pl.DeviceIdType.MESH,
                )
            )
            copies[-1].start()
    for copy in copies:
        copy.wait()


def exchange_halo(blocks, ids):
    hbm = pl.BlockSpec(memory_space=pl.ANY)
    return pl.pallas_call(
        halo_kernel,
        out_shape=(jax.ShapeDtypeStruct(blocks.shape, blocks.dtype), jax.ShapeDtypeStruct(ids.shape, ids.dtype)),
        in_specs=[hbm, hbm],
        out_specs=(hbm, hbm),
        scratch_shapes=[pltpu.SemaphoreType.DMA((2, 4)), pltpu.SemaphoreType.DMA((2, 4))],
        compiler_params=pltpu.CompilerParams(collective_id=1, has_side_effects=True),
        name="exchange_halo",
    )(blocks, ids)


def reduce_kernel(
    parts, ids, pieces, most_ref, came_parts, came_ids, sums, flag, came_flags, acc, send_sem, take_sem, flag_send, flag_take
):
    row, slab = lax.axis_index("row"), lax.axis_index("slab")
    n, slabs = lax.axis_size("row"), lax.axis_size("slab")
    blocks = parts.shape[1]
    targets, lanes = acc.shape
    share = targets // n
    barrier = pltpu.get_barrier_semaphore()
    mesh_id = pl.DeviceIdType.MESH

    def greet_row(o, unused):
        pl.semaphore_signal(barrier, inc=1, device_id={"row": lax.rem(row + o, n)}, device_id_type=mesh_id)
        return unused

    def greet_slab(o, unused):
        pl.semaphore_signal(barrier, inc=1, device_id={"slab": lax.rem(slab + o, slabs)}, device_id_type=mesh_id)
        return unused

    lax.fori_loop(1, n, greet_row, 0)
    lax.fori_loop(1, slabs, greet_slab, 0)
    pl.semaphore_wait(barrier, n + slabs - 2)

    def row_copy(x, o, src, dst, other):
        return pltpu.make_async_remote_copy(
            src_ref=src,
            dst_ref=dst,
            send_sem=send_sem.at[x, o],
            recv_sem=take_sem.at[x, o],
            device_id={"row": other},
            device_id_type=mesh_id,
        )

    def to_of(o):
        return lax.rem(row + o, n)

    def from_of(o):
        return lax.rem(row + n - o, n)

    def begin(o, unused):
        to = to_of(o)
        row_copy(0, o, ids.at[0], came_ids.at[row], to).start()
        row_copy(1, o, parts.at[to], came_parts.at[row], to).start()
        return unused

    lax.fori_loop(1, n, begin, 0)
    order = lax.broadcasted_iota(jnp.int32, (targets, blocks), 0)

    def spread(names, values):
        hot = jnp.where(order == names[:, :blocks], 1.0, 0.0).astype(jnp.bfloat16)
        return jnp.dot(hot, values, preferred_element_type=jnp.float32)

    own = ids[0]
    acc[...] = spread(own, parts[row])
    last = lax.broadcasted_iota(jnp.int32, own.shape, 1) == own.shape[1] - 1

    def add(o, most):
        came = from_of(o)
        row_copy(0, o, ids.at[0], came_ids.at[came], came).wait_recv()
        row_copy(1, o, parts.at[came], came_parts.at[came], came).wait_recv()
        names = came_ids[came]
        acc[...] += spread(names, came_parts[came])
        return jnp.maximum(most, names)

    most = lax.fori_loop(1, n, add, own)
    flag[...] = jnp.where(last, most, 0)

    def flag_copy(o, at, other):
        return pltpu.make_async_remote_copy(
            src_ref=flag,
            dst_ref=came_flags.at[at],
            send_sem=flag_send.at[o],
            recv_sem=flag_take.at[o],
            device_id={"slab": other},
            device_id_type=mesh_id,
        )

    def begin_flag(o, unused):
        flag_copy(o, slab, lax.rem(slab + o, slabs)).start()
        return unused

    lax.fori_loop(1, slabs, begin_flag, 0)
    for p in range(n):
        sums[p] = acc[p * share : (p + 1) * share, :].astype(jnp.bfloat16)

    def begin_sums(o, unused):
        to = to_of(o)
        row_copy(2, o, sums.at[to], pieces.at[row], to).start()
        return unused

    lax.fori_loop(1, n, begin_sums, 0)
    pieces[row] = sums[row]

    def end_flag(o, most):
        came = lax.rem(slab + slabs - o, slabs)
        flag_copy(o, slab, lax.rem(slab + o, slabs)).wait_send()
        flag_copy(o, came, came).wait_recv()
        return jnp.maximum(most, came_flags[came])

    most_ref[...] = lax.fori_loop(1, slabs, end_flag, flag[...])

    def end(o, unused):
        to, came = to_of(o), from_of(o)
        row_copy(0, o, ids.at[0], came_ids.at[row], to).wait_send()
        row_copy(1, o, parts.at[to], came_parts.at[row], to).wait_send()
        row_copy(2, o, sums.at[to], pieces.at[row], to).wait_send()
        row_copy(2, o, sums.at[came], pieces.at[came], came).wait_recv()
        return unused

    lax.fori_loop(1, n, end, 0)


def reduce_parts(parts, ids, share):
    n, slabs = lax.axis_size("row"), lax.axis_size("slab")
    _, blocks, lanes = parts.shape
    vmem = pl.BlockSpec(memory_space=pltpu.VMEM)
    return pl.pallas_call(
        reduce_kernel,
        out_shape=(
            jax.ShapeDtypeStruct((n, share, lanes), jnp.bfloat16),
            jax.ShapeDtypeStruct((1, IDS), jnp.int32),
        ),
        in_specs=[vmem, vmem],
        out_specs=(vmem, vmem),
        scratch_shapes=[
            pltpu.VMEM((n, blocks, lanes), jnp.bfloat16),
            pltpu.VMEM((n, 1, IDS), jnp.int32),
            pltpu.VMEM((n, share, lanes), jnp.bfloat16),
            pltpu.VMEM((1, IDS), jnp.int32),
            pltpu.VMEM((slabs, 1, IDS), jnp.int32),
            pltpu.VMEM((n * share, lanes), jnp.float32),
            pltpu.SemaphoreType.DMA((3, n)),
            pltpu.SemaphoreType.DMA((3, n)),
            pltpu.SemaphoreType.DMA((slabs,)),
            pltpu.SemaphoreType.DMA((slabs,)),
        ],
        compiler_params=pltpu.CompilerParams(
            collective_id=0, has_side_effects=True, vmem_limit_bytes=32 * 2**20
        ),
        name="reduce_parts",
    )(parts, ids)


def assemble_kernel(pieces_ref, out_ref, wide):
    n, targets, pair = pieces_ref.shape
    owned, width, outspan = out_ref.shape
    half = width // 2
    kc = targets // owned
    lower = lax.broadcasted_iota(jnp.int32, (half, pair), 1) < half * 2
    wide[...] = pieces_ref[...].reshape(n * targets, pair).astype(jnp.float32)
    for g in range(owned):
        for h in range(kc // 2):
            one = wide[pl.ds(g * kc + 2 * h, n, stride=targets), :]
            two = wide[pl.ds(g * kc + 2 * h + 1, n, stride=targets), :]
            span = slice(h * pair, (h + 1) * pair)
            out_ref[g, :half, span] = jnp.where(lower, one, pltpu.roll(two, width, 1))
            out_ref[g, half:, span] = jnp.where(lower, pltpu.roll(one, width, 1), two)


def assemble(pieces, width, kc):
    vmem = pl.BlockSpec(memory_space=pltpu.VMEM)
    n, targets, pair = pieces.shape
    return pl.pallas_call(
        assemble_kernel,
        out_shape=jax.ShapeDtypeStruct((NC, width, kc * width), jnp.float32),
        in_specs=[vmem],
        out_specs=vmem,
        scratch_shapes=[pltpu.VMEM((n * targets, pair), jnp.float32)],
        name="assemble",
    )(pieces)


def coarse_kernel(cols, words, a_hbm, p_hbm, halo_hbm, out_ref, a_v, ext_v, g_v, pt_v, acc, items, sems):
    rows, width, span = a_v.shape
    ka = span // width
    kp = ext_v.shape[2] // width
    nslots, _, outspan = out_ref.shape
    kc = outspan // width
    pair = 2 * width
    copies = load_operands(a_hbm, p_hbm, halo_hbm, a_v, ext_v, sems)
    for copy in copies:
        copy.start()
    clear_rows(acc, width, 0, acc.shape[0] // width)

    last = words.shape[0] - 1

    def more(state):
        return state[0] != last

    def take(state):
        at, count = state
        word = words[at]
        items[count] = at * 1024 + (word & 511)
        return (lax.shift_right_logical(word, 9), count + 1)

    _, count = lax.while_loop(more, take, (lax.shift_right_logical(words[last], 9), 0))
    for u in range(UNROLL):
        items[count + u] = nslots * kc
    for copy in copies:
        copy.wait()
    all_products(cols, a_v, ext_v, g_v, pt_v)
    add_items(count, items, pt_v, g_v, acc, width, ka, kp)
    lower = lax.broadcasted_iota(jnp.int32, (width, pair), 1) < width

    def finish(t, unused):
        for h in range(kc // 2):
            one = acc[pl.ds(pl.multiple_of((t * kc + 2 * h) * width, width), width), :]
            two = acc[pl.ds(pl.multiple_of((t * kc + 2 * h + 1) * width, width), width), :]
            one = one + pltpu.roll(one, width, 1)
            two = two + pltpu.roll(two, width, 1)
            out_ref[t, :, h * pair : (h + 1) * pair] = jnp.where(lower, one, two).astype(jnp.bfloat16)
        return unused

    lax.fori_loop(0, nslots, finish, 0)


def coarse_partials(cols, words, a_blocks, p_blocks, halo, nslots, kc):
    rows, width, span = a_blocks.shape
    kp = p_blocks.shape[2] // width
    ka = span // width
    extended = rows + halo.shape[0]
    smem = pl.BlockSpec(memory_space=pltpu.SMEM)
    hbm = pl.BlockSpec(memory_space=pl.ANY)
    return pl.pallas_call(
        coarse_kernel,
        out_shape=jax.ShapeDtypeStruct((nslots, width, kc * width), jnp.bfloat16),
        in_specs=[smem, smem, hbm, hbm, hbm],
        out_specs=pl.BlockSpec(memory_space=pltpu.VMEM),
        scratch_shapes=[
            pltpu.VMEM((rows, width, span), jnp.bfloat16),
            pltpu.VMEM((extended, width, kp * width), jnp.bfloat16),
            pltpu.VMEM((rows * ka * (kp // 2), width, 2 * width), jnp.bfloat16),
            pltpu.VMEM((rows * kp, width, width), jnp.bfloat16),
            pltpu.VMEM(((nslots * kc + 1) * width, 2 * width), jnp.float32),
            pltpu.SMEM((rows * kp * ka * kp + UNROLL,), jnp.int32),
            pltpu.SemaphoreType.DMA((3,)),
        ],
        compiler_params=pltpu.CompilerParams(vmem_limit_bytes=56 * 2**20),
        name="coarse_partials",
    )(cols, words, a_blocks, p_blocks, halo)


def sum_kernel(ids, parts, out_ref):
    out_ref[...] = jnp.zeros_like(out_ref)

    def one(n, unused):
        row = ids[n]

        @pl.when(row >= 0)
        def _():
            out_ref[row] = out_ref[row] + parts[n].astype(jnp.float32)

        return unused

    lax.fori_loop(0, parts.shape[0], one, 0)


def sum_parts(ids, parts):
    return pl.pallas_call(
        sum_kernel,
        out_shape=jax.ShapeDtypeStruct((NC,) + parts.shape[1:], jnp.float32),
        in_specs=[pl.BlockSpec(memory_space=pltpu.SMEM), pl.BlockSpec(memory_space=pltpu.VMEM)],
        out_specs=pl.BlockSpec(memory_space=pltpu.VMEM),
        compiler_params=pltpu.CompilerParams(vmem_limit_bytes=32 * 2**20),
        name="sum_parts",
    )(ids, parts)


def lookup(table, index):
    hot = index[..., None] == jnp.arange(table.shape[0], dtype=jnp.int32)
    return jnp.sum(jnp.where(hot, table, 0), axis=-1)


def find_matches(ext_ids, a_cols, p_slots, patterns):
    rows = a_cols.shape[0]
    kp = p_slots.shape[1]
    reached = jnp.stack([lookup(ext_ids[:, q], a_cols) for q in range(kp)], -1).reshape(rows, -1)
    wanted = jnp.stack([lookup(patterns[:, j], p_slots) for j in range(patterns.shape[1])], 0)
    order = jnp.arange(1, patterns.shape[1] + 1, dtype=jnp.int32)[:, None, None, None]
    places = jnp.sum(jnp.where(reached[None, :, None, :] == wanted[..., None], order, 0), 0)
    kq = reached.shape[1]
    heads = jnp.arange(rows * kp, dtype=jnp.int32)
    bits = jnp.arange(kq, dtype=jnp.int32)
    end = rows * kp * 32 - 1
    at = jnp.where(places > 0, heads.reshape(rows, kp, 1) * 32 + bits, end)
    first = jnp.min(at, -1)
    flat = first.reshape(-1)
    beyond = jnp.min(jnp.where(heads[None, :] > heads[:, None], flat[None, :], end), -1)
    follow = jnp.min(jnp.where(bits[None, :] > bits[:, None], at[:, :, None, :], end), -1)
    follow = jnp.minimum(follow, beyond.reshape(rows, kp, 1))
    words = follow * 512 + p_slots[..., None] * patterns.shape[1] + places - 1
    words = jnp.pad(words, ((0, 0), (0, 0), (0, 32 - kq))).reshape(-1)
    return jnp.where(jnp.arange(end + 1, dtype=jnp.int32) == end, jnp.min(flat) * 512, words)


def per_device(a_blocks, p_blocks, a_cols, p_slots, touched, touch_cols, halo_rows):
    nrow = lax.axis_size("row")
    nslab = lax.axis_size("slab")
    slab_at = lax.axis_index("slab")
    cap = touched.shape[2]
    slots = touched.shape[1] * cap
    table = touched.reshape(slots)
    patterns = touch_cols.reshape(slots, touch_cols.shape[3])
    kc = patterns.shape[1]
    coarse_ids = (slab_at * nrow + p_slots // cap) * NC + lookup(table, p_slots)
    lists = halo_rows[0]
    sent_blocks = p_blocks[lists]
    sent_ids = coarse_ids[lists]
    depth = lists.shape[1]
    kp = p_slots.shape[1]
    row_at = lax.axis_index("row")
    ids_out = jnp.pad(sent_ids.reshape(4, 1, depth * kp), ((0, 0), (0, 0), (0, 128 - depth * kp)))
    halo, halo_ids = exchange_halo(sent_blocks, ids_out)
    outside = jnp.stack([slab_at == 0, slab_at == nslab - 1, row_at == 0, row_at == nrow - 1])
    halo_ids = jnp.where(outside[:, None], -1, halo_ids[:, 0, : depth * kp]).reshape(4 * depth, kp)
    halo = halo.reshape((4 * depth,) + halo.shape[2:])
    ext_ids = jnp.concatenate([coarse_ids, halo_ids], 0)
    words = find_matches(ext_ids, a_cols, p_slots, patterns)
    width = a_blocks.shape[1]
    lists_in = (a_cols.reshape(-1), words)
    bases = (jnp.arange(slots, dtype=jnp.int32) // cap * NC + table) * kc
    packed, ids = packed_partials(*lists_in, bases, a_blocks, p_blocks, halo, kc)
    pieces, counts = reduce_parts(packed, ids.reshape(1, 1, IDS), NC * kc)

    def whole(unused):
        partial = coarse_partials(*lists_in, a_blocks, p_blocks, halo, slots, kc)
        parts = lax.all_to_all(partial.reshape(nrow, cap * width, kc * width), "row", 0, 0)
        owners = lax.all_to_all(touched[0], "row", 0, 0)
        return sum_parts(owners.reshape(-1), parts.reshape(slots, width, kc * width))

    return lax.cond(counts[0, IDS - 1] > BLOCKS, whole, lambda unused: assemble(pieces, width, kc), 0)


def solution(mesh):
    in_specs = (
        P(("slab", "row"), None, None),
        P(("slab", "row"), None, None),
        P(("slab", "row"), None),
        P(("slab", "row"), None),
        P(("slab", "row"), None, None),
        P(("slab", "row"), None, None, None),
        P(("slab", "row"), None, None),
    )
    out_specs = P(("slab", "row"), None, None)
    return jax.shard_map(per_device, mesh=mesh, in_specs=in_specs, out_specs=out_specs, check_vma=False)
```

```python
import functools

import jax
import jax.numpy as jnp
from jax import lax
from jax.experimental import pallas as pl
from jax.experimental.pallas import tpu as pltpu
from jax.sharding import PartitionSpec as P

NC = 4
UNROLL = 64
BLOCKS = 128
IDS = 256


def load_operands(a_hbm, p_hbm, halo_hbm, a_v, ext_v, sems):
    rows = p_hbm.shape[0]
    return (
        pltpu.make_async_copy(a_hbm, a_v, sems.at[0]),
        pltpu.make_async_copy(p_hbm, ext_v.at[pl.ds(0, rows)], sems.at[1]),
        pltpu.make_async_copy(halo_hbm, ext_v.at[pl.ds(rows, halo_hbm.shape[0])], sems.at[2]),
    )


def all_products(cols, a_v, ext_v, g_v, pt_v):
    rows, width, span = a_v.shape
    ka = span // width
    pairs = ext_v.shape[2] // (2 * width)
    pair = 2 * width

    def products(i, unused):
        row = a_v[i]
        turned = ext_v[i].T
        for m in range(2 * pairs):
            pt_v[i * 2 * pairs + m] = turned[m * width : (m + 1) * width, :]
        for k in range(ka):
            right = ext_v[cols[i * ka + k]]
            value = jnp.dot(row[:, k * width : (k + 1) * width], right, preferred_element_type=jnp.float32).astype(
                jnp.bfloat16
            )
            for h in range(pairs):
                g_v[(i * ka + k) * pairs + h] = value[:, h * pair : (h + 1) * pair]
        return unused

    lax.fori_loop(0, rows, products, 0, unroll=8)


def add_items(count, items, pt_v, g_v, acc, width, ka, kp):
    pair = 2 * width
    upper = (lax.broadcasted_iota(jnp.int32, (width, pair), 1) >= width).astype(jnp.int32)

    def batch(b, unused):
        found = []
        for u in range(UNROLL):
            word = items[b * UNROLL + u]
            target = word & 1023
            bit = lax.shift_right_logical(word, 10) & 31
            im = lax.shift_right_logical(word, 15)
            g = g_v[lax.shift_right_logical(im, kp.bit_length() - 1) * (ka * kp // 2) + lax.shift_right_logical(bit, 1)]
            g = jnp.where(upper == (bit & 1), g, jnp.zeros_like(g))
            z = jnp.dot(pt_v[im], g, preferred_element_type=jnp.float32)
            found.append((pl.ds(pl.multiple_of(target * width, width), width), z))
        for where, z in found:
            acc[where, :] = acc[where, :] + z
        return unused

    lax.fori_loop(0, lax.div(count + UNROLL - 1, UNROLL), batch, 0)


def clear_rows(acc, step, first, last):
    def clear(n, unused):
        acc[pl.ds(pl.multiple_of(n * step, step), step), :] = jnp.zeros((step, acc.shape[1]), jnp.float32)
        return unused

    lax.fori_loop(first, last, clear, 0)


def packed_kernel(
    cols, words, bases, a_hbm, p_hbm, halo_hbm, out_ref, ids_ref, a_v, ext_v, g_v, pt_v, acc, items, index, sems
):
    rows, width, span = a_v.shape
    ka = span // width
    kp = ext_v.shape[2] // width
    pair = 2 * width
    half = width // 2
    kc = index.shape[0] // bases.shape[0]
    copies = load_operands(a_hbm, p_hbm, halo_hbm, a_v, ext_v, sems)
    for copy in copies:
        copy.start()

    def unset(n, unused):
        for u in range(8):
            index[n * 8 + u] = -1
        return unused

    lax.fori_loop(0, index.shape[0] // 8, unset, 0)

    def no_id(n, unused):
        for u in range(8):
            ids_ref[0, n * 8 + u] = -1
        return unused

    lax.fori_loop(0, ids_ref.shape[1] // 8, no_id, 0)

    last = words.shape[0] - 1

    def more(state):
        return state[0] != last

    def take(state):
        at, count, blocks = state
        word = words[at]
        place = word & 511
        old = index[place]
        fresh = old < 0
        block = jnp.where(fresh, blocks, old)
        index[place] = block
        kept = jnp.minimum(block, BLOCKS)
        ids_ref[0, kept] = bases[lax.shift_right_logical(place, 3)] + (place & 7)
        items[count] = at * 1024 + kept
        return (lax.shift_right_logical(word, 9), count + 1, blocks + fresh.astype(jnp.int32))

    _, count, blocks = lax.while_loop(more, take, (lax.shift_right_logical(words[last], 9), 0, 0))
    for u in range(UNROLL):
        items[count + u] = BLOCKS
    ids_ref[0, IDS - 1] = blocks
    full = jnp.minimum(lax.div(blocks + 15, 16), BLOCKS // 16)
    clear_rows(acc, 16 * width, 0, full)
    clear_rows(acc, 16 * width, BLOCKS // 16, BLOCKS // 16 + 1)
    for copy in copies:
        copy.wait()
    all_products(cols, a_v, ext_v, g_v, pt_v)
    add_items(count, items, pt_v, g_v, acc, width, ka, kp)
    lower = lax.broadcasted_iota(jnp.int32, (16, pair), 1) < width

    def finish(n, unused):
        for r in range(half):
            one = acc[pl.ds(n * 16 * width + r, 16, stride=width), :]
            two = acc[pl.ds(n * 16 * width + half + r, 16, stride=width), :]
            one = one + pltpu.roll(one, width, 1)
            two = two + pltpu.roll(two, width, 1)
            out_ref[r, pl.ds(pl.multiple_of(n * 16, 16), 16), :] = jnp.where(lower, one, two).astype(jnp.bfloat16)
        return unused

    def empty(n, unused):
        for r in range(half):
            out_ref[r, pl.ds(pl.multiple_of(n * 16, 16), 16), :] = jnp.zeros((16, pair), jnp.bfloat16)
        return unused

    lax.fori_loop(0, full, finish, 0)
    lax.fori_loop(full, BLOCKS // 16, empty, 0)


def packed_partials(cols, words, bases, a_blocks, p_blocks, halo, kc):
    rows, width, span = a_blocks.shape
    kp = p_blocks.shape[2] // width
    ka = span // width
    extended = rows + halo.shape[0]
    smem = pl.BlockSpec(memory_space=pltpu.SMEM)
    vmem = pl.BlockSpec(memory_space=pltpu.VMEM)
    hbm = pl.BlockSpec(memory_space=pl.ANY)
    return pl.pallas_call(
        packed_kernel,
        out_shape=(
            jax.ShapeDtypeStruct((width // 2, BLOCKS, 2 * width), jnp.bfloat16),
            jax.ShapeDtypeStruct((1, IDS), jnp.int32),
        ),
        in_specs=[smem, smem, smem, hbm, hbm, hbm],
        out_specs=(vmem, smem),
        scratch_shapes=[
            pltpu.VMEM((rows, width, span), jnp.bfloat16),
            pltpu.VMEM((extended, width, kp * width), jnp.bfloat16),
            pltpu.VMEM((rows * ka * (kp // 2), width, 2 * width), jnp.bfloat16),
            pltpu.VMEM((rows * kp, width, width), jnp.bfloat16),
            pltpu.VMEM(((BLOCKS + 16) * width, 2 * width), jnp.float32),
            pltpu.SMEM((rows * kp * ka * kp + UNROLL,), jnp.int32),
            pltpu.SMEM((bases.shape[0] * kc,), jnp.int32),
            pltpu.SemaphoreType.DMA((3,)),
        ],
        compiler_params=pltpu.CompilerParams(vmem_limit_bytes=48 * 2**20),
        name="packed_partials",
    )(cols, words, bases, a_blocks, p_blocks, halo)


def halo_kernel(rows, p_ref, ids, out_blocks, out_ids, blocks, send_sem, take_sem):
    barrier = pltpu.get_barrier_semaphore()
    routes = []
    for x, axis, way, chosen in ((2, "row", 1, 3), (3, "row", -1, 2), (0, "slab", 1, 1), (1, "slab", -1, 0)):
        n = lax.axis_size(axis)
        routes.append((x, {axis: lax.rem(lax.axis_index(axis) + way + n, n)}, chosen))
    for _, to, _ in routes:
        pl.semaphore_signal(barrier, inc=1, device_id=to, device_id_type=pl.DeviceIdType.MESH)
    depth = blocks.shape[1]
    for y, x in enumerate((3, 2, 1, 0)):
        for h in range(depth):
            blocks[x, h] = p_ref[rows[0, x, h]]
        if y == 0:
            pl.semaphore_wait(barrier, len(routes))
        slot, to, chosen = routes[y]
        for z, (src, dst) in enumerate(((ids, out_ids), (blocks, out_blocks))):
            pltpu.make_async_remote_copy(
                src_ref=src.at[chosen],
                dst_ref=dst.at[slot],
                send_sem=send_sem.at[z, slot],
                recv_sem=take_sem.at[z, slot],
                device_id=to,
                device_id_type=pl.DeviceIdType.MESH,
            ).start()
    for slot, to, chosen in routes:
        for z, (src, dst) in enumerate(((ids, out_ids), (blocks, out_blocks))):
            pltpu.make_async_remote_copy(
                src_ref=src.at[chosen],
                dst_ref=dst.at[slot],
                send_sem=send_sem.at[z, slot],
                recv_sem=take_sem.at[z, slot],
                device_id=to,
                device_id_type=pl.DeviceIdType.MESH,
            ).wait()


def exchange_halo(rows, p_blocks, ids):
    vmem = pl.BlockSpec(memory_space=pltpu.VMEM)
    hbm = pl.BlockSpec(memory_space=pl.ANY)
    shape = rows.shape[1:] + p_blocks.shape[1:]
    return pl.pallas_call(
        halo_kernel,
        out_shape=(jax.ShapeDtypeStruct(shape, p_blocks.dtype), jax.ShapeDtypeStruct(ids.shape, ids.dtype)),
        in_specs=[pl.BlockSpec(memory_space=pltpu.SMEM), vmem, hbm],
        out_specs=(hbm, hbm),
        scratch_shapes=[
            pltpu.VMEM(shape, p_blocks.dtype),
            pltpu.SemaphoreType.DMA((2, 4)),
            pltpu.SemaphoreType.DMA((2, 4)),
        ],
        compiler_params=pltpu.CompilerParams(collective_id=1, has_side_effects=True, vmem_limit_bytes=32 * 2**20),
        name="exchange_halo",
    )(rows, p_blocks, ids)


def reduce_kernel(
    parts, ids, pieces, most_ref, came_parts, came_ids, sums, flag, came_flags, acc, send_sem, take_sem, flag_send, flag_take
):
    row, slab = lax.axis_index("row"), lax.axis_index("slab")
    n, slabs = lax.axis_size("row"), lax.axis_size("slab")
    blocks = parts.shape[1]
    targets, lanes = acc.shape
    share = targets // n
    barrier = pltpu.get_barrier_semaphore()
    mesh_id = pl.DeviceIdType.MESH

    def greet_row(o, unused):
        pl.semaphore_signal(barrier, inc=1, device_id={"row": lax.rem(row + o, n)}, device_id_type=mesh_id)
        return unused

    def greet_slab(o, unused):
        pl.semaphore_signal(barrier, inc=1, device_id={"slab": lax.rem(slab + o, slabs)}, device_id_type=mesh_id)
        return unused

    lax.fori_loop(1, n, greet_row, 0)
    lax.fori_loop(1, slabs, greet_slab, 0)
    pl.semaphore_wait(barrier, n + slabs - 2)

    def row_copy(x, o, src, dst, other):
        return pltpu.make_async_remote_copy(
            src_ref=src,
            dst_ref=dst,
            send_sem=send_sem.at[x, o],
            recv_sem=take_sem.at[x, o],
            device_id={"row": other},
            device_id_type=mesh_id,
        )

    def to_of(o):
        return lax.rem(row + o, n)

    def from_of(o):
        return lax.rem(row + n - o, n)

    def begin(o, unused):
        to = to_of(o)
        row_copy(0, o, ids.at[0], came_ids.at[row], to).start()
        row_copy(1, o, parts.at[to], came_parts.at[row], to).start()
        return unused

    lax.fori_loop(1, n, begin, 0)
    order = lax.broadcasted_iota(jnp.int32, (targets, blocks), 0)

    def spread(names, values):
        hot = jnp.where(order == names[:, :blocks], 1.0, 0.0).astype(jnp.bfloat16)
        return jnp.dot(hot, values, preferred_element_type=jnp.float32)

    own = ids[0]
    acc[...] = spread(own, parts[row])
    last = lax.broadcasted_iota(jnp.int32, own.shape, 1) == own.shape[1] - 1

    def add(o, most):
        came = from_of(o)
        row_copy(0, o, ids.at[0], came_ids.at[came], came).wait_recv()
        row_copy(1, o, parts.at[came], came_parts.at[came], came).wait_recv()
        names = came_ids[came]
        acc[...] += spread(names, came_parts[came])
        return jnp.maximum(most, names)

    most = lax.fori_loop(1, n, add, own)
    flag[...] = jnp.where(last, most, 0)

    def flag_copy(o, at, other):
        return pltpu.make_async_remote_copy(
            src_ref=flag,
            dst_ref=came_flags.at[at],
            send_sem=flag_send.at[o],
            recv_sem=flag_take.at[o],
            device_id={"slab": other},
            device_id_type=mesh_id,
        )

    def begin_flag(o, unused):
        flag_copy(o, slab, lax.rem(slab + o, slabs)).start()
        return unused

    lax.fori_loop(1, slabs, begin_flag, 0)
    for p in range(n):
        sums[p] = acc[p * share : (p + 1) * share, :].astype(jnp.bfloat16)

    def begin_sums(o, unused):
        to = to_of(o)
        row_copy(2, o, sums.at[to], pieces.at[row], to).start()
        return unused

    lax.fori_loop(1, n, begin_sums, 0)
    pieces[row] = sums[row]

    def end_flag(o, most):
        came = lax.rem(slab + slabs - o, slabs)
        flag_copy(o, slab, lax.rem(slab + o, slabs)).wait_send()
        flag_copy(o, came, came).wait_recv()
        return jnp.maximum(most, came_flags[came])

    most_ref[0, 0] = jnp.max(lax.fori_loop(1, slabs, end_flag, flag[...]))

    def end(o, unused):
        to, came = to_of(o), from_of(o)
        row_copy(0, o, ids.at[0], came_ids.at[row], to).wait_send()
        row_copy(1, o, parts.at[to], came_parts.at[row], to).wait_send()
        row_copy(2, o, sums.at[to], pieces.at[row], to).wait_send()
        row_copy(2, o, sums.at[came], pieces.at[came], came).wait_recv()
        return unused

    lax.fori_loop(1, n, end, 0)


def reduce_parts(parts, ids, share):
    n, slabs = lax.axis_size("row"), lax.axis_size("slab")
    _, blocks, lanes = parts.shape
    vmem = pl.BlockSpec(memory_space=pltpu.VMEM)
    return pl.pallas_call(
        reduce_kernel,
        out_shape=(
            jax.ShapeDtypeStruct((n, share, lanes), jnp.bfloat16),
            jax.ShapeDtypeStruct((1, 1), jnp.int32),
        ),
        in_specs=[vmem, vmem],
        out_specs=(vmem, pl.BlockSpec(memory_space=pltpu.SMEM)),
        scratch_shapes=[
            pltpu.VMEM((n, blocks, lanes), jnp.bfloat16),
            pltpu.VMEM((n, 1, IDS), jnp.int32),
            pltpu.VMEM((n, share, lanes), jnp.bfloat16),
            pltpu.VMEM((1, IDS), jnp.int32),
            pltpu.VMEM((slabs, 1, IDS), jnp.int32),
            pltpu.VMEM((n * share, lanes), jnp.float32),
            pltpu.SemaphoreType.DMA((3, n)),
            pltpu.SemaphoreType.DMA((3, n)),
            pltpu.SemaphoreType.DMA((slabs,)),
            pltpu.SemaphoreType.DMA((slabs,)),
        ],
        compiler_params=pltpu.CompilerParams(
            collective_id=0, has_side_effects=True, vmem_limit_bytes=32 * 2**20
        ),
        name="reduce_parts",
    )(parts, ids)


def assemble_kernel(pieces_ref, out_ref, wide):
    n, targets, pair = pieces_ref.shape
    owned, width, outspan = out_ref.shape
    half = width // 2
    kc = targets // owned
    lower = lax.broadcasted_iota(jnp.int32, (half, pair), 1) < half * 2
    wide[...] = pieces_ref[...].reshape(n * targets, pair).astype(jnp.float32)
    for g in range(owned):
        for h in range(kc // 2):
            one = wide[pl.ds(g * kc + 2 * h, n, stride=targets), :]
            two = wide[pl.ds(g * kc + 2 * h + 1, n, stride=targets), :]
            span = slice(h * pair, (h + 1) * pair)
            out_ref[g, :half, span] = jnp.where(lower, one, pltpu.roll(two, width, 1))
            out_ref[g, half:, span] = jnp.where(lower, pltpu.roll(one, width, 1), two)


def assemble(pieces, width, kc):
    vmem = pl.BlockSpec(memory_space=pltpu.VMEM)
    n, targets, pair = pieces.shape
    return pl.pallas_call(
        assemble_kernel,
        out_shape=jax.ShapeDtypeStruct((NC, width, kc * width), jnp.float32),
        in_specs=[vmem],
        out_specs=vmem,
        scratch_shapes=[pltpu.VMEM((n * targets, pair), jnp.float32)],
        name="assemble",
    )(pieces)


def coarse_kernel(cols, words, a_hbm, p_hbm, halo_hbm, out_ref, a_v, ext_v, g_v, pt_v, acc, items, sems):
    rows, width, span = a_v.shape
    ka = span // width
    kp = ext_v.shape[2] // width
    nslots, _, outspan = out_ref.shape
    kc = outspan // width
    pair = 2 * width
    copies = load_operands(a_hbm, p_hbm, halo_hbm, a_v, ext_v, sems)
    for copy in copies:
        copy.start()
    clear_rows(acc, width, 0, acc.shape[0] // width)

    last = words.shape[0] - 1

    def more(state):
        return state[0] != last

    def take(state):
        at, count = state
        word = words[at]
        items[count] = at * 1024 + (word & 511)
        return (lax.shift_right_logical(word, 9), count + 1)

    _, count = lax.while_loop(more, take, (lax.shift_right_logical(words[last], 9), 0))
    for u in range(UNROLL):
        items[count + u] = nslots * kc
    for copy in copies:
        copy.wait()
    all_products(cols, a_v, ext_v, g_v, pt_v)
    add_items(count, items, pt_v, g_v, acc, width, ka, kp)
    lower = lax.broadcasted_iota(jnp.int32, (width, pair), 1) < width

    def finish(t, unused):
        for h in range(kc // 2):
            one = acc[pl.ds(pl.multiple_of((t * kc + 2 * h) * width, width), width), :]
            two = acc[pl.ds(pl.multiple_of((t * kc + 2 * h + 1) * width, width), width), :]
            one = one + pltpu.roll(one, width, 1)
            two = two + pltpu.roll(two, width, 1)
            out_ref[t, :, h * pair : (h + 1) * pair] = jnp.where(lower, one, two).astype(jnp.bfloat16)
        return unused

    lax.fori_loop(0, nslots, finish, 0)


def coarse_partials(cols, words, a_blocks, p_blocks, halo, nslots, kc):
    rows, width, span = a_blocks.shape
    kp = p_blocks.shape[2] // width
    ka = span // width
    extended = rows + halo.shape[0]
    smem = pl.BlockSpec(memory_space=pltpu.SMEM)
    hbm = pl.BlockSpec(memory_space=pl.ANY)
    return pl.pallas_call(
        coarse_kernel,
        out_shape=jax.ShapeDtypeStruct((nslots, width, kc * width), jnp.bfloat16),
        in_specs=[smem, smem, hbm, hbm, hbm],
        out_specs=pl.BlockSpec(memory_space=pltpu.VMEM),
        scratch_shapes=[
            pltpu.VMEM((rows, width, span), jnp.bfloat16),
            pltpu.VMEM((extended, width, kp * width), jnp.bfloat16),
            pltpu.VMEM((rows * ka * (kp // 2), width, 2 * width), jnp.bfloat16),
            pltpu.VMEM((rows * kp, width, width), jnp.bfloat16),
            pltpu.VMEM(((nslots * kc + 1) * width, 2 * width), jnp.float32),
            pltpu.SMEM((rows * kp * ka * kp + UNROLL,), jnp.int32),
            pltpu.SemaphoreType.DMA((3,)),
        ],
        compiler_params=pltpu.CompilerParams(vmem_limit_bytes=56 * 2**20),
        name="coarse_partials",
    )(cols, words, a_blocks, p_blocks, halo)


def sum_kernel(ids, parts, out_ref):
    out_ref[...] = jnp.zeros_like(out_ref)

    def one(n, unused):
        row = ids[n]

        @pl.when(row >= 0)
        def _():
            out_ref[row] = out_ref[row] + parts[n].astype(jnp.float32)

        return unused

    lax.fori_loop(0, parts.shape[0], one, 0)


def sum_parts(ids, parts):
    return pl.pallas_call(
        sum_kernel,
        out_shape=jax.ShapeDtypeStruct((NC,) + parts.shape[1:], jnp.float32),
        in_specs=[pl.BlockSpec(memory_space=pltpu.SMEM), pl.BlockSpec(memory_space=pltpu.VMEM)],
        out_specs=pl.BlockSpec(memory_space=pltpu.VMEM),
        compiler_params=pltpu.CompilerParams(vmem_limit_bytes=32 * 2**20),
        name="sum_parts",
    )(ids, parts)


def lookup(table, index):
    hot = index[..., None] == jnp.arange(table.shape[0], dtype=jnp.int32)
    return jnp.sum(jnp.where(hot, table, 0), axis=-1)


def find_matches(ext_ids, a_cols, p_slots, patterns):
    rows = a_cols.shape[0]
    kp = p_slots.shape[1]
    reached = jnp.stack([lookup(ext_ids[:, q], a_cols) for q in range(kp)], -1).reshape(rows, -1)
    wanted = jnp.stack([lookup(patterns[:, j], p_slots) for j in range(patterns.shape[1])], 0)
    order = jnp.arange(1, patterns.shape[1] + 1, dtype=jnp.int32)[:, None, None, None]
    places = jnp.sum(jnp.where(reached[None, :, None, :] == wanted[..., None], order, 0), 0)
    kq = reached.shape[1]
    heads = jnp.arange(rows * kp, dtype=jnp.int32)
    bits = jnp.arange(kq, dtype=jnp.int32)
    end = rows * kp * 32 - 1
    at = jnp.where(places > 0, heads.reshape(rows, kp, 1) * 32 + bits, end)
    first = jnp.min(at, -1)
    flat = first.reshape(-1)
    beyond = jnp.min(jnp.where(heads[None, :] > heads[:, None], flat[None, :], end), -1)
    follow = jnp.min(jnp.where(bits[None, :] > bits[:, None], at[:, :, None, :], end), -1)
    follow = jnp.minimum(follow, beyond.reshape(rows, kp, 1))
    words = follow * 512 + p_slots[..., None] * patterns.shape[1] + places - 1
    words = jnp.pad(words, ((0, 0), (0, 0), (0, 32 - kq))).reshape(-1)
    return jnp.where(jnp.arange(end + 1, dtype=jnp.int32) == end, jnp.min(flat) * 512, words)


def per_device(a_blocks, p_blocks, a_cols, p_slots, touched, touch_cols, halo_rows):
    nrow = lax.axis_size("row")
    nslab = lax.axis_size("slab")
    slab_at = lax.axis_index("slab")
    cap = touched.shape[2]
    slots = touched.shape[1] * cap
    table = touched.reshape(slots)
    patterns = touch_cols.reshape(slots, touch_cols.shape[3])
    kc = patterns.shape[1]
    coarse_ids = (slab_at * nrow + p_slots // cap) * NC + lookup(table, p_slots)
    lists = halo_rows[0]
    sent_ids = coarse_ids[lists]
    depth = lists.shape[1]
    kp = p_slots.shape[1]
    row_at = lax.axis_index("row")
    ids_out = jnp.pad(sent_ids.reshape(4, 1, depth * kp), ((0, 0), (0, 0), (0, 128 - depth * kp)))
    halo, halo_ids = exchange_halo(halo_rows, p_blocks, ids_out)
    outside = jnp.stack([slab_at == 0, slab_at == nslab - 1, row_at == 0, row_at == nrow - 1])
    halo_ids = jnp.where(outside[:, None], -1, halo_ids[:, 0, : depth * kp]).reshape(4 * depth, kp)
    halo = halo.reshape((4 * depth,) + halo.shape[2:])
    ext_ids = jnp.concatenate([coarse_ids, halo_ids], 0)
    words = find_matches(ext_ids, a_cols, p_slots, patterns)
    width = a_blocks.shape[1]
    lists_in = (a_cols.reshape(-1), words)
    bases = (jnp.arange(slots, dtype=jnp.int32) // cap * NC + table) * kc
    packed, ids = packed_partials(*lists_in, bases, a_blocks, p_blocks, halo, kc)
    pieces, counts = reduce_parts(packed, ids.reshape(1, 1, IDS), NC * kc)

    def whole(unused):
        partial = coarse_partials(*lists_in, a_blocks, p_blocks, halo, slots, kc)
        parts = lax.all_to_all(partial.reshape(nrow, cap * width, kc * width), "row", 0, 0)
        owners = lax.all_to_all(touched[0], "row", 0, 0)
        return sum_parts(owners.reshape(-1), parts.reshape(slots, width, kc * width))

    return lax.cond(counts[0, 0] > BLOCKS, whole, lambda unused: assemble(pieces, width, kc), 0)


def solution(mesh):
    in_specs = (
        P(("slab", "row"), None, None),
        P(("slab", "row"), None, None),
        P(("slab", "row"), None),
        P(("slab", "row"), None),
        P(("slab", "row"), None, None),
        P(("slab", "row"), None, None, None),
        P(("slab", "row"), None, None),
    )
    out_specs = P(("slab", "row"), None, None)
    return jax.shard_map(per_device, mesh=mesh, in_specs=in_specs, out_specs=out_specs, check_vma=False)
```

```python
import functools

import jax
import jax.numpy as jnp
from jax import lax
from jax.experimental import pallas as pl
from jax.experimental.pallas import tpu as pltpu
from jax.sharding import PartitionSpec as P

NC = 4
UNROLL = 64
BLOCKS = 128
IDS = 256


def load_operands(a_hbm, p_hbm, halo_hbm, a_v, ext_v, sems):
    rows = p_hbm.shape[0]
    return (
        pltpu.make_async_copy(a_hbm, a_v, sems.at[0]),
        pltpu.make_async_copy(p_hbm, ext_v.at[pl.ds(0, rows)], sems.at[1]),
        pltpu.make_async_copy(halo_hbm, ext_v.at[pl.ds(rows, halo_hbm.shape[0])], sems.at[2]),
    )


def all_products(cols, a_v, ext_v, g_v, pt_v):
    rows, width, span = a_v.shape
    ka = span // width
    pairs = ext_v.shape[2] // (2 * width)
    pair = 2 * width

    def products(i, unused):
        row = a_v[i]
        turned = ext_v[i].T
        for m in range(2 * pairs):
            pt_v[i * 2 * pairs + m] = turned[m * width : (m + 1) * width, :]
        for k in range(ka):
            right = ext_v[cols[k, i]]
            value = jnp.dot(row[:, k * width : (k + 1) * width], right, preferred_element_type=jnp.float32).astype(
                jnp.bfloat16
            )
            for h in range(pairs):
                g_v[(i * ka + k) * pairs + h] = value[:, h * pair : (h + 1) * pair]
        return unused

    lax.fori_loop(0, rows, products, 0, unroll=8)


def add_items(count, items, pt_v, g_v, acc, width, ka, kp):
    pair = 2 * width
    upper = (lax.broadcasted_iota(jnp.int32, (width, pair), 1) >= width).astype(jnp.int32)

    def batch(b, unused):
        found = []
        for u in range(UNROLL):
            word = items[b * UNROLL + u]
            target = word & 1023
            g = g_v[lax.shift_right_logical(word, 11) & 1023]
            g = jnp.where(upper == (lax.shift_right_logical(word, 10) & 1), g, jnp.zeros_like(g))
            z = jnp.dot(pt_v[lax.shift_right_logical(word, 21)], g, preferred_element_type=jnp.float32)
            found.append((pl.ds(pl.multiple_of(target * width, width), width), z))
        for where, z in found:
            acc[where, :] = acc[where, :] + z
        return unused

    lax.fori_loop(0, lax.div(count + UNROLL - 1, UNROLL), batch, 0)


def clear_rows(acc, step, first, last):
    def clear(n, unused):
        acc[pl.ds(pl.multiple_of(n * step, step), step), :] = jnp.zeros((step, acc.shape[1]), jnp.float32)
        return unused

    lax.fori_loop(first, last, clear, 0)


def link_matches(cols_v, slots_v, own_ids, halo_ids, edges, patterns, at_v, follow_v, place_v):
    ka, rows = cols_v.shape
    kp = slots_v.shape[0]
    nslots, kc = patterns.shape
    sides, depth = halo_ids.shape[0], rows // 8
    end = at_v.shape[0] * 128 - 1
    cols = cols_v[...]
    reached = [jnp.full((ka, rows), -2, jnp.int32)] * kp
    for c in range(rows):
        hit = cols == c
        reached = [jnp.where(hit, own_ids[q, c], reached[q]) for q in range(kp)]
    for x in range(sides):
        for d in range(depth):
            hit = cols == rows + x * depth + d
            reached = [
                jnp.where(hit, jnp.where(edges[x], -1, halo_ids[x, 0, d * kp + q]), reached[q]) for q in range(kp)
            ]
    slots = slots_v[...]
    wanted = [jnp.full((kp, rows), -3, jnp.int32)] * kc
    for t in range(nslots):
        hit = slots == t
        wanted = [jnp.where(hit, patterns[t, j], wanted[j]) for j in range(kc)]
    at_v[...] = jnp.full(at_v.shape, end, jnp.int32)
    follow_v[...] = jnp.full(follow_v.shape, end, jnp.int32)
    place_v[...] = jnp.zeros(place_v.shape, jnp.int32)
    which = lax.broadcasted_iota(jnp.int32, (ka, rows), 0) * 128 + lax.broadcasted_iota(jnp.int32, (ka, rows), 1)
    for m in range(kp):
        for q in range(kp):
            place = jnp.full((ka, rows), -1, jnp.int32)
            for j in range(kc):
                place = jnp.where(reached[q] == wanted[j][m : m + 1, :], j, place)
            row = (m * kp + q) * 8
            at_v[row : row + ka, :rows] = jnp.where(place >= 0, which + row * 128, end)
            place_v[row : row + ka, :rows] = slots[m : m + 1, :] * kc + place
    run = jnp.full((1, 128), end, jnp.int32)
    for row in reversed(range(kp * kp * 8)):
        if row % 8 < ka:
            now = at_v[row : row + 1, :]
            follow_v[row : row + 1, :] = run
            run = jnp.minimum(run, now)
    lane = lax.broadcasted_iota(jnp.int32, (8, 128), 1)
    key = jnp.where(run == end, 128 * (end + 1) + end, lane * (end + 1) + run)
    beyond = pltpu.roll(key, 127, 1)
    for step in (1, 2, 4, 8, 16, 32):
        beyond = jnp.minimum(beyond, pltpu.roll(beyond, 128 - step, 1))
    beyond = (beyond & end)[:1, :]
    follow = follow_v[...]
    kinds = lax.broadcasted_iota(jnp.int32, at_v.shape, 0)
    spots = lax.broadcasted_iota(jnp.int32, at_v.shape, 1) - rows
    k = kinds & 7
    q = lax.shift_right_logical(kinds, 3) & (kp - 1)
    m = lax.shift_right_logical(kinds, 2 + kp.bit_length())
    info = ((spots * kp + m) * 1024 + (spots * ka + k) * (kp // 2) + lax.shift_right_logical(q, 1)) * 2 + (q & 1)
    links = jnp.where(follow == end, beyond, follow) * 512 + place_v[...]
    at_v[...] = jnp.where(spots < 0, links, info * 1024)
    start = jnp.min(key[:1], axis=1, keepdims=True) & end
    at_v[at_v.shape[0] - 1 :, :] = jnp.broadcast_to(start, (1, 128))


def packed_kernel(
    cols, words, bases, a_hbm, p_hbm, halo_hbm, out_ref, ids_ref, a_v, ext_v, g_v, pt_v, acc, items, index, sems
):
    rows, width, span = a_v.shape
    ka = span // width
    kp = ext_v.shape[2] // width
    pair = 2 * width
    half = width // 2
    kc = index.shape[0] // bases.shape[0]
    copies = load_operands(a_hbm, p_hbm, halo_hbm, a_v, ext_v, sems)
    for copy in copies:
        copy.start()

    def unset(n, unused):
        for u in range(8):
            index[n * 8 + u] = -1
        return unused

    lax.fori_loop(0, index.shape[0] // 8, unset, 0)

    def no_id(n, unused):
        for u in range(8):
            ids_ref[0, n * 8 + u] = -1
        return unused

    lax.fori_loop(0, ids_ref.shape[1] // 8, no_id, 0)

    last = words.shape[0] * 128 - 1
    first = words[words.shape[0] - 1, 0]

    def more(state):
        return state[0] != last

    def take(state):
        at, count, blocks = state
        word = words[lax.shift_right_logical(at, 7), at & 127]
        place = word & 511
        old = index[place]
        fresh = old < 0
        block = jnp.where(fresh, blocks, old)
        index[place] = block
        kept = jnp.minimum(block, BLOCKS)
        ids_ref[0, kept] = bases[lax.shift_right_logical(place, 3)] + (place & 7)
        items[count] = words[lax.shift_right_logical(at, 7), (at & 127) + rows] + kept
        return (lax.shift_right_logical(word, 9), count + 1, blocks + fresh.astype(jnp.int32))

    _, count, blocks = lax.while_loop(more, take, (first, 0, 0))
    for u in range(UNROLL):
        items[count + u] = BLOCKS
    ids_ref[0, IDS - 1] = blocks
    full = jnp.minimum(lax.div(blocks + 15, 16), BLOCKS // 16)
    clear_rows(acc, 16 * width, 0, full)
    clear_rows(acc, 16 * width, BLOCKS // 16, BLOCKS // 16 + 1)
    for copy in copies:
        copy.wait()
    all_products(cols, a_v, ext_v, g_v, pt_v)
    add_items(count, items, pt_v, g_v, acc, width, ka, kp)
    lower = lax.broadcasted_iota(jnp.int32, (16, pair), 1) < width

    def finish(n, unused):
        for r in range(half):
            one = acc[pl.ds(n * 16 * width + r, 16, stride=width), :]
            two = acc[pl.ds(n * 16 * width + half + r, 16, stride=width), :]
            one = one + pltpu.roll(one, width, 1)
            two = two + pltpu.roll(two, width, 1)
            out_ref[r, pl.ds(pl.multiple_of(n * 16, 16), 16), :] = jnp.where(lower, one, two).astype(jnp.bfloat16)
        return unused

    def empty(n, unused):
        for r in range(half):
            out_ref[r, pl.ds(pl.multiple_of(n * 16, 16), 16), :] = jnp.zeros((16, pair), jnp.bfloat16)
        return unused

    lax.fori_loop(0, full, finish, 0)
    lax.fori_loop(full, BLOCKS // 16, empty, 0)


def packed_partials(cols, words, bases, a_blocks, p_blocks, halo, kc):
    rows, width, span = a_blocks.shape
    kp = p_blocks.shape[2] // width
    ka = span // width
    extended = rows + halo.shape[0]
    smem = pl.BlockSpec(memory_space=pltpu.SMEM)
    vmem = pl.BlockSpec(memory_space=pltpu.VMEM)
    hbm = pl.BlockSpec(memory_space=pl.ANY)
    return pl.pallas_call(
        packed_kernel,
        out_shape=(
            jax.ShapeDtypeStruct((width // 2, BLOCKS, 2 * width), jnp.bfloat16),
            jax.ShapeDtypeStruct((1, IDS), jnp.int32),
        ),
        in_specs=[smem, smem, smem, hbm, hbm, hbm],
        out_specs=(vmem, smem),
        scratch_shapes=[
            pltpu.VMEM((rows, width, span), jnp.bfloat16),
            pltpu.VMEM((extended, width, kp * width), jnp.bfloat16),
            pltpu.VMEM((rows * ka * (kp // 2), width, 2 * width), jnp.bfloat16),
            pltpu.VMEM((rows * kp, width, width), jnp.bfloat16),
            pltpu.VMEM(((BLOCKS + 16) * width, 2 * width), jnp.float32),
            pltpu.SMEM((rows * kp * ka * kp + UNROLL,), jnp.int32),
            pltpu.SMEM((bases.shape[0] * kc,), jnp.int32),
            pltpu.SemaphoreType.DMA((3,)),
        ],
        compiler_params=pltpu.CompilerParams(vmem_limit_bytes=48 * 2**20),
        name="packed_partials",
    )(cols, words, bases, a_blocks, p_blocks, halo)


def halo_kernel(
    rows, own_ids, patterns, cols_v, slots_v, p_ref, ids, out_blocks, words, blocks, came_ids, halo_ids, follow_v, place_v,
    here_sem, send_sem, take_sem
):
    barrier = pltpu.get_barrier_semaphore()
    routes = []
    edges = [None] * 4
    for x, axis, way, chosen in ((2, "row", 1, 3), (3, "row", -1, 2), (0, "slab", 1, 1), (1, "slab", -1, 0)):
        n, at = lax.axis_size(axis), lax.axis_index(axis)
        routes.append((x, {axis: lax.rem(at + way + n, n)}, chosen))
        edges[x] = at == (0 if way == 1 else n - 1)
    for _, to, _ in routes:
        pl.semaphore_signal(barrier, inc=1, device_id=to, device_id_type=pl.DeviceIdType.MESH)
    for x in (3, 2, 1, 0):
        for h in range(blocks.shape[1]):
            blocks[x, h] = p_ref[rows[0, x, h]]
    pl.semaphore_wait(barrier, len(routes))

    def send(z, slot, to, chosen):
        src, dst = ((ids, came_ids), (blocks, out_blocks))[z]
        return pltpu.make_async_remote_copy(
            src_ref=src.at[chosen],
            dst_ref=dst.at[slot],
            send_sem=send_sem.at[z, slot],
            recv_sem=take_sem.at[z, slot],
            device_id=to,
            device_id_type=pl.DeviceIdType.MESH,
        )

    for z in range(2):
        for slot, to, chosen in routes:
            send(z, slot, to, chosen).start()
    for slot, to, chosen in routes:
        send(0, slot, to, chosen).wait()
    here = pltpu.make_async_copy(came_ids, halo_ids, here_sem.at[0])
    here.start()
    here.wait()
    link_matches(cols_v, slots_v, own_ids, halo_ids, edges, patterns, words, follow_v, place_v)
    for slot, to, chosen in routes:
        send(1, slot, to, chosen).wait()


def exchange_halo(rows, own_ids, patterns, cols, slots, p_blocks, ids):
    vmem = pl.BlockSpec(memory_space=pltpu.VMEM)
    smem = pl.BlockSpec(memory_space=pltpu.SMEM)
    hbm = pl.BlockSpec(memory_space=pl.ANY)
    shape = rows.shape[1:] + p_blocks.shape[1:]
    kp = slots.shape[0]
    linked = (kp * kp * 8, 128)
    return pl.pallas_call(
        halo_kernel,
        out_shape=(jax.ShapeDtypeStruct(shape, p_blocks.dtype), jax.ShapeDtypeStruct(linked, jnp.int32)),
        in_specs=[smem, smem, smem, vmem, vmem, vmem, hbm],
        out_specs=(hbm, vmem),
        scratch_shapes=[
            pltpu.VMEM(shape, p_blocks.dtype),
            pltpu.VMEM(ids.shape, jnp.int32),
            pltpu.SMEM(ids.shape, jnp.int32),
            pltpu.VMEM(linked, jnp.int32),
            pltpu.VMEM(linked, jnp.int32),
            pltpu.SemaphoreType.DMA((1,)),
            pltpu.SemaphoreType.DMA((2, 4)),
            pltpu.SemaphoreType.DMA((2, 4)),
        ],
        compiler_params=pltpu.CompilerParams(collective_id=1, has_side_effects=True, vmem_limit_bytes=32 * 2**20),
        name="exchange_halo",
    )(rows, own_ids, patterns, cols, slots, p_blocks, ids)


def reduce_kernel(
    parts, ids, pieces, most_ref, came_parts, came_ids, sums, flag, came_flags, acc, send_sem, take_sem, flag_send, flag_take
):
    row, slab = lax.axis_index("row"), lax.axis_index("slab")
    n, slabs = lax.axis_size("row"), lax.axis_size("slab")
    blocks = parts.shape[1]
    targets, lanes = acc.shape
    share = targets // n
    barrier = pltpu.get_barrier_semaphore()
    mesh_id = pl.DeviceIdType.MESH

    def greet_row(o, unused):
        pl.semaphore_signal(barrier, inc=1, device_id={"row": lax.rem(row + o, n)}, device_id_type=mesh_id)
        return unused

    def greet_slab(o, unused):
        pl.semaphore_signal(barrier, inc=1, device_id={"slab": lax.rem(slab + o, slabs)}, device_id_type=mesh_id)
        return unused

    lax.fori_loop(1, n, greet_row, 0)
    lax.fori_loop(1, slabs, greet_slab, 0)
    pl.semaphore_wait(barrier, n + slabs - 2)

    def row_copy(x, o, src, dst, other):
        return pltpu.make_async_remote_copy(
            src_ref=src,
            dst_ref=dst,
            send_sem=send_sem.at[x, o],
            recv_sem=take_sem.at[x, o],
            device_id={"row": other},
            device_id_type=mesh_id,
        )

    def to_of(o):
        return lax.rem(row + o, n)

    def from_of(o):
        return lax.rem(row + n - o, n)

    def begin(o, unused):
        to = to_of(o)
        row_copy(0, o, ids.at[0], came_ids.at[row], to).start()
        row_copy(1, o, parts.at[to], came_parts.at[row], to).start()
        return unused

    lax.fori_loop(1, n, begin, 0)
    order = lax.broadcasted_iota(jnp.int32, (targets, blocks), 0)

    def spread(names, values):
        hot = jnp.where(order == names[:, :blocks], 1.0, 0.0).astype(jnp.bfloat16)
        return jnp.dot(hot, values, preferred_element_type=jnp.float32)

    own = ids[0]
    acc[...] = spread(own, parts[row])
    last = lax.broadcasted_iota(jnp.int32, own.shape, 1) == own.shape[1] - 1

    def add(o, most):
        came = from_of(o)
        row_copy(0, o, ids.at[0], came_ids.at[came], came).wait_recv()
        row_copy(1, o, parts.at[came], came_parts.at[came], came).wait_recv()
        names = came_ids[came]
        acc[...] += spread(names, came_parts[came])
        return jnp.maximum(most, names)

    most = lax.fori_loop(1, n, add, own)
    flag[...] = jnp.where(last, most, 0)

    def flag_copy(o, at, other):
        return pltpu.make_async_remote_copy(
            src_ref=flag,
            dst_ref=came_flags.at[at],
            send_sem=flag_send.at[o],
            recv_sem=flag_take.at[o],
            device_id={"slab": other},
            device_id_type=mesh_id,
        )

    def begin_flag(o, unused):
        flag_copy(o, slab, lax.rem(slab + o, slabs)).start()
        return unused

    lax.fori_loop(1, slabs, begin_flag, 0)
    for p in range(n):
        sums[p] = acc[p * share : (p + 1) * share, :].astype(jnp.bfloat16)

    def begin_sums(o, unused):
        to = to_of(o)
        row_copy(2, o, sums.at[to], pieces.at[row], to).start()
        return unused

    lax.fori_loop(1, n, begin_sums, 0)
    pieces[row] = sums[row]

    def end_flag(o, most):
        came = lax.rem(slab + slabs - o, slabs)
        flag_copy(o, slab, lax.rem(slab + o, slabs)).wait_send()
        flag_copy(o, came, came).wait_recv()
        return jnp.maximum(most, came_flags[came])

    most_ref[0, 0] = jnp.max(lax.fori_loop(1, slabs, end_flag, flag[...]))

    def end(o, unused):
        to, came = to_of(o), from_of(o)
        row_copy(0, o, ids.at[0], came_ids.at[row], to).wait_send()
        row_copy(1, o, parts.at[to], came_parts.at[row], to).wait_send()
        row_copy(2, o, sums.at[to], pieces.at[row], to).wait_send()
        row_copy(2, o, sums.at[came], pieces.at[came], came).wait_recv()
        return unused

    lax.fori_loop(1, n, end, 0)


def reduce_parts(parts, ids, share):
    n, slabs = lax.axis_size("row"), lax.axis_size("slab")
    _, blocks, lanes = parts.shape
    vmem = pl.BlockSpec(memory_space=pltpu.VMEM)
    return pl.pallas_call(
        reduce_kernel,
        out_shape=(
            jax.ShapeDtypeStruct((n, share, lanes), jnp.bfloat16),
            jax.ShapeDtypeStruct((1, 1), jnp.int32),
        ),
        in_specs=[vmem, vmem],
        out_specs=(vmem, pl.BlockSpec(memory_space=pltpu.SMEM)),
        scratch_shapes=[
            pltpu.VMEM((n, blocks, lanes), jnp.bfloat16),
            pltpu.VMEM((n, 1, IDS), jnp.int32),
            pltpu.VMEM((n, share, lanes), jnp.bfloat16),
            pltpu.VMEM((1, IDS), jnp.int32),
            pltpu.VMEM((slabs, 1, IDS), jnp.int32),
            pltpu.VMEM((n * share, lanes), jnp.float32),
            pltpu.SemaphoreType.DMA((3, n)),
            pltpu.SemaphoreType.DMA((3, n)),
            pltpu.SemaphoreType.DMA((slabs,)),
            pltpu.SemaphoreType.DMA((slabs,)),
        ],
        compiler_params=pltpu.CompilerParams(
            collective_id=0, has_side_effects=True, vmem_limit_bytes=32 * 2**20
        ),
        name="reduce_parts",
    )(parts, ids)


def assemble_kernel(pieces_ref, out_ref, wide):
    n, targets, pair = pieces_ref.shape
    owned, width, outspan = out_ref.shape
    half = width // 2
    kc = targets // owned
    lower = lax.broadcasted_iota(jnp.int32, (half, pair), 1) < half * 2
    wide[...] = pieces_ref[...].reshape(n * targets, pair).astype(jnp.float32)
    for g in range(owned):
        for h in range(kc // 2):
            one = wide[pl.ds(g * kc + 2 * h, n, stride=targets), :]
            two = wide[pl.ds(g * kc + 2 * h + 1, n, stride=targets), :]
            span = slice(h * pair, (h + 1) * pair)
            out_ref[g, :half, span] = jnp.where(lower, one, pltpu.roll(two, width, 1))
            out_ref[g, half:, span] = jnp.where(lower, pltpu.roll(one, width, 1), two)


def assemble(pieces, width, kc):
    vmem = pl.BlockSpec(memory_space=pltpu.VMEM)
    n, targets, pair = pieces.shape
    return pl.pallas_call(
        assemble_kernel,
        out_shape=jax.ShapeDtypeStruct((NC, width, kc * width), jnp.float32),
        in_specs=[vmem],
        out_specs=vmem,
        scratch_shapes=[pltpu.VMEM((n * targets, pair), jnp.float32)],
        name="assemble",
    )(pieces)


def coarse_kernel(
    cols, words, a_hbm, p_hbm, halo_hbm, out_ref, a_v, ext_v, g_v, pt_v, acc, items, sems
):
    rows, width, span = a_v.shape
    ka = span // width
    kp = ext_v.shape[2] // width
    nslots, _, outspan = out_ref.shape
    kc = outspan // width
    pair = 2 * width
    copies = load_operands(a_hbm, p_hbm, halo_hbm, a_v, ext_v, sems)
    for copy in copies:
        copy.start()
    clear_rows(acc, width, 0, acc.shape[0] // width)

    last = words.shape[0] * 128 - 1
    first = words[words.shape[0] - 1, 0]

    def more(state):
        return state[0] != last

    def take(state):
        at, count = state
        word = words[lax.shift_right_logical(at, 7), at & 127]
        items[count] = words[lax.shift_right_logical(at, 7), (at & 127) + rows] + (word & 511)
        return (lax.shift_right_logical(word, 9), count + 1)

    _, count = lax.while_loop(more, take, (first, 0))
    for u in range(UNROLL):
        items[count + u] = nslots * kc
    for copy in copies:
        copy.wait()
    all_products(cols, a_v, ext_v, g_v, pt_v)
    add_items(count, items, pt_v, g_v, acc, width, ka, kp)
    lower = lax.broadcasted_iota(jnp.int32, (width, pair), 1) < width

    def finish(t, unused):
        for h in range(kc // 2):
            one = acc[pl.ds(pl.multiple_of((t * kc + 2 * h) * width, width), width), :]
            two = acc[pl.ds(pl.multiple_of((t * kc + 2 * h + 1) * width, width), width), :]
            one = one + pltpu.roll(one, width, 1)
            two = two + pltpu.roll(two, width, 1)
            out_ref[t, :, h * pair : (h + 1) * pair] = jnp.where(lower, one, two).astype(jnp.bfloat16)
        return unused

    lax.fori_loop(0, nslots, finish, 0)


def coarse_partials(cols, words, a_blocks, p_blocks, halo, nslots, kc):
    rows, width, span = a_blocks.shape
    kp = p_blocks.shape[2] // width
    ka = span // width
    extended = rows + halo.shape[0]
    smem = pl.BlockSpec(memory_space=pltpu.SMEM)
    hbm = pl.BlockSpec(memory_space=pl.ANY)
    vmem = pl.BlockSpec(memory_space=pltpu.VMEM)
    return pl.pallas_call(
        coarse_kernel,
        out_shape=jax.ShapeDtypeStruct((nslots, width, kc * width), jnp.bfloat16),
        in_specs=[smem, smem, hbm, hbm, hbm],
        out_specs=pl.BlockSpec(memory_space=pltpu.VMEM),
        scratch_shapes=[
            pltpu.VMEM((rows, width, span), jnp.bfloat16),
            pltpu.VMEM((extended, width, kp * width), jnp.bfloat16),
            pltpu.VMEM((rows * ka * (kp // 2), width, 2 * width), jnp.bfloat16),
            pltpu.VMEM((rows * kp, width, width), jnp.bfloat16),
            pltpu.VMEM(((nslots * kc + 1) * width, 2 * width), jnp.float32),
            pltpu.SMEM((rows * kp * ka * kp + UNROLL,), jnp.int32),
            pltpu.SemaphoreType.DMA((3,)),
        ],
        compiler_params=pltpu.CompilerParams(vmem_limit_bytes=56 * 2**20),
        name="coarse_partials",
    )(cols, words, a_blocks, p_blocks, halo)


def sum_kernel(ids, parts, out_ref):
    out_ref[...] = jnp.zeros_like(out_ref)

    def one(n, unused):
        row = ids[n]

        @pl.when(row >= 0)
        def _():
            out_ref[row] = out_ref[row] + parts[n].astype(jnp.float32)

        return unused

    lax.fori_loop(0, parts.shape[0], one, 0)


def sum_parts(ids, parts):
    return pl.pallas_call(
        sum_kernel,
        out_shape=jax.ShapeDtypeStruct((NC,) + parts.shape[1:], jnp.float32),
        in_specs=[pl.BlockSpec(memory_space=pltpu.SMEM), pl.BlockSpec(memory_space=pltpu.VMEM)],
        out_specs=pl.BlockSpec(memory_space=pltpu.VMEM),
        compiler_params=pltpu.CompilerParams(vmem_limit_bytes=32 * 2**20),
        name="sum_parts",
    )(ids, parts)


def lookup(table, index):
    hot = index[..., None] == jnp.arange(table.shape[0], dtype=jnp.int32)
    return jnp.sum(jnp.where(hot, table, 0), axis=-1)


def per_device(a_blocks, p_blocks, a_cols, p_slots, touched, touch_cols, halo_rows):
    nrow = lax.axis_size("row")
    slab_at = lax.axis_index("slab")
    cap = touched.shape[2]
    slots = touched.shape[1] * cap
    table = touched.reshape(slots)
    patterns = touch_cols.reshape(slots, touch_cols.shape[3])
    kc = patterns.shape[1]
    coarse_ids = (slab_at * nrow + p_slots // cap) * NC + lookup(table, p_slots)
    lists = halo_rows[0]
    sent_ids = coarse_ids[lists]
    depth = lists.shape[1]
    kp = p_slots.shape[1]
    ids_out = jnp.pad(sent_ids.reshape(4, 1, depth * kp), ((0, 0), (0, 0), (0, 128 - depth * kp)))
    columns = a_cols.T
    halo, words = exchange_halo(halo_rows, coarse_ids.T, patterns, columns, p_slots.T, p_blocks, ids_out)
    halo = halo.reshape((4 * depth,) + halo.shape[2:])
    width = a_blocks.shape[1]
    bases = (jnp.arange(slots, dtype=jnp.int32) // cap * NC + table) * kc
    packed, ids = packed_partials(columns, words, bases, a_blocks, p_blocks, halo, kc)
    pieces, counts = reduce_parts(packed, ids.reshape(1, 1, IDS), NC * kc)

    def whole(unused):
        partial = coarse_partials(columns, words, a_blocks, p_blocks, halo, slots, kc)
        parts = lax.all_to_all(partial.reshape(nrow, cap * width, kc * width), "row", 0, 0)
        owners = lax.all_to_all(touched[0], "row", 0, 0)
        return sum_parts(owners.reshape(-1), parts.reshape(slots, width, kc * width))

    return lax.cond(counts[0, 0] > BLOCKS, whole, lambda unused: assemble(pieces, width, kc), 0)


def solution(mesh):
    in_specs = (
        P(("slab", "row"), None, None),
        P(("slab", "row"), None, None),
        P(("slab", "row"), None),
        P(("slab", "row"), None),
        P(("slab", "row"), None, None),
        P(("slab", "row"), None, None, None),
        P(("slab", "row"), None, None),
    )
    out_specs = P(("slab", "row"), None, None)
    return jax.shard_map(per_device, mesh=mesh, in_specs=in_specs, out_specs=out_specs, check_vma=False)
```

```python
import functools

import jax
import jax.numpy as jnp
from jax import lax
from jax.experimental import pallas as pl
from jax.experimental.pallas import tpu as pltpu
from jax.sharding import PartitionSpec as P

NC = 4
UNROLL = 64
BLOCKS = 128
IDS = 256


def load_operands(a_hbm, p_hbm, halo_hbm, a_v, ext_v, sems):
    rows = p_hbm.shape[0]
    return (
        pltpu.make_async_copy(a_hbm, a_v, sems.at[0]),
        pltpu.make_async_copy(p_hbm, ext_v.at[pl.ds(0, rows)], sems.at[1]),
        pltpu.make_async_copy(halo_hbm, ext_v.at[pl.ds(rows, halo_hbm.shape[0])], sems.at[2]),
    )


def all_products(cols, a_v, ext_v, g_v, pt_v):
    rows, width, span = a_v.shape
    ka = span // width
    pairs = ext_v.shape[2] // (2 * width)
    pair = 2 * width

    def products(i, unused):
        row = a_v[i]
        turned = ext_v[i].T
        for m in range(2 * pairs):
            pt_v[i * 2 * pairs + m] = turned[m * width : (m + 1) * width, :]
        for k in range(ka):
            right = ext_v[cols[k, i]]
            value = jnp.dot(row[:, k * width : (k + 1) * width], right, preferred_element_type=jnp.float32).astype(
                jnp.bfloat16
            )
            for h in range(pairs):
                g_v[(i * ka + k) * pairs + h] = value[:, h * pair : (h + 1) * pair]
        return unused

    lax.fori_loop(0, rows, products, 0, unroll=8)


def add_items(count, items, pt_v, g_v, acc, width, ka, kp):
    pair = 2 * width
    upper = (lax.broadcasted_iota(jnp.int32, (width, pair), 1) >= width).astype(jnp.int32)

    def batch(b, unused):
        found = []
        for u in range(UNROLL):
            word = items[b * UNROLL + u]
            target = word & 1023
            g = g_v[lax.shift_right_logical(word, 11) & 1023]
            g = jnp.where(upper == (lax.shift_right_logical(word, 10) & 1), g, jnp.zeros_like(g))
            z = jnp.dot(pt_v[lax.shift_right_logical(word, 21)], g, preferred_element_type=jnp.float32)
            found.append((pl.ds(pl.multiple_of(target * width, width), width), z))
        for where, z in found:
            acc[where, :] = acc[where, :] + z
        return unused

    lax.fori_loop(0, lax.div(count + UNROLL - 1, UNROLL), batch, 0)


def clear_rows(acc, step, first, last):
    def clear(n, unused):
        acc[pl.ds(pl.multiple_of(n * step, step), step), :] = jnp.zeros((step, acc.shape[1]), jnp.float32)
        return unused

    lax.fori_loop(first, last, clear, 0)


def link_matches(cols_v, slots_v, own_ids, halo_ids, edges, patterns, at_v, follow_v, place_v):
    ka, rows = cols_v.shape
    kp = slots_v.shape[0]
    _, cap, kc, owners = patterns.shape
    sides, depth = halo_ids.shape[0], rows // 8
    end = at_v.shape[0] * 128 - 1
    cols = cols_v[...]
    reached = [jnp.full((ka, rows), -2, jnp.int32)] * kp
    for c in range(rows):
        hit = cols == c
        reached = [jnp.where(hit, own_ids[q, c], reached[q]) for q in range(kp)]
    for x in range(sides):
        for d in range(depth):
            hit = cols == rows + x * depth + d
            reached = [
                jnp.where(hit, jnp.where(edges[x], -1, halo_ids[x, 0, d * kp + q]), reached[q]) for q in range(kp)
            ]
    slots = slots_v[...]
    wanted = [jnp.full((kp, rows), -3, jnp.int32)] * kc
    for p in range(owners):
        for c in range(cap):
            hit = slots == p * cap + c
            wanted = [jnp.where(hit, patterns[0, c, j, p], wanted[j]) for j in range(kc)]
    at_v[...] = jnp.full(at_v.shape, end, jnp.int32)
    follow_v[...] = jnp.full(follow_v.shape, end, jnp.int32)
    place_v[...] = jnp.zeros(place_v.shape, jnp.int32)
    which = lax.broadcasted_iota(jnp.int32, (ka, rows), 0) * 128 + lax.broadcasted_iota(jnp.int32, (ka, rows), 1)
    for m in range(kp):
        for q in range(kp):
            place = jnp.full((ka, rows), -1, jnp.int32)
            for j in range(kc):
                place = jnp.where(reached[q] == wanted[j][m : m + 1, :], j, place)
            row = (m * kp + q) * 8
            at_v[row : row + ka, :rows] = jnp.where(place >= 0, which + row * 128, end)
            place_v[row : row + ka, :rows] = slots[m : m + 1, :] * kc + place
    run = jnp.full((1, 128), end, jnp.int32)
    for row in reversed(range(kp * kp * 8)):
        if row % 8 < ka:
            now = at_v[row : row + 1, :]
            follow_v[row : row + 1, :] = run
            run = jnp.minimum(run, now)
    lane = lax.broadcasted_iota(jnp.int32, (8, 128), 1)
    key = jnp.where(run == end, 128 * (end + 1) + end, lane * (end + 1) + run)
    beyond = pltpu.roll(key, 127, 1)
    for step in (1, 2, 4, 8, 16, 32):
        beyond = jnp.minimum(beyond, pltpu.roll(beyond, 128 - step, 1))
    beyond = (beyond & end)[:1, :]
    follow = follow_v[...]
    kinds = lax.broadcasted_iota(jnp.int32, at_v.shape, 0)
    spots = lax.broadcasted_iota(jnp.int32, at_v.shape, 1) - rows
    k = kinds & 7
    q = lax.shift_right_logical(kinds, 3) & (kp - 1)
    m = lax.shift_right_logical(kinds, 2 + kp.bit_length())
    info = ((spots * kp + m) * 1024 + (spots * ka + k) * (kp // 2) + lax.shift_right_logical(q, 1)) * 2 + (q & 1)
    links = jnp.where(follow == end, beyond, follow) * 512 + place_v[...]
    at_v[...] = jnp.where(spots < 0, links, info * 1024)
    start = jnp.min(key[:1], axis=1, keepdims=True) & end
    at_v[at_v.shape[0] - 1 :, :] = jnp.broadcast_to(start, (1, 128))


def packed_kernel(
    cols, words, table, a_hbm, p_hbm, halo_hbm, out_ref, ids_ref, a_v, ext_v, g_v, pt_v, acc, items, index, bases, sems
):
    rows, width, span = a_v.shape
    ka = span // width
    kp = ext_v.shape[2] // width
    pair = 2 * width
    half = width // 2
    kc = index.shape[0] // bases.shape[0]
    copies = load_operands(a_hbm, p_hbm, halo_hbm, a_v, ext_v, sems)
    for copy in copies:
        copy.start()

    for p in range(table.shape[2]):
        for c in range(table.shape[1]):
            bases[p * table.shape[1] + c] = (p * NC + table[0, c, p]) * kc

    def unset(n, unused):
        for u in range(8):
            index[n * 8 + u] = -1
        return unused

    lax.fori_loop(0, index.shape[0] // 8, unset, 0)

    def no_id(n, unused):
        for u in range(8):
            ids_ref[0, n * 8 + u] = -1
        return unused

    lax.fori_loop(0, ids_ref.shape[1] // 8, no_id, 0)

    last = words.shape[0] * 128 - 1
    first = words[words.shape[0] - 1, 0]

    def more(state):
        return state[0] != last

    def take(state):
        at, count, blocks = state
        word = words[lax.shift_right_logical(at, 7), at & 127]
        place = word & 511
        old = index[place]
        fresh = old < 0
        block = jnp.where(fresh, blocks, old)
        index[place] = block
        kept = jnp.minimum(block, BLOCKS)
        ids_ref[0, kept] = bases[lax.shift_right_logical(place, 3)] + (place & 7)
        items[count] = words[lax.shift_right_logical(at, 7), (at & 127) + rows] + kept
        return (lax.shift_right_logical(word, 9), count + 1, blocks + fresh.astype(jnp.int32))

    _, count, blocks = lax.while_loop(more, take, (first, 0, 0))
    for u in range(UNROLL):
        items[count + u] = BLOCKS
    ids_ref[0, IDS - 1] = blocks
    full = jnp.minimum(lax.div(blocks + 15, 16), BLOCKS // 16)
    clear_rows(acc, 16 * width, 0, full)
    clear_rows(acc, 16 * width, BLOCKS // 16, BLOCKS // 16 + 1)
    for copy in copies:
        copy.wait()
    all_products(cols, a_v, ext_v, g_v, pt_v)
    add_items(count, items, pt_v, g_v, acc, width, ka, kp)
    lower = lax.broadcasted_iota(jnp.int32, (16, pair), 1) < width

    def finish(n, unused):
        for r in range(half):
            one = acc[pl.ds(n * 16 * width + r, 16, stride=width), :]
            two = acc[pl.ds(n * 16 * width + half + r, 16, stride=width), :]
            one = one + pltpu.roll(one, width, 1)
            two = two + pltpu.roll(two, width, 1)
            out_ref[r, pl.ds(pl.multiple_of(n * 16, 16), 16), :] = jnp.where(lower, one, two).astype(jnp.bfloat16)
        return unused

    def empty(n, unused):
        for r in range(half):
            out_ref[r, pl.ds(pl.multiple_of(n * 16, 16), 16), :] = jnp.zeros((16, pair), jnp.bfloat16)
        return unused

    lax.fori_loop(0, full, finish, 0)
    lax.fori_loop(full, BLOCKS // 16, empty, 0)


def packed_partials(cols, words, table, a_blocks, p_blocks, halo, kc):
    rows, width, span = a_blocks.shape
    kp = p_blocks.shape[2] // width
    ka = span // width
    extended = rows + halo.shape[0]
    nslots = table.shape[1] * table.shape[2]
    smem = pl.BlockSpec(memory_space=pltpu.SMEM)
    vmem = pl.BlockSpec(memory_space=pltpu.VMEM)
    hbm = pl.BlockSpec(memory_space=pl.ANY)
    return pl.pallas_call(
        packed_kernel,
        out_shape=(
            jax.ShapeDtypeStruct((width // 2, BLOCKS, 2 * width), jnp.bfloat16),
            jax.ShapeDtypeStruct((1, IDS), jnp.int32),
        ),
        in_specs=[smem, smem, smem, hbm, hbm, hbm],
        out_specs=(vmem, smem),
        scratch_shapes=[
            pltpu.VMEM((rows, width, span), jnp.bfloat16),
            pltpu.VMEM((extended, width, kp * width), jnp.bfloat16),
            pltpu.VMEM((rows * ka * (kp // 2), width, 2 * width), jnp.bfloat16),
            pltpu.VMEM((rows * kp, width, width), jnp.bfloat16),
            pltpu.VMEM(((BLOCKS + 16) * width, 2 * width), jnp.float32),
            pltpu.SMEM((rows * kp * ka * kp + UNROLL,), jnp.int32),
            pltpu.SMEM((nslots * kc,), jnp.int32),
            pltpu.SMEM((nslots,), jnp.int32),
            pltpu.SemaphoreType.DMA((3,)),
        ],
        compiler_params=pltpu.CompilerParams(vmem_limit_bytes=48 * 2**20),
        name="packed_partials",
    )(cols, words, table, a_blocks, p_blocks, halo)


def halo_kernel(
    rows, table, patterns, cols_v, slots_v, p_ref, out_blocks, words, blocks, own_v, own_ids, ids, came_ids, halo_ids,
    follow_v, place_v, here_sem, send_sem, take_sem
):
    barrier = pltpu.get_barrier_semaphore()
    routes = []
    edges = [None] * 4
    for x, axis, way, chosen in ((2, "row", 1, 3), (3, "row", -1, 2), (0, "slab", 1, 1), (1, "slab", -1, 0)):
        n, at = lax.axis_size(axis), lax.axis_index(axis)
        routes.append((x, {axis: lax.rem(at + way + n, n)}, chosen))
        edges[x] = at == (0 if way == 1 else n - 1)
    for _, to, _ in routes:
        pl.semaphore_signal(barrier, inc=1, device_id=to, device_id_type=pl.DeviceIdType.MESH)
    for x in (3, 2, 1, 0):
        for h in range(blocks.shape[1]):
            blocks[x, h] = p_ref[rows[0, x, h]]
    pl.semaphore_wait(barrier, len(routes))

    def send(z, slot, to, chosen):
        src, dst = ((ids, came_ids), (blocks, out_blocks))[z]
        return pltpu.make_async_remote_copy(
            src_ref=src.at[chosen],
            dst_ref=dst.at[slot],
            send_sem=send_sem.at[z, slot],
            recv_sem=take_sem.at[z, slot],
            device_id=to,
            device_id_type=pl.DeviceIdType.MESH,
        )

    for slot, to, chosen in routes:
        send(1, slot, to, chosen).start()
    slots = slots_v[...]
    kp, cap = slots.shape[0], table.shape[1]
    local = jnp.zeros_like(slots)
    for p in range(table.shape[2]):
        for c in range(cap):
            local = jnp.where(slots == p * cap + c, table[0, c, p], local)
    owner = lax.axis_index("slab") * lax.axis_size("row") + lax.div(slots, cap)
    own_v[...] = jnp.zeros(own_v.shape, jnp.int32)
    own_v[:kp, : slots.shape[1]] = owner * NC + local
    here = pltpu.make_async_copy(own_v, own_ids, here_sem.at[1])
    here.start()
    here.wait()
    lane = lax.broadcasted_iota(jnp.int32, (1, 128), 1)
    for x in range(rows.shape[1]):
        listed = jnp.zeros((1, 128), jnp.int32)
        for d in range(rows.shape[2]):
            at = rows[0, x, d]
            for m in range(kp):
                listed = jnp.where(lane == d * kp + m, own_ids[m, at], listed)
        ids[x] = listed
    for slot, to, chosen in routes:
        send(0, slot, to, chosen).start()
    for slot, to, chosen in routes:
        send(0, slot, to, chosen).wait()
    here = pltpu.make_async_copy(came_ids, halo_ids, here_sem.at[0])
    here.start()
    here.wait()
    link_matches(cols_v, slots_v, own_ids, halo_ids, edges, patterns, words, follow_v, place_v)
    for slot, to, chosen in routes:
        send(1, slot, to, chosen).wait()


def exchange_halo(rows, table, patterns, cols, slots, p_blocks):
    vmem = pl.BlockSpec(memory_space=pltpu.VMEM)
    smem = pl.BlockSpec(memory_space=pltpu.SMEM)
    hbm = pl.BlockSpec(memory_space=pl.ANY)
    shape = rows.shape[1:] + p_blocks.shape[1:]
    kp = slots.shape[0]
    linked = (kp * kp * 8, 128)
    return pl.pallas_call(
        halo_kernel,
        out_shape=(jax.ShapeDtypeStruct(shape, p_blocks.dtype), jax.ShapeDtypeStruct(linked, jnp.int32)),
        in_specs=[smem, smem, smem, vmem, vmem, vmem],
        out_specs=(hbm, vmem),
        scratch_shapes=[
            pltpu.VMEM(shape, p_blocks.dtype),
            pltpu.VMEM((8, 128), jnp.int32),
            pltpu.SMEM((8, 128), jnp.int32),
            pltpu.VMEM((4, 1, 128), jnp.int32),
            pltpu.VMEM((4, 1, 128), jnp.int32),
            pltpu.SMEM((4, 1, 128), jnp.int32),
            pltpu.VMEM(linked, jnp.int32),
            pltpu.VMEM(linked, jnp.int32),
            pltpu.SemaphoreType.DMA((2,)),
            pltpu.SemaphoreType.DMA((2, 4)),
            pltpu.SemaphoreType.DMA((2, 4)),
        ],
        compiler_params=pltpu.CompilerParams(collective_id=1, has_side_effects=True, vmem_limit_bytes=32 * 2**20),
        name="exchange_halo",
    )(rows, table, patterns, cols, slots, p_blocks)


def reduce_kernel(
    parts, ids, pieces, most_ref, came_parts, came_ids, sums, flag, came_flags, acc, send_sem, take_sem, flag_send, flag_take
):
    row, slab = lax.axis_index("row"), lax.axis_index("slab")
    n, slabs = lax.axis_size("row"), lax.axis_size("slab")
    blocks = parts.shape[1]
    targets, lanes = acc.shape
    share = targets // n
    barrier = pltpu.get_barrier_semaphore()
    mesh_id = pl.DeviceIdType.MESH

    def greet_row(o, unused):
        pl.semaphore_signal(barrier, inc=1, device_id={"row": lax.rem(row + o, n)}, device_id_type=mesh_id)
        return unused

    def greet_slab(o, unused):
        pl.semaphore_signal(barrier, inc=1, device_id={"slab": lax.rem(slab + o, slabs)}, device_id_type=mesh_id)
        return unused

    lax.fori_loop(1, n, greet_row, 0)
    lax.fori_loop(1, slabs, greet_slab, 0)
    pl.semaphore_wait(barrier, n + slabs - 2)

    def row_copy(x, o, src, dst, other):
        return pltpu.make_async_remote_copy(
            src_ref=src,
            dst_ref=dst,
            send_sem=send_sem.at[x, o],
            recv_sem=take_sem.at[x, o],
            device_id={"row": other},
            device_id_type=mesh_id,
        )

    def to_of(o):
        return lax.rem(row + o, n)

    def from_of(o):
        return lax.rem(row + n - o, n)

    def begin(o, unused):
        to = to_of(o)
        row_copy(0, o, ids.at[0], came_ids.at[row], to).start()
        row_copy(1, o, parts.at[to], came_parts.at[row], to).start()
        return unused

    lax.fori_loop(1, n, begin, 0)
    order = lax.broadcasted_iota(jnp.int32, (targets, blocks), 0)

    def spread(names, values):
        hot = jnp.where(order == names[:, :blocks], 1.0, 0.0).astype(jnp.bfloat16)
        return jnp.dot(hot, values, preferred_element_type=jnp.float32)

    own = ids[0]
    acc[...] = spread(own, parts[row])
    last = lax.broadcasted_iota(jnp.int32, own.shape, 1) == own.shape[1] - 1

    def add(o, most):
        came = from_of(o)
        row_copy(0, o, ids.at[0], came_ids.at[came], came).wait_recv()
        row_copy(1, o, parts.at[came], came_parts.at[came], came).wait_recv()
        names = came_ids[came]
        acc[...] += spread(names, came_parts[came])
        return jnp.maximum(most, names)

    most = lax.fori_loop(1, n, add, own)
    flag[...] = jnp.where(last, most, 0)

    def flag_copy(o, at, other):
        return pltpu.make_async_remote_copy(
            src_ref=flag,
            dst_ref=came_flags.at[at],
            send_sem=flag_send.at[o],
            recv_sem=flag_take.at[o],
            device_id={"slab": other},
            device_id_type=mesh_id,
        )

    def begin_flag(o, unused):
        flag_copy(o, slab, lax.rem(slab + o, slabs)).start()
        return unused

    lax.fori_loop(1, slabs, begin_flag, 0)
    for p in range(n):
        sums[p] = acc[p * share : (p + 1) * share, :].astype(jnp.bfloat16)

    def begin_sums(o, unused):
        to = to_of(o)
        row_copy(2, o, sums.at[to], pieces.at[row], to).start()
        return unused

    lax.fori_loop(1, n, begin_sums, 0)
    pieces[row] = sums[row]

    def end_flag(o, most):
        came = lax.rem(slab + slabs - o, slabs)
        flag_copy(o, slab, lax.rem(slab + o, slabs)).wait_send()
        flag_copy(o, came, came).wait_recv()
        return jnp.maximum(most, came_flags[came])

    most_ref[0, 0] = jnp.max(lax.fori_loop(1, slabs, end_flag, flag[...]))

    def end(o, unused):
        to, came = to_of(o), from_of(o)
        row_copy(0, o, ids.at[0], came_ids.at[row], to).wait_send()
        row_copy(1, o, parts.at[to], came_parts.at[row], to).wait_send()
        row_copy(2, o, sums.at[to], pieces.at[row], to).wait_send()
        row_copy(2, o, sums.at[came], pieces.at[came], came).wait_recv()
        return unused

    lax.fori_loop(1, n, end, 0)


def reduce_parts(parts, ids, share):
    n, slabs = lax.axis_size("row"), lax.axis_size("slab")
    _, blocks, lanes = parts.shape
    vmem = pl.BlockSpec(memory_space=pltpu.VMEM)
    return pl.pallas_call(
        reduce_kernel,
        out_shape=(
            jax.ShapeDtypeStruct((n, share, lanes), jnp.bfloat16),
            jax.ShapeDtypeStruct((1, 1), jnp.int32),
        ),
        in_specs=[vmem, vmem],
        out_specs=(vmem, pl.BlockSpec(memory_space=pltpu.SMEM)),
        scratch_shapes=[
            pltpu.VMEM((n, blocks, lanes), jnp.bfloat16),
            pltpu.VMEM((n, 1, IDS), jnp.int32),
            pltpu.VMEM((n, share, lanes), jnp.bfloat16),
            pltpu.VMEM((1, IDS), jnp.int32),
            pltpu.VMEM((slabs, 1, IDS), jnp.int32),
            pltpu.VMEM((n * share, lanes), jnp.float32),
            pltpu.SemaphoreType.DMA((3, n)),
            pltpu.SemaphoreType.DMA((3, n)),
            pltpu.SemaphoreType.DMA((slabs,)),
            pltpu.SemaphoreType.DMA((slabs,)),
        ],
        compiler_params=pltpu.CompilerParams(
            collective_id=0, has_side_effects=True, vmem_limit_bytes=32 * 2**20
        ),
        name="reduce_parts",
    )(parts, ids)


def assemble_kernel(pieces_ref, out_ref, wide):
    n, targets, pair = pieces_ref.shape
    owned, width, outspan = out_ref.shape
    half = width // 2
    kc = targets // owned
    lower = lax.broadcasted_iota(jnp.int32, (half, pair), 1) < half * 2
    wide[...] = pieces_ref[...].reshape(n * targets, pair).astype(jnp.float32)
    for g in range(owned):
        for h in range(kc // 2):
            one = wide[pl.ds(g * kc + 2 * h, n, stride=targets), :]
            two = wide[pl.ds(g * kc + 2 * h + 1, n, stride=targets), :]
            span = slice(h * pair, (h + 1) * pair)
            out_ref[g, :half, span] = jnp.where(lower, one, pltpu.roll(two, width, 1))
            out_ref[g, half:, span] = jnp.where(lower, pltpu.roll(one, width, 1), two)


def assemble(pieces, width, kc):
    vmem = pl.BlockSpec(memory_space=pltpu.VMEM)
    n, targets, pair = pieces.shape
    return pl.pallas_call(
        assemble_kernel,
        out_shape=jax.ShapeDtypeStruct((NC, width, kc * width), jnp.float32),
        in_specs=[vmem],
        out_specs=vmem,
        scratch_shapes=[pltpu.VMEM((n * targets, pair), jnp.float32)],
        name="assemble",
    )(pieces)


def coarse_kernel(
    cols, words, a_hbm, p_hbm, halo_hbm, out_ref, a_v, ext_v, g_v, pt_v, acc, items, sems
):
    rows, width, span = a_v.shape
    ka = span // width
    kp = ext_v.shape[2] // width
    nslots, _, outspan = out_ref.shape
    kc = outspan // width
    pair = 2 * width
    copies = load_operands(a_hbm, p_hbm, halo_hbm, a_v, ext_v, sems)
    for copy in copies:
        copy.start()
    clear_rows(acc, width, 0, acc.shape[0] // width)

    last = words.shape[0] * 128 - 1
    first = words[words.shape[0] - 1, 0]

    def more(state):
        return state[0] != last

    def take(state):
        at, count = state
        word = words[lax.shift_right_logical(at, 7), at & 127]
        items[count] = words[lax.shift_right_logical(at, 7), (at & 127) + rows] + (word & 511)
        return (lax.shift_right_logical(word, 9), count + 1)

    _, count = lax.while_loop(more, take, (first, 0))
    for u in range(UNROLL):
        items[count + u] = nslots * kc
    for copy in copies:
        copy.wait()
    all_products(cols, a_v, ext_v, g_v, pt_v)
    add_items(count, items, pt_v, g_v, acc, width, ka, kp)
    lower = lax.broadcasted_iota(jnp.int32, (width, pair), 1) < width

    def finish(t, unused):
        for h in range(kc // 2):
            one = acc[pl.ds(pl.multiple_of((t * kc + 2 * h) * width, width), width), :]
            two = acc[pl.ds(pl.multiple_of((t * kc + 2 * h + 1) * width, width), width), :]
            one = one + pltpu.roll(one, width, 1)
            two = two + pltpu.roll(two, width, 1)
            out_ref[t, :, h * pair : (h + 1) * pair] = jnp.where(lower, one, two).astype(jnp.bfloat16)
        return unused

    lax.fori_loop(0, nslots, finish, 0)


def coarse_partials(cols, words, a_blocks, p_blocks, halo, nslots, kc):
    rows, width, span = a_blocks.shape
    kp = p_blocks.shape[2] // width
    ka = span // width
    extended = rows + halo.shape[0]
    smem = pl.BlockSpec(memory_space=pltpu.SMEM)
    hbm = pl.BlockSpec(memory_space=pl.ANY)
    vmem = pl.BlockSpec(memory_space=pltpu.VMEM)
    return pl.pallas_call(
        coarse_kernel,
        out_shape=jax.ShapeDtypeStruct((nslots, width, kc * width), jnp.bfloat16),
        in_specs=[smem, smem, hbm, hbm, hbm],
        out_specs=pl.BlockSpec(memory_space=pltpu.VMEM),
        scratch_shapes=[
            pltpu.VMEM((rows, width, span), jnp.bfloat16),
            pltpu.VMEM((extended, width, kp * width), jnp.bfloat16),
            pltpu.VMEM((rows * ka * (kp // 2), width, 2 * width), jnp.bfloat16),
            pltpu.VMEM((rows * kp, width, width), jnp.bfloat16),
            pltpu.VMEM(((nslots * kc + 1) * width, 2 * width), jnp.float32),
            pltpu.SMEM((rows * kp * ka * kp + UNROLL,), jnp.int32),
            pltpu.SemaphoreType.DMA((3,)),
        ],
        compiler_params=pltpu.CompilerParams(vmem_limit_bytes=56 * 2**20),
        name="coarse_partials",
    )(cols, words, a_blocks, p_blocks, halo)


def sum_kernel(ids, parts, out_ref):
    out_ref[...] = jnp.zeros_like(out_ref)

    def one(n, unused):
        row = ids[n]

        @pl.when(row >= 0)
        def _():
            out_ref[row] = out_ref[row] + parts[n].astype(jnp.float32)

        return unused

    lax.fori_loop(0, parts.shape[0], one, 0)


def sum_parts(ids, parts):
    return pl.pallas_call(
        sum_kernel,
        out_shape=jax.ShapeDtypeStruct((NC,) + parts.shape[1:], jnp.float32),
        in_specs=[pl.BlockSpec(memory_space=pltpu.SMEM), pl.BlockSpec(memory_space=pltpu.VMEM)],
        out_specs=pl.BlockSpec(memory_space=pltpu.VMEM),
        compiler_params=pltpu.CompilerParams(vmem_limit_bytes=32 * 2**20),
        name="sum_parts",
    )(ids, parts)


def per_device(a_blocks, p_blocks, a_cols, p_slots, touched, touch_cols, halo_rows):
    nrow = lax.axis_size("row")
    cap = touched.shape[2]
    slots = touched.shape[1] * cap
    kc = touch_cols.shape[3]
    table = touched.transpose(0, 2, 1)
    patterns = touch_cols.transpose(0, 2, 3, 1)
    columns = a_cols.T
    halo, words = exchange_halo(halo_rows, table, patterns, columns, p_slots.T, p_blocks)
    halo = halo.reshape((-1,) + halo.shape[2:])
    width = a_blocks.shape[1]
    packed, ids = packed_partials(columns, words, table, a_blocks, p_blocks, halo, kc)
    pieces, counts = reduce_parts(packed, ids.reshape(1, 1, IDS), NC * kc)

    def whole(unused):
        partial = coarse_partials(columns, words, a_blocks, p_blocks, halo, slots, kc)
        parts = lax.all_to_all(partial.reshape(nrow, cap * width, kc * width), "row", 0, 0)
        owners = lax.all_to_all(touched[0], "row", 0, 0)
        return sum_parts(owners.reshape(-1), parts.reshape(slots, width, kc * width))

    return lax.cond(counts[0, 0] > BLOCKS, whole, lambda unused: assemble(pieces, width, kc), 0)


def solution(mesh):
    in_specs = (
        P(("slab", "row"), None, None),
        P(("slab", "row"), None, None),
        P(("slab", "row"), None),
        P(("slab", "row"), None),
        P(("slab", "row"), None, None),
        P(("slab", "row"), None, None, None),
        P(("slab", "row"), None, None),
    )
    out_specs = P(("slab", "row"), None, None)
    return jax.shard_map(per_device, mesh=mesh, in_specs=in_specs, out_specs=out_specs, check_vma=False)
```

```python
import functools

import jax
import jax.numpy as jnp
from jax import lax
from jax.experimental import pallas as pl
from jax.experimental.pallas import tpu as pltpu
from jax.sharding import PartitionSpec as P

NC = 4
UNROLL = 64
BLOCKS = 128
IDS = 256


def load_operands(a_hbm, p_hbm, halo_hbm, a_v, ext_v, sems):
    rows = p_hbm.shape[0]
    return (
        pltpu.make_async_copy(a_hbm, a_v, sems.at[0]),
        pltpu.make_async_copy(p_hbm, ext_v.at[pl.ds(0, rows)], sems.at[1]),
        pltpu.make_async_copy(halo_hbm, ext_v.at[pl.ds(rows, halo_hbm.shape[0])], sems.at[2]),
    )


def all_products(cols, a_v, ext_v, g_v, pt_v):
    rows, width, span = a_v.shape
    ka = span // width
    pairs = ext_v.shape[2] // (2 * width)
    pair = 2 * width

    def products(i, unused):
        row = a_v[i]
        turned = ext_v[i].T
        for m in range(2 * pairs):
            pt_v[i * 2 * pairs + m] = turned[m * width : (m + 1) * width, :]
        for k in range(ka):
            right = ext_v[cols[k, i]]
            value = jnp.dot(row[:, k * width : (k + 1) * width], right, preferred_element_type=jnp.float32).astype(
                jnp.bfloat16
            )
            for h in range(pairs):
                g_v[(i * ka + k) * pairs + h] = value[:, h * pair : (h + 1) * pair]
        return unused

    lax.fori_loop(0, rows, products, 0, unroll=8)


def add_items(count, items, pt_v, g_v, acc, width, ka, kp):
    pair = 2 * width
    upper = (lax.broadcasted_iota(jnp.int32, (width, pair), 1) >= width).astype(jnp.int32)

    def batch(b, unused):
        found = []
        for u in range(UNROLL):
            word = items[b * UNROLL + u]
            target = word & 1023
            g = g_v[lax.shift_right_logical(word, 11) & 1023]
            g = jnp.where(upper == (lax.shift_right_logical(word, 10) & 1), g, jnp.zeros_like(g))
            z = jnp.dot(pt_v[lax.shift_right_logical(word, 21)], g, preferred_element_type=jnp.float32)
            found.append((pl.ds(pl.multiple_of(target * width, width), width), z))
        for where, z in found:
            acc[where, :] = acc[where, :] + z
        return unused

    lax.fori_loop(0, lax.div(count + UNROLL - 1, UNROLL), batch, 0)


def clear_rows(acc, step, first, last):
    def clear(n, unused):
        acc[pl.ds(pl.multiple_of(n * step, step), step), :] = jnp.zeros((step, acc.shape[1]), jnp.float32)
        return unused

    lax.fori_loop(first, last, clear, 0)


def link_matches(cols_v, slots_v, own_ids, halo_ids, edges, patterns, at_v, follow_v, place_v):
    ka, rows = cols_v.shape
    kp = slots_v.shape[0]
    _, cap, kc, owners = patterns.shape
    sides, depth = halo_ids.shape[0], rows // 8
    end = at_v.shape[0] * 128 - 1
    cols = cols_v[...]
    reached = [jnp.full((ka, rows), -2, jnp.int32)] * kp
    for c in range(rows):
        hit = cols == c
        reached = [jnp.where(hit, own_ids[q, c], reached[q]) for q in range(kp)]
    for x in range(sides):
        for d in range(depth):
            hit = cols == rows + x * depth + d
            reached = [
                jnp.where(hit, jnp.where(edges[x], -1, halo_ids[x, 0, d * kp + q]), reached[q]) for q in range(kp)
            ]
    slots = slots_v[...]
    wanted = [jnp.full((kp, rows), -3, jnp.int32)] * kc
    for p in range(owners):
        for c in range(cap):
            hit = slots == p * cap + c
            wanted = [jnp.where(hit, patterns[0, c, j, p], wanted[j]) for j in range(kc)]
    at_v[...] = jnp.full(at_v.shape, end, jnp.int32)
    follow_v[...] = jnp.full(follow_v.shape, end, jnp.int32)
    place_v[...] = jnp.zeros(place_v.shape, jnp.int32)
    which = lax.broadcasted_iota(jnp.int32, (ka, rows), 0) * 128 + lax.broadcasted_iota(jnp.int32, (ka, rows), 1)
    for m in range(kp):
        for q in range(kp):
            place = jnp.full((ka, rows), -1, jnp.int32)
            for j in range(kc):
                place = jnp.where(reached[q] == wanted[j][m : m + 1, :], j, place)
            row = (m * kp + q) * 8
            at_v[row : row + ka, :rows] = jnp.where(place >= 0, which + row * 128, end)
            place_v[row : row + ka, :rows] = slots[m : m + 1, :] * kc + place
    run = jnp.full((1, 128), end, jnp.int32)
    for row in reversed(range(kp * kp * 8)):
        if row % 8 < ka:
            now = at_v[row : row + 1, :]
            follow_v[row : row + 1, :] = run
            run = jnp.minimum(run, now)
    lane = lax.broadcasted_iota(jnp.int32, (8, 128), 1)
    key = jnp.where(run == end, 128 * (end + 1) + end, lane * (end + 1) + run)
    beyond = pltpu.roll(key, 127, 1)
    for step in (1, 2, 4, 8, 16, 32):
        beyond = jnp.minimum(beyond, pltpu.roll(beyond, 128 - step, 1))
    beyond = (beyond & end)[:1, :]
    follow = follow_v[...]
    kinds = lax.broadcasted_iota(jnp.int32, at_v.shape, 0)
    spots = lax.broadcasted_iota(jnp.int32, at_v.shape, 1) - rows
    k = kinds & 7
    q = lax.shift_right_logical(kinds, 3) & (kp - 1)
    m = lax.shift_right_logical(kinds, 2 + kp.bit_length())
    info = ((spots * kp + m) * 1024 + (spots * ka + k) * (kp // 2) + lax.shift_right_logical(q, 1)) * 2 + (q & 1)
    links = jnp.where(follow == end, beyond, follow) * 512 + place_v[...]
    at_v[...] = jnp.where(spots < 0, links, info * 1024)
    start = jnp.min(key[:1], axis=1, keepdims=True) & end
    at_v[at_v.shape[0] - 1 :, :] = jnp.broadcast_to(start, (1, 128))


def packed_kernel(
    cols, words, table, a_hbm, p_hbm, halo_hbm, out_ref, ids_ref, a_v, ext_v, g_v, pt_v, acc, items, index, bases, sems
):
    rows, width, span = a_v.shape
    ka = span // width
    kp = ext_v.shape[2] // width
    pair = 2 * width
    half = width // 2
    kc = index.shape[0] // bases.shape[0]
    copies = load_operands(a_hbm, p_hbm, halo_hbm, a_v, ext_v, sems)
    for copy in copies:
        copy.start()

    for p in range(table.shape[2]):
        for c in range(table.shape[1]):
            bases[p * table.shape[1] + c] = (p * NC + table[0, c, p]) * kc

    def unset(n, unused):
        for u in range(8):
            index[n * 8 + u] = -1
        return unused

    lax.fori_loop(0, index.shape[0] // 8, unset, 0)

    def no_id(n, unused):
        for u in range(8):
            ids_ref[0, n * 8 + u] = -1
        return unused

    lax.fori_loop(0, ids_ref.shape[1] // 8, no_id, 0)

    last = words.shape[0] - 1
    first = words[words.shape[0] - 128]

    def more(state):
        return state[0] != last

    def take(state):
        at, count, blocks = state
        word = words[at]
        place = word & 511
        old = index[place]
        fresh = old < 0
        block = jnp.where(fresh, blocks, old)
        index[place] = block
        kept = jnp.minimum(block, BLOCKS)
        ids_ref[0, kept] = bases[lax.shift_right_logical(place, 3)] + (place & 7)
        items[count] = words[at + rows] + kept
        return (lax.shift_right_logical(word, 9), count + 1, blocks + fresh.astype(jnp.int32))

    _, count, blocks = lax.while_loop(more, take, (first, 0, 0))
    for u in range(UNROLL):
        items[count + u] = BLOCKS
    ids_ref[0, IDS - 1] = blocks
    full = jnp.minimum(lax.div(blocks + 15, 16), BLOCKS // 16)
    clear_rows(acc, 16 * width, 0, full)
    clear_rows(acc, 16 * width, BLOCKS // 16, BLOCKS // 16 + 1)
    for copy in copies:
        copy.wait()
    all_products(cols, a_v, ext_v, g_v, pt_v)
    add_items(count, items, pt_v, g_v, acc, width, ka, kp)
    lower = lax.broadcasted_iota(jnp.int32, (16, pair), 1) < width

    def finish(n, unused):
        for r in range(half):
            one = acc[pl.ds(n * 16 * width + r, 16, stride=width), :]
            two = acc[pl.ds(n * 16 * width + half + r, 16, stride=width), :]
            one = one + pltpu.roll(one, width, 1)
            two = two + pltpu.roll(two, width, 1)
            out_ref[r, pl.ds(pl.multiple_of(n * 16, 16), 16), :] = jnp.where(lower, one, two).astype(jnp.bfloat16)
        return unused

    def empty(n, unused):
        for r in range(half):
            out_ref[r, pl.ds(pl.multiple_of(n * 16, 16), 16), :] = jnp.zeros((16, pair), jnp.bfloat16)
        return unused

    lax.fori_loop(0, full, finish, 0)
    lax.fori_loop(full, BLOCKS // 16, empty, 0)


def packed_partials(cols, words, table, a_blocks, p_blocks, halo, kc):
    rows, width, span = a_blocks.shape
    kp = p_blocks.shape[2] // width
    ka = span // width
    extended = rows + halo.shape[0]
    nslots = table.shape[1] * table.shape[2]
    smem = pl.BlockSpec(memory_space=pltpu.SMEM)
    vmem = pl.BlockSpec(memory_space=pltpu.VMEM)
    hbm = pl.BlockSpec(memory_space=pl.ANY)
    return pl.pallas_call(
        packed_kernel,
        out_shape=(
            jax.ShapeDtypeStruct((width // 2, BLOCKS, 2 * width), jnp.bfloat16),
            jax.ShapeDtypeStruct((1, IDS), jnp.int32),
        ),
        in_specs=[smem, smem, smem, hbm, hbm, hbm],
        out_specs=(vmem, smem),
        scratch_shapes=[
            pltpu.VMEM((rows, width, span), jnp.bfloat16),
            pltpu.VMEM((extended, width, kp * width), jnp.bfloat16),
            pltpu.VMEM((rows * ka * (kp // 2), width, 2 * width), jnp.bfloat16),
            pltpu.VMEM((rows * kp, width, width), jnp.bfloat16),
            pltpu.VMEM(((BLOCKS + 16) * width, 2 * width), jnp.float32),
            pltpu.SMEM((rows * kp * ka * kp + UNROLL,), jnp.int32),
            pltpu.SMEM((nslots * kc,), jnp.int32),
            pltpu.SMEM((nslots,), jnp.int32),
            pltpu.SemaphoreType.DMA((3,)),
        ],
        compiler_params=pltpu.CompilerParams(vmem_limit_bytes=48 * 2**20),
        name="packed_partials",
    )(cols, words, table, a_blocks, p_blocks, halo)


def halo_kernel(
    rows, table, patterns, cols_v, slots_v, p_ref, out_blocks, words, blocks, own_v, own_ids, ids, came_ids, halo_ids,
    follow_v, place_v, here_sem, send_sem, take_sem
):
    barrier = pltpu.get_barrier_semaphore()
    routes = []
    edges = [None] * 4
    for x, axis, way, chosen in ((2, "row", 1, 3), (3, "row", -1, 2), (0, "slab", 1, 1), (1, "slab", -1, 0)):
        n, at = lax.axis_size(axis), lax.axis_index(axis)
        routes.append((x, {axis: lax.rem(at + way + n, n)}, chosen))
        edges[x] = at == (0 if way == 1 else n - 1)
    for _, to, _ in routes:
        pl.semaphore_signal(barrier, inc=1, device_id=to, device_id_type=pl.DeviceIdType.MESH)
    for x in (3, 2, 1, 0):
        for h in range(blocks.shape[1]):
            blocks[x, h] = p_ref[rows[0, x, h]]
    pl.semaphore_wait(barrier, len(routes))

    def send(z, slot, to, chosen):
        src, dst = ((ids, came_ids), (blocks, out_blocks))[z]
        return pltpu.make_async_remote_copy(
            src_ref=src.at[chosen],
            dst_ref=dst.at[slot],
            send_sem=send_sem.at[z, slot],
            recv_sem=take_sem.at[z, slot],
            device_id=to,
            device_id_type=pl.DeviceIdType.MESH,
        )

    for slot, to, chosen in routes:
        send(1, slot, to, chosen).start()
    slots = slots_v[...]
    kp, cap = slots.shape[0], table.shape[1]
    local = jnp.zeros_like(slots)
    for p in range(table.shape[2]):
        for c in range(cap):
            local = jnp.where(slots == p * cap + c, table[0, c, p], local)
    owner = lax.axis_index("slab") * lax.axis_size("row") + lax.div(slots, cap)
    own_v[...] = jnp.zeros(own_v.shape, jnp.int32)
    own_v[:kp, : slots.shape[1]] = owner * NC + local
    here = pltpu.make_async_copy(own_v, own_ids, here_sem.at[1])
    here.start()
    here.wait()
    lane = lax.broadcasted_iota(jnp.int32, (1, 128), 1)
    for x in range(rows.shape[1]):
        listed = jnp.zeros((1, 128), jnp.int32)
        for d in range(rows.shape[2]):
            at = rows[0, x, d]
            for m in range(kp):
                listed = jnp.where(lane == d * kp + m, own_ids[m, at], listed)
        ids[x] = listed
    for slot, to, chosen in routes:
        send(0, slot, to, chosen).start()
    for slot, to, chosen in routes:
        send(0, slot, to, chosen).wait()
    here = pltpu.make_async_copy(came_ids, halo_ids, here_sem.at[0])
    here.start()
    here.wait()
    link_matches(cols_v, slots_v, own_ids, halo_ids, edges, patterns, words, follow_v, place_v)
    for slot, to, chosen in routes:
        send(1, slot, to, chosen).wait()


def exchange_halo(rows, table, patterns, cols, slots, p_blocks):
    vmem = pl.BlockSpec(memory_space=pltpu.VMEM)
    smem = pl.BlockSpec(memory_space=pltpu.SMEM)
    hbm = pl.BlockSpec(memory_space=pl.ANY)
    shape = rows.shape[1:] + p_blocks.shape[1:]
    kp = slots.shape[0]
    linked = (kp * kp * 8, 128)
    return pl.pallas_call(
        halo_kernel,
        out_shape=(jax.ShapeDtypeStruct(shape, p_blocks.dtype), jax.ShapeDtypeStruct(linked, jnp.int32)),
        in_specs=[smem, smem, smem, vmem, vmem, vmem],
        out_specs=(hbm, vmem),
        scratch_shapes=[
            pltpu.VMEM(shape, p_blocks.dtype),
            pltpu.VMEM((8, 128), jnp.int32),
            pltpu.SMEM((8, 128), jnp.int32),
            pltpu.VMEM((4, 1, 128), jnp.int32),
            pltpu.VMEM((4, 1, 128), jnp.int32),
            pltpu.SMEM((4, 1, 128), jnp.int32),
            pltpu.VMEM(linked, jnp.int32),
            pltpu.VMEM(linked, jnp.int32),
            pltpu.SemaphoreType.DMA((2,)),
            pltpu.SemaphoreType.DMA((2, 4)),
            pltpu.SemaphoreType.DMA((2, 4)),
        ],
        compiler_params=pltpu.CompilerParams(collective_id=1, has_side_effects=True, vmem_limit_bytes=60 * 2**20),
        name="exchange_halo",
    )(rows, table, patterns, cols, slots, p_blocks)


def reduce_kernel(
    parts, ids, pieces, most_ref, came_parts, came_ids, sums, flag, came_flags, acc, send_sem, take_sem, flag_send, flag_take
):
    row, slab = lax.axis_index("row"), lax.axis_index("slab")
    n, slabs = lax.axis_size("row"), lax.axis_size("slab")
    blocks = parts.shape[1]
    targets, lanes = acc.shape
    share = targets // n
    barrier = pltpu.get_barrier_semaphore()
    mesh_id = pl.DeviceIdType.MESH

    def greet_row(o, unused):
        pl.semaphore_signal(barrier, inc=1, device_id={"row": lax.rem(row + o, n)}, device_id_type=mesh_id)
        return unused

    def greet_slab(o, unused):
        pl.semaphore_signal(barrier, inc=1, device_id={"slab": lax.rem(slab + o, slabs)}, device_id_type=mesh_id)
        return unused

    lax.fori_loop(1, n, greet_row, 0)
    lax.fori_loop(1, slabs, greet_slab, 0)
    pl.semaphore_wait(barrier, n + slabs - 2)

    def row_copy(x, o, src, dst, other):
        return pltpu.make_async_remote_copy(
            src_ref=src,
            dst_ref=dst,
            send_sem=send_sem.at[x, o],
            recv_sem=take_sem.at[x, o],
            device_id={"row": other},
            device_id_type=mesh_id,
        )

    def to_of(o):
        return lax.rem(row + o, n)

    def from_of(o):
        return lax.rem(row + n - o, n)

    def begin(o, unused):
        to = to_of(o)
        row_copy(0, o, ids.at[0], came_ids.at[row], to).start()
        row_copy(1, o, parts.at[to], came_parts.at[row], to).start()
        return unused

    lax.fori_loop(1, n, begin, 0)
    order = lax.broadcasted_iota(jnp.int32, (targets, blocks), 0)

    def spread(names, values):
        hot = jnp.where(order == names[:, :blocks], 1.0, 0.0).astype(jnp.bfloat16)
        return jnp.dot(hot, values, preferred_element_type=jnp.float32)

    own = ids[0]
    acc[...] = spread(own, parts[row])
    last = lax.broadcasted_iota(jnp.int32, own.shape, 1) == own.shape[1] - 1

    def add(o, most):
        came = from_of(o)
        row_copy(0, o, ids.at[0], came_ids.at[came], came).wait_recv()
        row_copy(1, o, parts.at[came], came_parts.at[came], came).wait_recv()
        names = came_ids[came]
        acc[...] += spread(names, came_parts[came])
        return jnp.maximum(most, names)

    most = lax.fori_loop(1, n, add, own)
    flag[...] = jnp.where(last, most, 0)

    def flag_copy(o, at, other):
        return pltpu.make_async_remote_copy(
            src_ref=flag,
            dst_ref=came_flags.at[at],
            send_sem=flag_send.at[o],
            recv_sem=flag_take.at[o],
            device_id={"slab": other},
            device_id_type=mesh_id,
        )

    def begin_flag(o, unused):
        flag_copy(o, slab, lax.rem(slab + o, slabs)).start()
        return unused

    lax.fori_loop(1, slabs, begin_flag, 0)
    for p in range(n):
        sums[p] = acc[p * share : (p + 1) * share, :].astype(jnp.bfloat16)

    def begin_sums(o, unused):
        to = to_of(o)
        row_copy(2, o, sums.at[to], pieces.at[row], to).start()
        return unused

    lax.fori_loop(1, n, begin_sums, 0)
    pieces[row] = sums[row]

    def end_flag(o, most):
        came = lax.rem(slab + slabs - o, slabs)
        flag_copy(o, slab, lax.rem(slab + o, slabs)).wait_send()
        flag_copy(o, came, came).wait_recv()
        return jnp.maximum(most, came_flags[came])

    most_ref[0, 0] = jnp.max(lax.fori_loop(1, slabs, end_flag, flag[...]))

    def end(o, unused):
        to, came = to_of(o), from_of(o)
        row_copy(0, o, ids.at[0], came_ids.at[row], to).wait_send()
        row_copy(1, o, parts.at[to], came_parts.at[row], to).wait_send()
        row_copy(2, o, sums.at[to], pieces.at[row], to).wait_send()
        row_copy(2, o, sums.at[came], pieces.at[came], came).wait_recv()
        return unused

    lax.fori_loop(1, n, end, 0)


def reduce_parts(parts, ids, share):
    n, slabs = lax.axis_size("row"), lax.axis_size("slab")
    _, blocks, lanes = parts.shape
    vmem = pl.BlockSpec(memory_space=pltpu.VMEM)
    return pl.pallas_call(
        reduce_kernel,
        out_shape=(
            jax.ShapeDtypeStruct((n, share, lanes), jnp.bfloat16),
            jax.ShapeDtypeStruct((1, 1), jnp.int32),
        ),
        in_specs=[vmem, vmem],
        out_specs=(vmem, pl.BlockSpec(memory_space=pltpu.SMEM)),
        scratch_shapes=[
            pltpu.VMEM((n, blocks, lanes), jnp.bfloat16),
            pltpu.VMEM((n, 1, IDS), jnp.int32),
            pltpu.VMEM((n, share, lanes), jnp.bfloat16),
            pltpu.VMEM((1, IDS), jnp.int32),
            pltpu.VMEM((slabs, 1, IDS), jnp.int32),
            pltpu.VMEM((n * share, lanes), jnp.float32),
            pltpu.SemaphoreType.DMA((3, n)),
            pltpu.SemaphoreType.DMA((3, n)),
            pltpu.SemaphoreType.DMA((slabs,)),
            pltpu.SemaphoreType.DMA((slabs,)),
        ],
        compiler_params=pltpu.CompilerParams(
            collective_id=0, has_side_effects=True, vmem_limit_bytes=32 * 2**20
        ),
        name="reduce_parts",
    )(parts, ids)


def assemble_kernel(pieces_ref, out_ref, wide):
    n, targets, pair = pieces_ref.shape
    owned, width, outspan = out_ref.shape
    half = width // 2
    kc = targets // owned
    lower = lax.broadcasted_iota(jnp.int32, (half, pair), 1) < half * 2
    wide[...] = pieces_ref[...].reshape(n * targets, pair).astype(jnp.float32)
    for g in range(owned):
        for h in range(kc // 2):
            one = wide[pl.ds(g * kc + 2 * h, n, stride=targets), :]
            two = wide[pl.ds(g * kc + 2 * h + 1, n, stride=targets), :]
            span = slice(h * pair, (h + 1) * pair)
            out_ref[g, :half, span] = jnp.where(lower, one, pltpu.roll(two, width, 1))
            out_ref[g, half:, span] = jnp.where(lower, pltpu.roll(one, width, 1), two)


def assemble(pieces, width, kc):
    vmem = pl.BlockSpec(memory_space=pltpu.VMEM)
    n, targets, pair = pieces.shape
    return pl.pallas_call(
        assemble_kernel,
        out_shape=jax.ShapeDtypeStruct((NC, width, kc * width), jnp.float32),
        in_specs=[vmem],
        out_specs=vmem,
        scratch_shapes=[pltpu.VMEM((n * targets, pair), jnp.float32)],
        name="assemble",
    )(pieces)


def coarse_kernel(
    cols, words, a_hbm, p_hbm, halo_hbm, out_ref, a_v, ext_v, g_v, pt_v, acc, items, sems
):
    rows, width, span = a_v.shape
    ka = span // width
    kp = ext_v.shape[2] // width
    nslots, _, outspan = out_ref.shape
    kc = outspan // width
    pair = 2 * width
    copies = load_operands(a_hbm, p_hbm, halo_hbm, a_v, ext_v, sems)
    for copy in copies:
        copy.start()
    clear_rows(acc, width, 0, acc.shape[0] // width)

    last = words.shape[0] - 1
    first = words[words.shape[0] - 128]

    def more(state):
        return state[0] != last

    def take(state):
        at, count = state
        word = words[at]
        items[count] = words[at + rows] + (word & 511)
        return (lax.shift_right_logical(word, 9), count + 1)

    _, count = lax.while_loop(more, take, (first, 0))
    for u in range(UNROLL):
        items[count + u] = nslots * kc
    for copy in copies:
        copy.wait()
    all_products(cols, a_v, ext_v, g_v, pt_v)
    add_items(count, items, pt_v, g_v, acc, width, ka, kp)
    lower = lax.broadcasted_iota(jnp.int32, (width, pair), 1) < width

    def finish(t, unused):
        for h in range(kc // 2):
            one = acc[pl.ds(pl.multiple_of((t * kc + 2 * h) * width, width), width), :]
            two = acc[pl.ds(pl.multiple_of((t * kc + 2 * h + 1) * width, width), width), :]
            one = one + pltpu.roll(one, width, 1)
            two = two + pltpu.roll(two, width, 1)
            out_ref[t, :, h * pair : (h + 1) * pair] = jnp.where(lower, one, two).astype(jnp.bfloat16)
        return unused

    lax.fori_loop(0, nslots, finish, 0)


def coarse_partials(cols, words, a_blocks, p_blocks, halo, nslots, kc):
    rows, width, span = a_blocks.shape
    kp = p_blocks.shape[2] // width
    ka = span // width
    extended = rows + halo.shape[0]
    smem = pl.BlockSpec(memory_space=pltpu.SMEM)
    hbm = pl.BlockSpec(memory_space=pl.ANY)
    vmem = pl.BlockSpec(memory_space=pltpu.VMEM)
    return pl.pallas_call(
        coarse_kernel,
        out_shape=jax.ShapeDtypeStruct((nslots, width, kc * width), jnp.bfloat16),
        in_specs=[smem, smem, hbm, hbm, hbm],
        out_specs=pl.BlockSpec(memory_space=pltpu.VMEM),
        scratch_shapes=[
            pltpu.VMEM((rows, width, span), jnp.bfloat16),
            pltpu.VMEM((extended, width, kp * width), jnp.bfloat16),
            pltpu.VMEM((rows * ka * (kp // 2), width, 2 * width), jnp.bfloat16),
            pltpu.VMEM((rows * kp, width, width), jnp.bfloat16),
            pltpu.VMEM(((nslots * kc + 1) * width, 2 * width), jnp.float32),
            pltpu.SMEM((rows * kp * ka * kp + UNROLL,), jnp.int32),
            pltpu.SemaphoreType.DMA((3,)),
        ],
        compiler_params=pltpu.CompilerParams(vmem_limit_bytes=56 * 2**20),
        name="coarse_partials",
    )(cols, words, a_blocks, p_blocks, halo)


def sum_kernel(ids, parts, out_ref):
    out_ref[...] = jnp.zeros_like(out_ref)

    def one(n, unused):
        row = ids[n]

        @pl.when(row >= 0)
        def _():
            out_ref[row] = out_ref[row] + parts[n].astype(jnp.float32)

        return unused

    lax.fori_loop(0, parts.shape[0], one, 0)


def sum_parts(ids, parts):
    return pl.pallas_call(
        sum_kernel,
        out_shape=jax.ShapeDtypeStruct((NC,) + parts.shape[1:], jnp.float32),
        in_specs=[pl.BlockSpec(memory_space=pltpu.SMEM), pl.BlockSpec(memory_space=pltpu.VMEM)],
        out_specs=pl.BlockSpec(memory_space=pltpu.VMEM),
        compiler_params=pltpu.CompilerParams(vmem_limit_bytes=32 * 2**20),
        name="sum_parts",
    )(ids, parts)


def per_device(a_blocks, p_blocks, a_cols, p_slots, touched, touch_cols, halo_rows):
    nrow = lax.axis_size("row")
    cap = touched.shape[2]
    slots = touched.shape[1] * cap
    kc = touch_cols.shape[3]
    table = touched.transpose(0, 2, 1)
    patterns = touch_cols.transpose(0, 2, 3, 1)
    columns = a_cols.T
    halo, words = exchange_halo(halo_rows, table, patterns, columns, p_slots.T, p_blocks)
    halo = halo.reshape((-1,) + halo.shape[2:])
    words = words.reshape(-1)
    width = a_blocks.shape[1]
    packed, ids = packed_partials(columns, words, table, a_blocks, p_blocks, halo, kc)
    pieces, counts = reduce_parts(packed, ids.reshape(1, 1, IDS), NC * kc)

    def whole(unused):
        partial = coarse_partials(columns, words, a_blocks, p_blocks, halo, slots, kc)
        parts = lax.all_to_all(partial.reshape(nrow, cap * width, kc * width), "row", 0, 0)
        owners = lax.all_to_all(touched[0], "row", 0, 0)
        return sum_parts(owners.reshape(-1), parts.reshape(slots, width, kc * width))

    return lax.cond(counts[0, 0] > BLOCKS, whole, lambda unused: assemble(pieces, width, kc), 0)


def solution(mesh):
    in_specs = (
        P(("slab", "row"), None, None),
        P(("slab", "row"), None, None),
        P(("slab", "row"), None),
        P(("slab", "row"), None),
        P(("slab", "row"), None, None),
        P(("slab", "row"), None, None, None),
        P(("slab", "row"), None, None),
    )
    out_specs = P(("slab", "row"), None, None)
    return jax.shard_map(per_device, mesh=mesh, in_specs=in_specs, out_specs=out_specs, check_vma=False)
```

```python
import functools

import jax
import jax.numpy as jnp
from jax import lax
from jax.experimental import pallas as pl
from jax.experimental.pallas import tpu as pltpu
from jax.sharding import PartitionSpec as P

NC = 4
UNROLL = 64
BLOCKS = 128
IDS = 256


def load_operands(a_hbm, p_hbm, halo_hbm, a_v, ext_v, sems):
    rows = p_hbm.shape[0]
    return (
        pltpu.make_async_copy(a_hbm, a_v, sems.at[0]),
        pltpu.make_async_copy(p_hbm, ext_v.at[pl.ds(0, rows)], sems.at[1]),
        pltpu.make_async_copy(halo_hbm, ext_v.at[pl.ds(rows, halo_hbm.shape[0])], sems.at[2]),
    )


def all_products(cols, a_v, ext_v, g_v, pt_v):
    rows, width, span = a_v.shape
    ka = span // width
    pairs = ext_v.shape[2] // (2 * width)
    pair = 2 * width

    def products(i, unused):
        row = a_v[i]
        turned = ext_v[i].T
        for m in range(2 * pairs):
            pt_v[i * 2 * pairs + m] = turned[m * width : (m + 1) * width, :]
        for k in range(ka):
            right = ext_v[cols[k, i]]
            value = jnp.dot(row[:, k * width : (k + 1) * width], right, preferred_element_type=jnp.float32).astype(
                jnp.bfloat16
            )
            for h in range(pairs):
                g_v[(i * ka + k) * pairs + h] = value[:, h * pair : (h + 1) * pair]
        return unused

    lax.fori_loop(0, rows, products, 0, unroll=16)


def add_items(count, items, pt_v, g_v, acc, width, ka, kp):
    pair = 2 * width
    upper = (lax.broadcasted_iota(jnp.int32, (width, pair), 1) >= width).astype(jnp.int32)

    def batch(b, unused):
        found = []
        for u in range(UNROLL):
            word = items[b * UNROLL + u]
            target = word & 1023
            g = g_v[lax.shift_right_logical(word, 11) & 1023]
            g = jnp.where(upper == (lax.shift_right_logical(word, 10) & 1), g, jnp.zeros_like(g))
            z = jnp.dot(pt_v[lax.shift_right_logical(word, 21)], g, preferred_element_type=jnp.float32)
            found.append((pl.ds(pl.multiple_of(target * width, width), width), z))
        for where, z in found:
            acc[where, :] = acc[where, :] + z
        return unused

    lax.fori_loop(0, lax.div(count + UNROLL - 1, UNROLL), batch, 0)


def clear_rows(acc, step, first, last):
    def clear(n, unused):
        acc[pl.ds(pl.multiple_of(n * step, step), step), :] = jnp.zeros((step, acc.shape[1]), jnp.float32)
        return unused

    lax.fori_loop(first, last, clear, 0)


def link_matches(cols_v, slots_v, own_ids, halo_ids, edges, patterns, at_v, follow_v, place_v):
    ka, rows = cols_v.shape
    kp = slots_v.shape[0]
    _, cap, kc, owners = patterns.shape
    sides, depth = halo_ids.shape[0], rows // 8
    end = at_v.shape[0] * 128 - 1
    cols = cols_v[...]
    reached = [jnp.full((ka, rows), -2, jnp.int32)] * kp
    for c in range(rows):
        hit = cols == c
        reached = [jnp.where(hit, own_ids[q, c], reached[q]) for q in range(kp)]
    for x in range(sides):
        for d in range(depth):
            hit = cols == rows + x * depth + d
            reached = [
                jnp.where(hit, jnp.where(edges[x], -1, halo_ids[x, 0, d * kp + q]), reached[q]) for q in range(kp)
            ]
    slots = slots_v[...]
    wanted = [jnp.full((kp, rows), -3, jnp.int32)] * kc
    for p in range(owners):
        for c in range(cap):
            hit = slots == p * cap + c
            wanted = [jnp.where(hit, patterns[0, c, j, p], wanted[j]) for j in range(kc)]
    at_v[...] = jnp.full(at_v.shape, end, jnp.int32)
    follow_v[...] = jnp.full(follow_v.shape, end, jnp.int32)
    place_v[...] = jnp.zeros(place_v.shape, jnp.int32)
    which = lax.broadcasted_iota(jnp.int32, (ka, rows), 0) * 128 + lax.broadcasted_iota(jnp.int32, (ka, rows), 1)
    for m in range(kp):
        for q in range(kp):
            place = jnp.full((ka, rows), -1, jnp.int32)
            for j in range(kc):
                place = jnp.where(reached[q] == wanted[j][m : m + 1, :], j, place)
            row = (m * kp + q) * 8
            at_v[row : row + ka, :rows] = jnp.where(place >= 0, which + row * 128, end)
            place_v[row : row + ka, :rows] = slots[m : m + 1, :] * kc + place
    run = jnp.full((1, 128), end, jnp.int32)
    for row in reversed(range(kp * kp * 8)):
        if row % 8 < ka:
            now = at_v[row : row + 1, :]
            follow_v[row : row + 1, :] = run
            run = jnp.minimum(run, now)
    lane = lax.broadcasted_iota(jnp.int32, (8, 128), 1)
    key = jnp.where(run == end, 128 * (end + 1) + end, lane * (end + 1) + run)
    beyond = pltpu.roll(key, 127, 1)
    for step in (1, 2, 4, 8, 16, 32):
        beyond = jnp.minimum(beyond, pltpu.roll(beyond, 128 - step, 1))
    beyond = (beyond & end)[:1, :]
    follow = follow_v[...]
    kinds = lax.broadcasted_iota(jnp.int32, at_v.shape, 0)
    spots = lax.broadcasted_iota(jnp.int32, at_v.shape, 1) - rows
    k = kinds & 7
    q = lax.shift_right_logical(kinds, 3) & (kp - 1)
    m = lax.shift_right_logical(kinds, 2 + kp.bit_length())
    info = ((spots * kp + m) * 1024 + (spots * ka + k) * (kp // 2) + lax.shift_right_logical(q, 1)) * 2 + (q & 1)
    links = jnp.where(follow == end, beyond, follow) * 512 + place_v[...]
    at_v[...] = jnp.where(spots < 0, links, info * 1024)
    start = jnp.min(key[:1], axis=1, keepdims=True) & end
    at_v[at_v.shape[0] - 1 :, :] = jnp.broadcast_to(start, (1, 128))


def packed_kernel(
    cols, words, table, a_hbm, p_hbm, halo_hbm, out_ref, ids_ref, a_v, ext_v, g_v, pt_v, acc, items, index, bases, sems
):
    rows, width, span = a_v.shape
    ka = span // width
    kp = ext_v.shape[2] // width
    pair = 2 * width
    half = width // 2
    kc = index.shape[0] // bases.shape[0]
    copies = load_operands(a_hbm, p_hbm, halo_hbm, a_v, ext_v, sems)
    for copy in copies:
        copy.start()

    for p in range(table.shape[2]):
        for c in range(table.shape[1]):
            bases[p * table.shape[1] + c] = (p * NC + table[0, c, p]) * kc

    def unset(n, unused):
        for u in range(8):
            index[n * 8 + u] = -1
        return unused

    lax.fori_loop(0, index.shape[0] // 8, unset, 0)

    def no_id(n, unused):
        for u in range(8):
            ids_ref[0, n * 8 + u] = -1
        return unused

    lax.fori_loop(0, ids_ref.shape[1] // 8, no_id, 0)

    last = words.shape[0] - 1
    first = words[words.shape[0] - 128]

    def more(state):
        return state[0] != last

    def take(state):
        at, count, blocks = state
        word = words[at]
        place = word & 511
        old = index[place]
        fresh = old < 0
        block = jnp.where(fresh, blocks, old)
        index[place] = block
        kept = jnp.minimum(block, BLOCKS)
        ids_ref[0, kept] = bases[lax.shift_right_logical(place, 3)] + (place & 7)
        items[count] = words[at + rows] + kept
        return (lax.shift_right_logical(word, 9), count + 1, blocks + fresh.astype(jnp.int32))

    _, count, blocks = lax.while_loop(more, take, (first, 0, 0))
    for u in range(UNROLL):
        items[count + u] = BLOCKS
    ids_ref[0, IDS - 1] = blocks
    full = jnp.minimum(lax.div(blocks + 15, 16), BLOCKS // 16)
    clear_rows(acc, 16 * width, 0, full)
    clear_rows(acc, 16 * width, BLOCKS // 16, BLOCKS // 16 + 1)
    for copy in copies:
        copy.wait()
    all_products(cols, a_v, ext_v, g_v, pt_v)
    add_items(count, items, pt_v, g_v, acc, width, ka, kp)
    lower = lax.broadcasted_iota(jnp.int32, (16, pair), 1) < width

    def finish(n, unused):
        for r in range(half):
            one = acc[pl.ds(n * 16 * width + r, 16, stride=width), :]
            two = acc[pl.ds(n * 16 * width + half + r, 16, stride=width), :]
            one = one + pltpu.roll(one, width, 1)
            two = two + pltpu.roll(two, width, 1)
            out_ref[r, pl.ds(pl.multiple_of(n * 16, 16), 16), :] = jnp.where(lower, one, two).astype(jnp.bfloat16)
        return unused

    def empty(n, unused):
        for r in range(half):
            out_ref[r, pl.ds(pl.multiple_of(n * 16, 16), 16), :] = jnp.zeros((16, pair), jnp.bfloat16)
        return unused

    lax.fori_loop(0, full, finish, 0)
    lax.fori_loop(full, BLOCKS // 16, empty, 0)


def packed_partials(cols, words, table, a_blocks, p_blocks, halo, kc):
    rows, width, span = a_blocks.shape
    kp = p_blocks.shape[2] // width
    ka = span // width
    extended = rows + halo.shape[0]
    nslots = table.shape[1] * table.shape[2]
    smem = pl.BlockSpec(memory_space=pltpu.SMEM)
    vmem = pl.BlockSpec(memory_space=pltpu.VMEM)
    hbm = pl.BlockSpec(memory_space=pl.ANY)
    return pl.pallas_call(
        packed_kernel,
        out_shape=(
            jax.ShapeDtypeStruct((width // 2, BLOCKS, 2 * width), jnp.bfloat16),
            jax.ShapeDtypeStruct((1, IDS), jnp.int32),
        ),
        in_specs=[smem, smem, smem, hbm, hbm, hbm],
        out_specs=(vmem, smem),
        scratch_shapes=[
            pltpu.VMEM((rows, width, span), jnp.bfloat16),
            pltpu.VMEM((extended, width, kp * width), jnp.bfloat16),
            pltpu.VMEM((rows * ka * (kp // 2), width, 2 * width), jnp.bfloat16),
            pltpu.VMEM((rows * kp, width, width), jnp.bfloat16),
            pltpu.VMEM(((BLOCKS + 16) * width, 2 * width), jnp.float32),
            pltpu.SMEM((rows * kp * ka * kp + UNROLL,), jnp.int32),
            pltpu.SMEM((nslots * kc,), jnp.int32),
            pltpu.SMEM((nslots,), jnp.int32),
            pltpu.SemaphoreType.DMA((3,)),
        ],
        compiler_params=pltpu.CompilerParams(vmem_limit_bytes=48 * 2**20),
        name="packed_partials",
    )(cols, words, table, a_blocks, p_blocks, halo)


def halo_kernel(
    rows, table, patterns, cols_v, slots_v, p_ref, out_blocks, words, blocks, own_v, own_ids, ids, came_ids, halo_ids,
    follow_v, place_v, here_sem, send_sem, take_sem
):
    barrier = pltpu.get_barrier_semaphore()
    routes = []
    edges = [None] * 4
    for x, axis, way, chosen in ((2, "row", 1, 3), (3, "row", -1, 2), (0, "slab", 1, 1), (1, "slab", -1, 0)):
        n, at = lax.axis_size(axis), lax.axis_index(axis)
        routes.append((x, {axis: lax.rem(at + way + n, n)}, chosen))
        edges[x] = at == (0 if way == 1 else n - 1)
    for _, to, _ in routes:
        pl.semaphore_signal(barrier, inc=1, device_id=to, device_id_type=pl.DeviceIdType.MESH)
    for x in (3, 2, 1, 0):
        for h in range(blocks.shape[1]):
            blocks[x, h] = p_ref[rows[0, x, h]]
    pl.semaphore_wait(barrier, len(routes))

    def send(z, slot, to, chosen):
        src, dst = ((ids, came_ids), (blocks, out_blocks))[z]
        return pltpu.make_async_remote_copy(
            src_ref=src.at[chosen],
            dst_ref=dst.at[slot],
            send_sem=send_sem.at[z, slot],
            recv_sem=take_sem.at[z, slot],
            device_id=to,
            device_id_type=pl.DeviceIdType.MESH,
        )

    for slot, to, chosen in routes:
        send(1, slot, to, chosen).start()
    slots = slots_v[...]
    kp, cap = slots.shape[0], table.shape[1]
    local = jnp.zeros_like(slots)
    for p in range(table.shape[2]):
        for c in range(cap):
            local = jnp.where(slots == p * cap + c, table[0, c, p], local)
    owner = lax.axis_index("slab") * lax.axis_size("row") + lax.div(slots, cap)
    own_v[...] = jnp.zeros(own_v.shape, jnp.int32)
    own_v[:kp, : slots.shape[1]] = owner * NC + local
    here = pltpu.make_async_copy(own_v, own_ids, here_sem.at[1])
    here.start()
    here.wait()
    lane = lax.broadcasted_iota(jnp.int32, (1, 128), 1)
    for x in range(rows.shape[1]):
        listed = jnp.zeros((1, 128), jnp.int32)
        for d in range(rows.shape[2]):
            at = rows[0, x, d]
            for m in range(kp):
                listed = jnp.where(lane == d * kp + m, own_ids[m, at], listed)
        ids[x] = listed
    for slot, to, chosen in routes:
        send(0, slot, to, chosen).start()
    for slot, to, chosen in routes:
        send(0, slot, to, chosen).wait()
    here = pltpu.make_async_copy(came_ids, halo_ids, here_sem.at[0])
    here.start()
    here.wait()
    link_matches(cols_v, slots_v, own_ids, halo_ids, edges, patterns, words, follow_v, place_v)
    for slot, to, chosen in routes:
        send(1, slot, to, chosen).wait()


def exchange_halo(rows, table, patterns, cols, slots, p_blocks):
    vmem = pl.BlockSpec(memory_space=pltpu.VMEM)
    smem = pl.BlockSpec(memory_space=pltpu.SMEM)
    hbm = pl.BlockSpec(memory_space=pl.ANY)
    shape = rows.shape[1:] + p_blocks.shape[1:]
    kp = slots.shape[0]
    linked = (kp * kp * 8, 128)
    return pl.pallas_call(
        halo_kernel,
        out_shape=(jax.ShapeDtypeStruct(shape, p_blocks.dtype), jax.ShapeDtypeStruct(linked, jnp.int32)),
        in_specs=[smem, smem, smem, vmem, vmem, vmem],
        out_specs=(hbm, vmem),
        scratch_shapes=[
            pltpu.VMEM(shape, p_blocks.dtype),
            pltpu.VMEM((8, 128), jnp.int32),
            pltpu.SMEM((8, 128), jnp.int32),
            pltpu.VMEM((4, 1, 128), jnp.int32),
            pltpu.VMEM((4, 1, 128), jnp.int32),
            pltpu.SMEM((4, 1, 128), jnp.int32),
            pltpu.VMEM(linked, jnp.int32),
            pltpu.VMEM(linked, jnp.int32),
            pltpu.SemaphoreType.DMA((2,)),
            pltpu.SemaphoreType.DMA((2, 4)),
            pltpu.SemaphoreType.DMA((2, 4)),
        ],
        compiler_params=pltpu.CompilerParams(collective_id=1, has_side_effects=True, vmem_limit_bytes=60 * 2**20),
        name="exchange_halo",
    )(rows, table, patterns, cols, slots, p_blocks)


def reduce_kernel(
    parts, ids, pieces, most_ref, came_parts, came_ids, sums, flag, came_flags, acc, send_sem, take_sem, flag_send, flag_take
):
    row, slab = lax.axis_index("row"), lax.axis_index("slab")
    n, slabs = lax.axis_size("row"), lax.axis_size("slab")
    blocks = parts.shape[1]
    targets, lanes = acc.shape
    share = targets // n
    barrier = pltpu.get_barrier_semaphore()
    mesh_id = pl.DeviceIdType.MESH

    def greet_row(o, unused):
        pl.semaphore_signal(barrier, inc=1, device_id={"row": lax.rem(row + o, n)}, device_id_type=mesh_id)
        return unused

    def greet_slab(o, unused):
        pl.semaphore_signal(barrier, inc=1, device_id={"slab": lax.rem(slab + o, slabs)}, device_id_type=mesh_id)
        return unused

    lax.fori_loop(1, n, greet_row, 0)
    lax.fori_loop(1, slabs, greet_slab, 0)
    pl.semaphore_wait(barrier, n + slabs - 2)

    def row_copy(x, o, src, dst, other):
        return pltpu.make_async_remote_copy(
            src_ref=src,
            dst_ref=dst,
            send_sem=send_sem.at[x, o],
            recv_sem=take_sem.at[x, o],
            device_id={"row": other},
            device_id_type=mesh_id,
        )

    def to_of(o):
        return lax.rem(row + o, n)

    def from_of(o):
        return lax.rem(row + n - o, n)

    def begin(o, unused):
        to = to_of(o)
        row_copy(0, o, ids.at[0], came_ids.at[row], to).start()
        row_copy(1, o, parts.at[to], came_parts.at[row], to).start()
        return unused

    lax.fori_loop(1, n, begin, 0)
    order = lax.broadcasted_iota(jnp.int32, (targets, blocks), 0)

    def spread(names, values):
        hot = jnp.where(order == names[:, :blocks], 1.0, 0.0).astype(jnp.bfloat16)
        return jnp.dot(hot, values, preferred_element_type=jnp.float32)

    own = ids[0]
    acc[...] = spread(own, parts[row])
    last = lax.broadcasted_iota(jnp.int32, own.shape, 1) == own.shape[1] - 1

    def add(o, most):
        came = from_of(o)
        row_copy(0, o, ids.at[0], came_ids.at[came], came).wait_recv()
        row_copy(1, o, parts.at[came], came_parts.at[came], came).wait_recv()
        names = came_ids[came]
        acc[...] += spread(names, came_parts[came])
        return jnp.maximum(most, names)

    most = lax.fori_loop(1, n, add, own)
    flag[...] = jnp.where(last, most, 0)

    def flag_copy(o, at, other):
        return pltpu.make_async_remote_copy(
            src_ref=flag,
            dst_ref=came_flags.at[at],
            send_sem=flag_send.at[o],
            recv_sem=flag_take.at[o],
            device_id={"slab": other},
            device_id_type=mesh_id,
        )

    def begin_flag(o, unused):
        flag_copy(o, slab, lax.rem(slab + o, slabs)).start()
        return unused

    lax.fori_loop(1, slabs, begin_flag, 0)
    for p in range(n):
        sums[p] = acc[p * share : (p + 1) * share, :].astype(jnp.bfloat16)

    def begin_sums(o, unused):
        to = to_of(o)
        row_copy(2, o, sums.at[to], pieces.at[row], to).start()
        return unused

    lax.fori_loop(1, n, begin_sums, 0)
    pieces[row] = sums[row]

    def end_flag(o, most):
        came = lax.rem(slab + slabs - o, slabs)
        flag_copy(o, slab, lax.rem(slab + o, slabs)).wait_send()
        flag_copy(o, came, came).wait_recv()
        return jnp.maximum(most, came_flags[came])

    most_ref[0, 0] = jnp.max(lax.fori_loop(1, slabs, end_flag, flag[...]))

    def end(o, unused):
        to, came = to_of(o), from_of(o)
        row_copy(0, o, ids.at[0], came_ids.at[row], to).wait_send()
        row_copy(1, o, parts.at[to], came_parts.at[row], to).wait_send()
        row_copy(2, o, sums.at[to], pieces.at[row], to).wait_send()
        row_copy(2, o, sums.at[came], pieces.at[came], came).wait_recv()
        return unused

    lax.fori_loop(1, n, end, 0)


def reduce_parts(parts, ids, share):
    n, slabs = lax.axis_size("row"), lax.axis_size("slab")
    _, blocks, lanes = parts.shape
    vmem = pl.BlockSpec(memory_space=pltpu.VMEM)
    return pl.pallas_call(
        reduce_kernel,
        out_shape=(
            jax.ShapeDtypeStruct((n, share, lanes), jnp.bfloat16),
            jax.ShapeDtypeStruct((1, 1), jnp.int32),
        ),
        in_specs=[vmem, vmem],
        out_specs=(vmem, pl.BlockSpec(memory_space=pltpu.SMEM)),
        scratch_shapes=[
            pltpu.VMEM((n, blocks, lanes), jnp.bfloat16),
            pltpu.VMEM((n, 1, IDS), jnp.int32),
            pltpu.VMEM((n, share, lanes), jnp.bfloat16),
            pltpu.VMEM((1, IDS), jnp.int32),
            pltpu.VMEM((slabs, 1, IDS), jnp.int32),
            pltpu.VMEM((n * share, lanes), jnp.float32),
            pltpu.SemaphoreType.DMA((3, n)),
            pltpu.SemaphoreType.DMA((3, n)),
            pltpu.SemaphoreType.DMA((slabs,)),
            pltpu.SemaphoreType.DMA((slabs,)),
        ],
        compiler_params=pltpu.CompilerParams(
            collective_id=0, has_side_effects=True, vmem_limit_bytes=32 * 2**20
        ),
        name="reduce_parts",
    )(parts, ids)


def assemble_kernel(pieces_ref, out_ref, wide):
    n, targets, pair = pieces_ref.shape
    owned, width, outspan = out_ref.shape
    half = width // 2
    kc = targets // owned
    lower = lax.broadcasted_iota(jnp.int32, (half, pair), 1) < half * 2
    wide[...] = pieces_ref[...].reshape(n * targets, pair).astype(jnp.float32)
    for g in range(owned):
        for h in range(kc // 2):
            one = wide[pl.ds(g * kc + 2 * h, n, stride=targets), :]
            two = wide[pl.ds(g * kc + 2 * h + 1, n, stride=targets), :]
            span = slice(h * pair, (h + 1) * pair)
            out_ref[g, :half, span] = jnp.where(lower, one, pltpu.roll(two, width, 1))
            out_ref[g, half:, span] = jnp.where(lower, pltpu.roll(one, width, 1), two)


def assemble(pieces, width, kc):
    vmem = pl.BlockSpec(memory_space=pltpu.VMEM)
    n, targets, pair = pieces.shape
    return pl.pallas_call(
        assemble_kernel,
        out_shape=jax.ShapeDtypeStruct((NC, width, kc * width), jnp.float32),
        in_specs=[vmem],
        out_specs=vmem,
        scratch_shapes=[pltpu.VMEM((n * targets, pair), jnp.float32)],
        name="assemble",
    )(pieces)


def coarse_kernel(
    cols, words, a_hbm, p_hbm, halo_hbm, out_ref, a_v, ext_v, g_v, pt_v, acc, items, sems
):
    rows, width, span = a_v.shape
    ka = span // width
    kp = ext_v.shape[2] // width
    nslots, _, outspan = out_ref.shape
    kc = outspan // width
    pair = 2 * width
    copies = load_operands(a_hbm, p_hbm, halo_hbm, a_v, ext_v, sems)
    for copy in copies:
        copy.start()
    clear_rows(acc, width, 0, acc.shape[0] // width)

    last = words.shape[0] - 1
    first = words[words.shape[0] - 128]

    def more(state):
        return state[0] != last

    def take(state):
        at, count = state
        word = words[at]
        items[count] = words[at + rows] + (word & 511)
        return (lax.shift_right_logical(word, 9), count + 1)

    _, count = lax.while_loop(more, take, (first, 0))
    for u in range(UNROLL):
        items[count + u] = nslots * kc
    for copy in copies:
        copy.wait()
    all_products(cols, a_v, ext_v, g_v, pt_v)
    add_items(count, items, pt_v, g_v, acc, width, ka, kp)
    lower = lax.broadcasted_iota(jnp.int32, (width, pair), 1) < width

    def finish(t, unused):
        for h in range(kc // 2):
            one = acc[pl.ds(pl.multiple_of((t * kc + 2 * h) * width, width), width), :]
            two = acc[pl.ds(pl.multiple_of((t * kc + 2 * h + 1) * width, width), width), :]
            one = one + pltpu.roll(one, width, 1)
            two = two + pltpu.roll(two, width, 1)
            out_ref[t, :, h * pair : (h + 1) * pair] = jnp.where(lower, one, two).astype(jnp.bfloat16)
        return unused

    lax.fori_loop(0, nslots, finish, 0)


def coarse_partials(cols, words, a_blocks, p_blocks, halo, nslots, kc):
    rows, width, span = a_blocks.shape
    kp = p_blocks.shape[2] // width
    ka = span // width
    extended = rows + halo.shape[0]
    smem = pl.BlockSpec(memory_space=pltpu.SMEM)
    hbm = pl.BlockSpec(memory_space=pl.ANY)
    vmem = pl.BlockSpec(memory_space=pltpu.VMEM)
    return pl.pallas_call(
        coarse_kernel,
        out_shape=jax.ShapeDtypeStruct((nslots, width, kc * width), jnp.bfloat16),
        in_specs=[smem, smem, hbm, hbm, hbm],
        out_specs=pl.BlockSpec(memory_space=pltpu.VMEM),
        scratch_shapes=[
            pltpu.VMEM((rows, width, span), jnp.bfloat16),
            pltpu.VMEM((extended, width, kp * width), jnp.bfloat16),
            pltpu.VMEM((rows * ka * (kp // 2), width, 2 * width), jnp.bfloat16),
            pltpu.VMEM((rows * kp, width, width), jnp.bfloat16),
            pltpu.VMEM(((nslots * kc + 1) * width, 2 * width), jnp.float32),
            pltpu.SMEM((rows * kp * ka * kp + UNROLL,), jnp.int32),
            pltpu.SemaphoreType.DMA((3,)),
        ],
        compiler_params=pltpu.CompilerParams(vmem_limit_bytes=56 * 2**20),
        name="coarse_partials",
    )(cols, words, a_blocks, p_blocks, halo)


def sum_kernel(ids, parts, out_ref):
    out_ref[...] = jnp.zeros_like(out_ref)

    def one(n, unused):
        row = ids[n]

        @pl.when(row >= 0)
        def _():
            out_ref[row] = out_ref[row] + parts[n].astype(jnp.float32)

        return unused

    lax.fori_loop(0, parts.shape[0], one, 0)


def sum_parts(ids, parts):
    return pl.pallas_call(
        sum_kernel,
        out_shape=jax.ShapeDtypeStruct((NC,) + parts.shape[1:], jnp.float32),
        in_specs=[pl.BlockSpec(memory_space=pltpu.SMEM), pl.BlockSpec(memory_space=pltpu.VMEM)],
        out_specs=pl.BlockSpec(memory_space=pltpu.VMEM),
        compiler_params=pltpu.CompilerParams(vmem_limit_bytes=32 * 2**20),
        name="sum_parts",
    )(ids, parts)


def per_device(a_blocks, p_blocks, a_cols, p_slots, touched, touch_cols, halo_rows):
    nrow = lax.axis_size("row")
    cap = touched.shape[2]
    slots = touched.shape[1] * cap
    kc = touch_cols.shape[3]
    table = touched.transpose(0, 2, 1)
    patterns = touch_cols.transpose(0, 2, 3, 1)
    columns = a_cols.T
    halo, words = exchange_halo(halo_rows, table, patterns, columns, p_slots.T, p_blocks)
    halo = halo.reshape((-1,) + halo.shape[2:])
    words = words.reshape(-1)
    width = a_blocks.shape[1]
    packed, ids = packed_partials(columns, words, table, a_blocks, p_blocks, halo, kc)
    pieces, counts = reduce_parts(packed, ids.reshape(1, 1, IDS), NC * kc)

    def whole(unused):
        partial = coarse_partials(columns, words, a_blocks, p_blocks, halo, slots, kc)
        parts = lax.all_to_all(partial.reshape(nrow, cap * width, kc * width), "row", 0, 0)
        owners = lax.all_to_all(touched[0], "row", 0, 0)
        return sum_parts(owners.reshape(-1), parts.reshape(slots, width, kc * width))

    return lax.cond(counts[0, 0] > BLOCKS, whole, lambda unused: assemble(pieces, width, kc), 0)


def solution(mesh):
    in_specs = (
        P(("slab", "row"), None, None),
        P(("slab", "row"), None, None),
        P(("slab", "row"), None),
        P(("slab", "row"), None),
        P(("slab", "row"), None, None),
        P(("slab", "row"), None, None, None),
        P(("slab", "row"), None, None),
    )
    out_specs = P(("slab", "row"), None, None)
    return jax.shard_map(per_device, mesh=mesh, in_specs=in_specs, out_specs=out_specs, check_vma=False)
```
